512 devices in a mesh: store: 32 (over x, z), tp: 16 (over y, core).
Axes of the slice: x: 4, y: 8, z: 8, core: 2. Of those that a mesh axis runs over, the one named last changes fastest.
Arguments:
- hidden: bfloat16 [32, 64, 8192], P('store', None, 'tp'), may hold values from -6 to 6
- norm_gain: bfloat16 [8192], replicated, may hold values from 0.25 to 1.75
- q_weight: bfloat16 [8192, 16, 512], P('store', 'tp'), may hold values from -1 to 1
- kv_weight: bfloat16 [8192, 16, 128], P('store', 'tp'), may hold values from -0.0625 to 0.0625
- cache_store: bfloat16 [256, 16, 128, 256], P('store', 'tp'), may hold values from -6 to 6
- location: int32 [256], replicated, may hold values from 0 to 255, as said below
- stretch_ids: int32 [32, 32], P('store'), may hold values from -1 to 255, as said below
- rec_pos: int32 [32, 64], P('store'), may hold values from 0 to 8191, as said below
Outputs:
- attended: bfloat16 [32, 64, 16, 512], P('store', None, 'tp')
The draws below stay inside these ranges and needn't reach their ends.
Inputs may be any that keep to these rules, and one draw needn't show every extreme that they name: A permutation: stretch c is row location[c] of cache_store, on store shard location[c] // 8. `stretch_ids`: each row holds 8 to 32 distinct stretch ids followed by -1s, and some row holds 32; at most 1 of one request's stretches lie on one store shard, and every request reaches that many on some shard. `rec_pos`: each row: 64 distinct increasing positions below 256 times the request's number of stretches; the request's last position is always among them.
All inputs are finite; a program needn't handle non-finite values.
Results may differ from the reference program's by a relative error of at most 0.014.
Values may be sent and summed in bfloat16 or wider, within the bound.
No kernel may reach another device: no remote copies, remote signals or barrier semaphores. Data moves between devices by JAX's collectives and lax.ppermute only.
A program may use at most 64 MiB of HBM per device.

```python
import math
import jax
import jax.numpy as jnp
from jax import lax

D = 8192
KVH = 8
HD = 128
STRETCH = 256
MAXC = 32
MINC = 8
ROWS = 64
CH_DEV = 8
QS = 4
HALF = 128
SLOTS = 1
REQUESTS = 32
STRETCHES = 256
N_STORE = 32


def layout_table(key):
    return jax.random.permutation(key, jnp.arange(STRETCHES, dtype=jnp.int32)).astype(jnp.int32)


def stretch_counts(key):
    key = jax.random.fold_in(key, 101)
    first_key, second_key = jax.random.split(key)
    counts = jax.random.randint(first_key, (REQUESTS,), MINC, MAXC + 1)
    widest = jax.random.randint(second_key, (), 0, REQUESTS)
    return jnp.where(jnp.arange(REQUESTS) == widest, MAXC, counts).astype(jnp.int32)


def draw_hidden(key, part):
    key = jax.random.fold_in(key, 23)
    noise = jnp.clip(jax.random.normal(key, (REQUESTS, ROWS, D), jnp.float32), -6.0, 6.0)
    values_out = noise
    return values_out.astype(jnp.bfloat16)


def draw_q_weight(key, part):
    key = jax.random.fold_in(key, 29)
    base = jnp.clip(jax.random.normal(key, (D, 2 * KVH, QS * HD), jnp.float32), -4.0, 4.0) * (1.0 / math.sqrt(D))
    return base.astype(jnp.bfloat16)


def draw_cache_store(key, part):
    key = jax.random.fold_in(key, 31)
    base_key = jax.random.fold_in(key, 0)
    base = jnp.clip(jax.random.normal(base_key, (STRETCHES, 2 * KVH, HALF, 2 * HD), jnp.float32), -6.0, 6.0)
    return base.astype(jnp.bfloat16)


def draw_location(key, part):
    return layout_table(key)


def draw_stretch_ids(key, part):
    location = layout_table(key)
    counts = stretch_counts(key)
    stored = jnp.argsort(location).astype(jnp.int32)
    key = jax.random.fold_in(key, 7)
    request_keys = jax.random.split(key, REQUESTS)

    def one_request(request_key, stretch_count):
        order_key, local_key = jax.random.split(request_key)
        shards = jax.random.permutation(order_key, jnp.arange(N_STORE, dtype=jnp.int32))
        scores = jax.random.randint(local_key, (N_STORE, CH_DEV), 0, 1 << 20) * CH_DEV
        scores = scores + jnp.arange(CH_DEV, dtype=jnp.int32)[None, :]
        local_table = jnp.argsort(scores, axis=1).astype(jnp.int32)
        places = jnp.arange(MAXC, dtype=jnp.int32)
        shard_seq = shards[places // SLOTS]
        local_seq = local_table[shard_seq, places % SLOTS]
        chosen = stored[shard_seq * CH_DEV + local_seq]
        return jnp.where(places < stretch_count, chosen, -1)
    return jax.vmap(one_request)(request_keys, counts).astype(jnp.int32)


def draw_rec_pos(key, part):
    counts = stretch_counts(key)
    key = jax.random.fold_in(key, 11)
    request_keys = jax.random.split(key, REQUESTS)
    span_total = MAXC * STRETCH

    def one_request(request_key, stretch_count):
        places = jnp.arange(span_total, dtype=jnp.int32)
        scores = jax.random.permutation(request_key, places)
        context_len = stretch_count * STRETCH
        scores = jnp.where(places < context_len, scores, -1 - places)
        scores = jnp.where(places == context_len - 1, span_total, scores)
        chosen = lax.top_k(scores, ROWS)[1]
        return jnp.sort(chosen.astype(jnp.int32))
    return jax.vmap(one_request)(request_keys, counts).astype(jnp.int32)


def shard_levels(rng, shape, cuts, least, top_value):
    def one(axis_at, blocks):
        draws = jax.random.uniform(jax.random.fold_in(jax.random.fold_in(rng, 6), axis_at), (blocks,), jnp.float32, least / len(cuts), top_value / len(cuts))
        return jnp.repeat(jnp.exp(draws), shape[axis_at] // blocks).reshape((-1,) + (1,) * (len(shape) - axis_at - 1))

    gain = one(*cuts[0])
    for cut in cuts[1:]:
        gain = gain * one(*cut)
    return gain


def normal_values(key, dims, scale, bound, pieces=(), kind=jnp.bfloat16):
    array = scale * jax.random.normal(key, dims, jnp.float32)
    if pieces:
        array = array * shard_levels(key, dims, pieces, -0.22, 0.18)
    return jnp.clip(array, -bound, bound).astype(kind)


def setup_inputs(seed: int = 0) -> dict:
    key_of = jax.random.split(jax.random.key(seed), 9)
    return {
        "hidden": draw_hidden(jax.random.fold_in(key_of[8], 71), 0),
        "norm_gain": jnp.clip(1.0 + 0.15 * jax.random.normal(key_of[1], (D,), jnp.float32), 0.25, 1.75).astype(jnp.bfloat16),
        "q_weight": draw_q_weight(jax.random.fold_in(key_of[8], 71), 0),
        "kv_weight": normal_values(key_of[3], (D, 2 * KVH, HD), D ** -0.5, 0.0625, ((0, 32), (1, 16))),
        "cache_store": draw_cache_store(jax.random.fold_in(key_of[8], 71), 0),
        "location": draw_location(jax.random.fold_in(key_of[8], 71), 0),
        "stretch_ids": draw_stretch_ids(jax.random.fold_in(key_of[8], 71), 0),
        "rec_pos": draw_rec_pos(jax.random.fold_in(key_of[8], 71), 0),
    }


theta_base = 500000.0
neg_large = -1e+30

def rotary(values_in, positions):
    half_width = values_in.shape[-1] // 2
    frequency = jnp.exp(-math.log(theta_base) * jnp.arange(half_width, dtype=jnp.float32) / half_width)
    angles = positions.astype(jnp.float32)[:, None] * frequency[None, :]
    angle_shape = (angles.shape[0],) + (1,) * (values_in.ndim - 2) + (half_width,)
    cosine = jnp.cos(angles).reshape(angle_shape)
    sine_part = jnp.sin(angles).reshape(angle_shape)
    first_part = values_in[..., :half_width]
    second = values_in[..., half_width:]
    return jnp.concatenate([first_part * cosine - second * sine_part, second * cosine + first_part * sine_part], axis=-1)

def rms_normed(states, norm_gain):
    widened = states.astype(jnp.float32)
    variance = lax.optimization_barrier(jnp.mean(widened * widened, axis=-1, keepdims=True))
    return (widened * lax.rsqrt(variance + 1e-05) * norm_gain.astype(jnp.float32)).astype(jnp.bfloat16)

def reference(hidden, norm_gain, q_weight, kv_weight, cache_store, location, stretch_ids, rec_pos):
    score_scale = 1.0 / math.sqrt(HD)

    def one_request(operands):
        states, stretch_list, positions = operands
        normed = rms_normed(states, norm_gain)
        queries = jnp.einsum('rd,dgc->rgc', normed.astype(jnp.float32), q_weight.astype(jnp.float32))
        queries = rotary(queries.reshape(ROWS, 2, KVH, QS, HD), positions).astype(jnp.bfloat16)
        fresh_sum = jnp.einsum('rd,dgc->rgc', normed.astype(jnp.float32), kv_weight.astype(jnp.float32))
        fresh_sum = fresh_sum.reshape(ROWS, 2, KVH, HD)
        fresh_keys = rotary(fresh_sum[:, 0], positions).astype(jnp.bfloat16)
        fresh_values = fresh_sum[:, 1].astype(jnp.bfloat16)
        stretch_count = jnp.sum((stretch_list >= 0).astype(jnp.int32))
        stored_rows = location[jnp.maximum(stretch_list, 0)]
        joined = cache_store[stored_rows].reshape(MAXC, 2, KVH, HALF, 2 * HD)
        joined = jnp.transpose(joined, (0, 1, 3, 2, 4)).reshape(MAXC * STRETCH, KVH, 2 * HD)
        joined_keys = joined[..., :HD].at[positions].set(fresh_keys)
        joined_values = joined[..., HD:].at[positions].set(fresh_values)
        key_pos = jnp.arange(MAXC * STRETCH, dtype=jnp.int32)
        allowed = (key_pos[None, :] < stretch_count * STRETCH) & (key_pos[None, :] <= positions[:, None])
        allowed = allowed[:, None, None, None, :]
        scores = jnp.einsum('rsghc,lgc->rsghl', queries.astype(jnp.float32), joined_keys.astype(jnp.float32)) * score_scale
        row_peak = lax.optimization_barrier(jnp.max(jnp.where(allowed, scores, neg_large), axis=-1, keepdims=True))
        weights = jnp.where(allowed, jnp.exp(scores - row_peak), 0.0)
        weight_sum = lax.optimization_barrier(jnp.sum(weights, axis=-1))
        rounded = lax.optimization_barrier(weights.astype(jnp.bfloat16))
        mixed_values = jnp.einsum('rsghl,lgc->rsghc', rounded.astype(jnp.float32), joined_values.astype(jnp.float32))
        attended = (mixed_values / weight_sum[..., None]).astype(jnp.bfloat16)
        return attended.reshape(ROWS, 2 * KVH, QS * HD)
    return lax.map(one_request, (hidden, stretch_ids, rec_pos))
```

```python
import math

import jax
import jax.numpy as jnp
from jax import lax
from jax.experimental import pallas as pl
from jax.experimental.pallas import tpu as pltpu
from jax.sharding import Mesh
from jax.sharding import PartitionSpec as P

NX, NZ, NY, NC = 4, 8, 8, 2
KVH = 8
HD = 128
STRETCH = 256
MAXC = 32
CH_DEV = 8
QS = 4
HALF = 128
ROWS = 64
D = 8192
QW = QS * HD
COLS = QW + HD
QROWS = QS * ROWS

theta_base = 500000.0
neg_large = -1e30
far_away = 1 << 29

STORE = ("x", "z")
TP = ("y", "c")


def exchange(block):
    return lax.ppermute(block, "y", [(i, (i + NY // 2) % NY) for i in range(NY)])


def call(kernel, outs, name, flops=0, bytes_accessed=0):
    return pl.pallas_call(
        kernel,
        out_shape=outs,
        name=name,
        compiler_params=pltpu.CompilerParams(vmem_limit_bytes=32 * 1024 * 1024),
        cost_estimate=pl.CostEstimate(
            flops=flops, bytes_accessed=bytes_accessed, transcendentals=0
        ),
    )


def finish_kernel(parts_ref, inv_ref, cos_ref, sin_ref, fcos_ref, fsin_ref, out_ref):
    inv = inv_ref[...]
    for group in range(QS + 1):
        lanes = pl.ds(group * HD, HD)
        total = parts_ref[0, :, lanes].astype(jnp.float32)
        for part in range(1, NZ):
            total += parts_ref[part, :, lanes].astype(jnp.float32)
        total = total * inv
        cos = cos_ref[...] if group < QS else fcos_ref[...]
        sin = sin_ref[...] if group < QS else fsin_ref[...]
        turned = total * cos + pltpu.roll(total, HD // 2, 1) * sin
        out_ref[pl.ds(group * ROWS, ROWS), :] = turned.astype(jnp.bfloat16)


def attend_kernel(
    count_ref,
    shard_ref,
    flag_ref,
    own_ref,
    other_ref,
    kv_ref,
    eff_ref,
    fresh_eff_ref,
    pos_ref,
    own_out_ref,
    stat_ref,
    sent_ref,
    acc_ref,
    run_ref,
):
    is_first = flag_ref[0] == 0
    queries = jnp.concatenate([own_ref[:QROWS, :], other_ref[:QROWS, :]], axis=0)
    own_piece = own_ref[QROWS:, :]
    other_piece = other_ref[QROWS:, :]
    first = jnp.broadcast_to(is_first, own_piece.shape)
    fresh_keys = jnp.where(first, own_piece, other_piece)
    fresh_values = jnp.where(first, other_piece, own_piece)
    pos = pos_ref[...]
    nt = (((1,), (1,)), ((), ()))
    tn = (((0,), (0,)), ((), ()))

    scores = lax.dot_general(fresh_keys, queries, nt, preferred_element_type=jnp.float32)
    scores = jnp.where(fresh_eff_ref[:, 0:1] <= pos, scores, neg_large)
    peak = jnp.max(scores, axis=0, keepdims=True)
    weights = jnp.exp2(scores - peak)
    run_ref[0:1, :] = peak
    run_ref[1:2, :] = jnp.sum(weights, axis=0, keepdims=True)
    acc_ref[...] = lax.dot_general(
        fresh_values, weights.astype(jnp.bfloat16), tn, preferred_element_type=jnp.float32
    )

    per = 4
    for group in range(MAXC // per):

        @pl.when(group * per < count_ref[0])
        def _():
            pieces = []
            for j in range(group * per, group * per + per):
                keys = kv_ref[shard_ref[j], :, :HD]
                piece = lax.dot_general(keys, queries, nt, preferred_element_type=jnp.float32)
                pieces.append(jnp.where(eff_ref[:, j : j + 1] <= pos, piece, neg_large))
            old_peak = run_ref[0:1, :]
            new_peak = old_peak
            for piece in pieces:
                new_peak = jnp.maximum(new_peak, jnp.max(piece, axis=0, keepdims=True))
            factor = jnp.exp2(old_peak - new_peak)
            total = run_ref[1:2, :] * factor
            acc = acc_ref[...] * factor
            for at, piece in enumerate(pieces):
                weights = jnp.exp2(piece - new_peak)
                total += jnp.sum(weights, axis=0, keepdims=True)
                values = kv_ref[shard_ref[group * per + at], :, HD:]
                acc += lax.dot_general(
                    values,
                    weights.astype(jnp.bfloat16),
                    tn,
                    preferred_element_type=jnp.float32,
                )
            run_ref[0:1, :] = new_peak
            run_ref[1:2, :] = total
            acc_ref[...] = acc

    peak = run_ref[0:1, :]
    total = run_ref[1:2, :]
    mixed = acc_ref[...] / total
    own_out_ref[...] = mixed[:, :QROWS]
    stat_ref[0:1, :] = peak[:, :QROWS]
    stat_ref[1:2, :] = total[:, :QROWS]
    stat_ref[2:8, :] = jnp.zeros((6, QROWS), jnp.float32)
    peak = peak[:, QROWS:]
    total = total[:, QROWS:]
    peak_high = peak.astype(jnp.bfloat16).astype(jnp.float32)
    total_high = total.astype(jnp.bfloat16).astype(jnp.float32)
    stats = jnp.concatenate(
        [
            peak_high,
            peak - peak_high,
            total_high,
            total - total_high,
            jnp.zeros((12, QROWS), jnp.float32),
        ],
        axis=0,
    )
    sent_ref[:HD, :] = mixed[:, QROWS:].astype(jnp.bfloat16)
    sent_ref[HD:, :] = stats.astype(jnp.bfloat16)


def merge_kernel(own_ref, stat_ref, got_ref, out_ref):
    stats = got_ref[HD:, :].astype(jnp.float32)
    got_peak = stats[0:1, :] + stats[1:2, :]
    got_total = stats[2:3, :] + stats[3:4, :]
    peak = stat_ref[0:1, :]
    total = stat_ref[1:2, :]
    joint = jnp.maximum(peak, got_peak)
    mine = jnp.exp2(peak - joint) * total
    theirs = jnp.exp2(got_peak - joint) * got_total
    whole = mine + theirs
    mixed = own_ref[...] * (mine / whole) + got_ref[:HD, :].astype(jnp.float32) * (theirs / whole)
    turned = mixed.T.astype(jnp.bfloat16)
    for head in range(QS):
        out_ref[:, pl.ds(head * HD, HD)] = turned[head * ROWS : (head + 1) * ROWS, :]


def body(hidden, norm_gain, q_weight, kv_weight, cache_store, location, stretch_ids, rec_pos):
    x = lax.axis_index("x")
    z = lax.axis_index("z")
    y = lax.axis_index("y")
    c = lax.axis_index("c")
    my_store = x * NZ + z
    my_tp = y * NC + c
    which_half = my_tp // KVH
    is_first = which_half == 0
    positions = rec_pos[0]
    own_list = stretch_ids[0]

    lists = lax.all_to_all(
        jnp.broadcast_to(stretch_ids[None], (NX * NZ, 1, MAXC)), STORE, 0, 0, tiled=True
    )[:, 0]

    weight = jnp.concatenate([q_weight[:, 0], kv_weight[:, 0]], axis=1)
    weight = lax.all_gather(weight, "x", axis=0)

    states = hidden[0]
    squares = lax.psum(jnp.sum(jnp.square(states.astype(jnp.float32)), axis=1), TP)
    gain = lax.dynamic_slice_in_dim(norm_gain, my_tp * 512, 512)
    gained = (states.astype(jnp.float32) * gain.astype(jnp.float32)).astype(jnp.bfloat16)
    blocks = gained.reshape(NY, 8, 2, NC, HD).transpose(2, 0, 3, 1, 4)
    blocks = jnp.broadcast_to(blocks[None], (4, 2, NY, NC, 8, HD)).reshape(NZ * NY * NC, 8, HD)
    blocks = lax.all_to_all(blocks, ("z", "y", "c"), 0, 0, tiled=True)
    blocks = blocks.reshape(NZ, NX, 4, 8, HD)
    blocks = lax.dynamic_index_in_dim(blocks, z // 2, 2, keepdims=False)
    blocks = blocks.transpose(0, 2, 1, 3).reshape(NZ, 8, NX * HD)
    tokens = lax.all_to_all(
        jnp.broadcast_to(blocks[None], (NY * NC, NZ, 8, NX * HD)), TP, 0, 0, tiled=True
    )
    tokens = tokens.reshape(NY, NC, NZ, 8, NX * HD).transpose(2, 0, 3, 1, 4)
    tokens = tokens.reshape(NZ * ROWS, NC * NX * HD)
    weight = weight.reshape(NX, NC, HD, COLS).transpose(1, 0, 2, 3).reshape(NC * NX * HD, COLS)
    partial = jnp.dot(tokens, weight, preferred_element_type=jnp.float32).astype(jnp.bfloat16)
    parts = lax.all_to_all(partial.reshape(NZ, ROWS, COLS), "z", 0, 0, tiled=True)

    row_ids = my_store * CH_DEV + jnp.arange(CH_DEV, dtype=jnp.int32)
    here = location[None, :] == row_ids[:, None]
    held = jnp.sum(jnp.where(here, jnp.arange(location.shape[0], dtype=jnp.int32), 0), axis=1)
    wanted = jnp.any(lists[:, :, None] == held[None, None, :], axis=1)
    send_rows = jnp.sum(jnp.where(wanted, jnp.arange(CH_DEV, dtype=jnp.int32)[None], 0), axis=1)
    outgoing = cache_store[:, 0][send_rows]
    arrived = lax.all_to_all(outgoing, STORE, 0, 0, tiled=True)

    inverse = lax.rsqrt(squares * (1.0 / D) + 1e-05)
    frequency = jnp.exp(
        -math.log(theta_base) * jnp.arange(HD // 2, dtype=jnp.float32) / (HD // 2)
    )
    angles = positions.astype(jnp.float32)[:, None] * frequency[None, :]
    cos = jnp.cos(angles)
    sin = jnp.sin(angles)
    cos = jnp.concatenate([cos, cos], axis=1)
    sin = jnp.concatenate([-sin, sin], axis=1)
    fresh_cos = jnp.where(is_first, cos, 1.0)
    fresh_sin = jnp.where(is_first, sin, 0.0)
    scale = math.log2(math.e) / math.sqrt(HD)
    inverse = jnp.broadcast_to(inverse[:, None], (ROWS, HD))

    own = call(
        finish_kernel, jax.ShapeDtypeStruct((QROWS + ROWS, HD), jnp.bfloat16), "finish"
    )(parts, inverse, cos * scale, sin * scale, fresh_cos, fresh_sin)
    other = exchange(own)

    table = jnp.arange(location.shape[0], dtype=jnp.int32)
    own_row = jnp.sum(jnp.where(own_list[:, None] == table[None, :], location[None, :], 0), axis=1)
    own_shard = own_row // CH_DEV
    count = jnp.sum((own_list >= 0).astype(jnp.int32)).reshape(1)
    order = jnp.arange(MAXC, dtype=jnp.int32)
    key_pos = (
        order[None, :] * STRETCH
        + which_half * HALF
        + jnp.arange(HALF, dtype=jnp.int32)[:, None]
    )
    replaced = jnp.any(key_pos[:, :, None] == positions[None, None, :], axis=2)
    eff = jnp.where(replaced | (order >= count[0])[None, :], far_away, key_pos)
    fresh_eff = jnp.where(positions % STRETCH // HALF == which_half, positions, far_away)
    fresh_eff = jnp.broadcast_to(fresh_eff[:, None], (ROWS, HD))
    pos_row = jnp.tile(positions, 2 * QS).reshape(1, 2 * QROWS)

    smem = pl.BlockSpec(memory_space=pltpu.SMEM)
    vmem = pl.BlockSpec(memory_space=pltpu.VMEM)
    own_part, stats, sent = pl.pallas_call(
        attend_kernel,
        out_shape=[
            jax.ShapeDtypeStruct((HD, QROWS), jnp.float32),
            jax.ShapeDtypeStruct((8, QROWS), jnp.float32),
            jax.ShapeDtypeStruct((HD + 16, QROWS), jnp.bfloat16),
        ],
        in_specs=[smem] * 3 + [vmem] * 6,
        out_specs=[vmem] * 3,
        scratch_shapes=[
            pltpu.VMEM((HD, 2 * QROWS), jnp.float32),
            pltpu.VMEM((8, 2 * QROWS), jnp.float32),
        ],
        name="attend",
        compiler_params=pltpu.CompilerParams(vmem_limit_bytes=32 * 1024 * 1024),
        cost_estimate=pl.CostEstimate(
            flops=4 * 2 * QROWS * MAXC * HALF * HD,
            bytes_accessed=MAXC * HALF * 2 * HD * 2,
            transcendentals=2 * QROWS * MAXC * HALF,
        ),
    )(count, own_shard, which_half.reshape(1), own, other, arrived, eff, fresh_eff, pos_row)
    got = exchange(sent)
    attended = call(merge_kernel, jax.ShapeDtypeStruct((ROWS, QW), jnp.bfloat16), "merge")(
        own_part, stats, got
    )
    return attended.reshape(1, ROWS, 1, QW)


def solution(mesh):
    fine = Mesh(mesh.devices.reshape(NX, NZ, NY, NC), ("x", "z", "y", "c"))
    in_specs = (
        P(STORE, None, TP),
        P(),
        P(STORE, TP, None),
        P(STORE, TP, None),
        P(STORE, TP, None, None),
        P(),
        P(STORE, None),
        P(STORE, None),
    )
    return jax.shard_map(
        body, mesh=fine, in_specs=in_specs, out_specs=P(STORE, None, TP, None), check_vma=False
    )
```

```python
import math

import jax
import jax.numpy as jnp
from jax import lax
from jax.experimental import pallas as pl
from jax.experimental.pallas import tpu as pltpu
from jax.sharding import Mesh
from jax.sharding import PartitionSpec as P

NX, NZ, NY, NC = 4, 8, 8, 2
KVH = 8
HD = 128
STRETCH = 256
MAXC = 32
CH_DEV = 8
QS = 4
HALF = 128
ROWS = 64
D = 8192
QW = QS * HD
COLS = QW + HD
QROWS = QS * ROWS

theta_base = 500000.0
neg_large = -1e30
far_away = 1 << 29

STORE = ("x", "z")
TP = ("y", "c")


def exchange(block):
    return lax.ppermute(block, "y", [(i, (i + NY // 2) % NY) for i in range(NY)])


def shifted(block, axis, count, by):
    return lax.ppermute(block, axis, [(i, (i + by) % count) for i in range(count)])


def call(kernel, outs, name, flops=0, bytes_accessed=0):
    return pl.pallas_call(
        kernel,
        out_shape=outs,
        name=name,
        compiler_params=pltpu.CompilerParams(vmem_limit_bytes=32 * 1024 * 1024),
        cost_estimate=pl.CostEstimate(
            flops=flops, bytes_accessed=bytes_accessed, transcendentals=0
        ),
    )


def project_kernel(tokens_ref, weight_ref, out_ref):
    rows = []
    stats = []
    for request in range(NZ):
        wide = jnp.concatenate(
            [
                jnp.concatenate(
                    [tokens_ref[y * NC + c, request].astype(jnp.float32) for c in range(NC)],
                    axis=1,
                )
                for y in range(NY)
            ],
            axis=0,
        )
        rows.append(wide.astype(jnp.bfloat16))
        squares = jnp.zeros((ROWS, HD), jnp.float32)
        for at in range(0, wide.shape[1], HD):
            piece = wide[:, at : at + HD]
            squares += piece * piece
        squares = jnp.concatenate([squares, jnp.zeros_like(squares)], axis=0)
        row = jnp.sum(squares.T, axis=0, keepdims=True)
        high = row.astype(jnp.bfloat16).astype(jnp.float32)
        stat = jnp.concatenate([high, row - high, jnp.zeros((6, HD), jnp.float32)], axis=0)
        stats.append(jnp.concatenate([stat, jnp.zeros((8, QW), jnp.float32)], axis=1))
    total = jnp.dot(
        jnp.concatenate(rows, axis=0), weight_ref[...], preferred_element_type=jnp.float32
    )
    for request in range(NZ):
        block = jnp.concatenate([total[request * ROWS : (request + 1) * ROWS], stats[request]], axis=0)
        out_ref[request] = block.astype(jnp.bfloat16)


def finish_kernel(parts_ref, cos_ref, sin_ref, fcos_ref, fsin_ref, out_ref):
    inverse = None
    for group in range(QS + 1):
        lanes = pl.ds(group * HD, HD)
        total = parts_ref[0, :, lanes].astype(jnp.float32)
        for part in range(1, NZ):
            total += parts_ref[part, :, lanes].astype(jnp.float32)
        if inverse is None:
            squares = total[ROWS : ROWS + 1, :] + total[ROWS + 1 : ROWS + 2, :]
            inverse = lax.rsqrt(squares * (1.0 / D) + 1e-05)
            inverse = jnp.broadcast_to(inverse, (HD, HD)).T[:ROWS]
        total = total[:ROWS] * inverse
        cos = cos_ref[...] if group < QS else fcos_ref[...]
        sin = sin_ref[...] if group < QS else fsin_ref[...]
        turned = total * cos + pltpu.roll(total, HD // 2, 1) * sin
        out_ref[pl.ds(group * ROWS, ROWS), :] = turned.astype(jnp.bfloat16)


def pick_kernel(rows_ref, *refs):
    stores, outs, sem = refs[:NX], refs[NX : NX + NZ], refs[NX + NZ]
    copies = []
    for step in range(NZ):
        for k in range(NX):
            copies.append(
                pltpu.make_async_copy(
                    stores[k].at[rows_ref[step * NX + k]],
                    outs[step].at[k],
                    sem.at[step * NX + k],
                )
            )
            copies[-1].start()
    for copy in copies:
        copy.wait()


def attend_kernel(flag_ref, own_ref, other_ref, eff_ref, fresh_eff_ref, pos_ref, *refs):
    kv_refs, (own_out_ref, stat_ref, sent_ref, acc_ref, run_ref) = refs[:NZ], refs[NZ:]
    is_first = flag_ref[0] == 0
    queries = jnp.concatenate([own_ref[:QROWS, :], other_ref[:QROWS, :]], axis=0)
    own_piece = own_ref[QROWS:, :]
    other_piece = other_ref[QROWS:, :]
    first = jnp.broadcast_to(is_first, own_piece.shape)
    fresh_keys = jnp.where(first, own_piece, other_piece)
    fresh_values = jnp.where(first, other_piece, own_piece)
    pos = pos_ref[...]
    nt = (((1,), (1,)), ((), ()))
    tn = (((0,), (0,)), ((), ()))

    scores = lax.dot_general(fresh_keys, queries, nt, preferred_element_type=jnp.float32)
    scores = jnp.where(fresh_eff_ref[:, 0:1] <= pos, scores, neg_large)
    peak = jnp.max(scores, axis=0, keepdims=True)
    weights = jnp.exp2(scores - peak)
    run_ref[0:1, :] = peak
    run_ref[1:2, :] = jnp.sum(weights, axis=0, keepdims=True)
    acc_ref[...] = lax.dot_general(
        fresh_values, weights.astype(jnp.bfloat16), tn, preferred_element_type=jnp.float32
    )

    for step in range(NZ):
        kv_ref = kv_refs[step]
        pieces = []
        for k in range(NX):
            slot = step * NX + k
            piece = lax.dot_general(
                kv_ref[k, :, :HD], queries, nt, preferred_element_type=jnp.float32
            )
            pieces.append(jnp.where(eff_ref[:, slot : slot + 1] <= pos, piece, neg_large))
        old_peak = run_ref[0:1, :]
        new_peak = old_peak
        for piece in pieces:
            new_peak = jnp.maximum(new_peak, jnp.max(piece, axis=0, keepdims=True))
        factor = jnp.exp2(old_peak - new_peak)
        total = run_ref[1:2, :] * factor
        acc = acc_ref[...] * factor
        for k, piece in enumerate(pieces):
            weights = jnp.exp2(piece - new_peak)
            total += jnp.sum(weights, axis=0, keepdims=True)
            acc += lax.dot_general(
                kv_ref[k, :, HD:],
                weights.astype(jnp.bfloat16),
                tn,
                preferred_element_type=jnp.float32,
            )
        run_ref[0:1, :] = new_peak
        run_ref[1:2, :] = total
        acc_ref[...] = acc

    peak = run_ref[0:1, :]
    total = run_ref[1:2, :]
    mixed = acc_ref[...] / total
    own_out_ref[...] = mixed[:, :QROWS]
    stat_ref[0:1, :] = peak[:, :QROWS]
    stat_ref[1:2, :] = total[:, :QROWS]
    stat_ref[2:8, :] = jnp.zeros((6, QROWS), jnp.float32)
    peak = peak[:, QROWS:]
    total = total[:, QROWS:]
    peak_high = peak.astype(jnp.bfloat16).astype(jnp.float32)
    total_high = total.astype(jnp.bfloat16).astype(jnp.float32)
    stats = jnp.concatenate(
        [
            peak_high,
            peak - peak_high,
            total_high,
            total - total_high,
            jnp.zeros((12, QROWS), jnp.float32),
        ],
        axis=0,
    )
    sent_ref[:HD, :] = mixed[:, QROWS:].astype(jnp.bfloat16)
    sent_ref[HD:, :] = stats.astype(jnp.bfloat16)


def merge_kernel(own_ref, stat_ref, got_ref, out_ref):
    stats = got_ref[HD:, :].astype(jnp.float32)
    got_peak = stats[0:1, :] + stats[1:2, :]
    got_total = stats[2:3, :] + stats[3:4, :]
    peak = stat_ref[0:1, :]
    total = stat_ref[1:2, :]
    joint = jnp.maximum(peak, got_peak)
    mine = jnp.exp2(peak - joint) * total
    theirs = jnp.exp2(got_peak - joint) * got_total
    whole = mine + theirs
    mixed = own_ref[...] * (mine / whole) + got_ref[:HD, :].astype(jnp.float32) * (theirs / whole)
    turned = mixed.T.astype(jnp.bfloat16)
    for head in range(QS):
        out_ref[:, pl.ds(head * HD, HD)] = turned[head * ROWS : (head + 1) * ROWS, :]


def body(hidden, norm_gain, q_weight, kv_weight, cache_store, location, stretch_ids, rec_pos):
    x = lax.axis_index("x")
    z = lax.axis_index("z")
    y = lax.axis_index("y")
    c = lax.axis_index("c")
    my_tp = y * NC + c
    which_half = my_tp // KVH
    is_first = which_half == 0
    positions = rec_pos[0]
    own_list = stretch_ids[0]
    int_rows = jnp.arange(CH_DEV, dtype=jnp.int32)
    table = jnp.arange(location.shape[0], dtype=jnp.int32)

    blocks = hidden[0].reshape(NY, 8, 2, NC, HD).transpose(2, 0, 3, 1, 4)
    listed = jnp.pad(own_list.astype(jnp.bfloat16), (0, HD - MAXC))
    pair = jnp.arange(4, dtype=jnp.int32).reshape(4, 1, 1, 1, 1, 1)
    blocks = jnp.where(pair == my_tp % 4, blocks[None], listed)
    blocks = blocks.reshape(NZ * NY * NC, 8, HD)
    blocks = lax.all_to_all(blocks, ("z", "y", "c"), 0, 0, tiled=True)
    blocks = blocks.reshape(NZ, NX, 4, 8, HD)
    lists = lax.dynamic_index_in_dim(blocks[:, 0, :, 0, :MAXC], (z // 2 + 1) % 4, 1, keepdims=False)
    lists = lists.astype(jnp.int32)
    blocks = lax.dynamic_index_in_dim(blocks, z // 2, 2, keepdims=False)
    blocks = blocks.transpose(0, 2, 1, 3).reshape(NZ, 8, NX * HD)
    tokens = lax.all_to_all(
        jnp.broadcast_to(blocks[None], (NY * NC, NZ, 8, NX * HD)), TP, 0, 0, tiled=True
    )

    weight = jnp.concatenate([q_weight[:, 0], kv_weight[:, 0]], axis=1)
    weight = lax.all_gather(weight, "x", axis=0)
    gain = lax.dynamic_index_in_dim(norm_gain.reshape(NX, NZ, NC, HD), z, 1, keepdims=False)
    weight = weight.reshape(NX, NC, HD, COLS).transpose(1, 0, 2, 3).astype(jnp.float32)
    weight = weight * gain.transpose(1, 0, 2)[..., None].astype(jnp.float32)
    weight = weight.astype(jnp.bfloat16).reshape(NC * NX * HD, COLS)

    store = cache_store[:, 0]
    stores = [store] + [shifted(store, "x", NX, k) for k in range(1, NX)]
    from_x = (x - jnp.arange(NX, dtype=jnp.int32)) % NX
    row_ids = (from_x[:, None] * NZ + z) * CH_DEV + int_rows[None, :]
    here = location[None, None, :] == row_ids[:, :, None]
    held = jnp.sum(jnp.where(here, table, 0), axis=2)
    wanted = jnp.any(lists[:, :, None, None] == held[None, None], axis=1)
    send_rows = jnp.sum(jnp.where(wanted, int_rows, 0), axis=2)
    steps = jnp.arange(NZ, dtype=jnp.int32)
    ahead = (z + steps) % NZ
    turn = ahead[:, None] == steps[None, :]
    send_rows = jnp.sum(jnp.where(turn[:, :, None], send_rows[None], 0), axis=1)
    smem = pl.BlockSpec(memory_space=pltpu.SMEM)
    vmem = pl.BlockSpec(memory_space=pltpu.VMEM)
    hbm = pl.BlockSpec(memory_space=pl.ANY)
    outgoing = pl.pallas_call(
        pick_kernel,
        out_shape=[jax.ShapeDtypeStruct((NX, HALF, 2 * HD), jnp.bfloat16)] * NZ,
        in_specs=[smem] + [hbm] * NX,
        out_specs=[hbm] * NZ,
        scratch_shapes=[pltpu.SemaphoreType.DMA((NZ * NX,))],
        name="pick",
        cost_estimate=pl.CostEstimate(flops=0, bytes_accessed=1 << 22, transcendentals=0),
    )(send_rows.reshape(-1), *stores)
    weight, outgoing = lax.optimization_barrier((weight, outgoing))
    partial = call(
        project_kernel,
        jax.ShapeDtypeStruct((NZ, ROWS + 8, COLS), jnp.bfloat16),
        "project",
        flops=2 * NZ * ROWS * 1024 * COLS,
        bytes_accessed=1 << 22,
    )(tokens, weight)
    late = [1, 2, 3]
    partial, *held_back = lax.optimization_barrier((partial, *[outgoing[k] for k in late]))
    outgoing = list(outgoing)
    for k, block in zip(late, held_back):
        outgoing[k] = block
    parts = lax.all_to_all(partial, "z", 0, 0, tiled=True)

    arrived = [outgoing[0]] + [shifted(outgoing[k], "z", NZ, k) for k in range(1, NZ)]

    frequency = jnp.exp(
        -math.log(theta_base) * jnp.arange(HD // 2, dtype=jnp.float32) / (HD // 2)
    )
    angles = positions.astype(jnp.float32)[:, None] * frequency[None, :]
    cos = jnp.cos(angles)
    sin = jnp.sin(angles)
    cos = jnp.concatenate([cos, cos], axis=1)
    sin = jnp.concatenate([-sin, sin], axis=1)
    fresh_cos = jnp.where(is_first, cos, 1.0)
    fresh_sin = jnp.where(is_first, sin, 0.0)
    scale = math.log2(math.e) / math.sqrt(HD)

    own = call(
        finish_kernel, jax.ShapeDtypeStruct((QROWS + ROWS, HD), jnp.bfloat16), "finish"
    )(parts, cos * scale, sin * scale, fresh_cos, fresh_sin)
    other = exchange(own)

    own_row = jnp.sum(jnp.where(own_list[:, None] == table[None, :], location[None, :], 0), axis=1)
    own_shard = own_row // CH_DEV
    slot_shard = (from_x[None, :] * NZ + ((z - steps) % NZ)[:, None]).reshape(-1)
    match = (own_shard[None, :] == slot_shard[:, None]) & (own_list >= 0)[None, :]
    slot_order = jnp.sum(jnp.where(match, jnp.arange(MAXC, dtype=jnp.int32), 0), axis=1)
    slot_live = jnp.any(match, axis=1)
    key_pos = (
        slot_order[None, :] * STRETCH
        + which_half * HALF
        + jnp.arange(HALF, dtype=jnp.int32)[:, None]
    )
    replaced = jnp.any(key_pos[:, :, None] == positions[None, None, :], axis=2)
    eff = jnp.where(replaced | ~slot_live[None, :], far_away, key_pos)
    fresh_eff = jnp.where(positions % STRETCH // HALF == which_half, positions, far_away)
    fresh_eff = jnp.broadcast_to(fresh_eff[:, None], (ROWS, HD))
    pos_row = jnp.tile(positions, 2 * QS).reshape(1, 2 * QROWS)

    own_part, stats, sent = pl.pallas_call(
        attend_kernel,
        out_shape=[
            jax.ShapeDtypeStruct((HD, QROWS), jnp.float32),
            jax.ShapeDtypeStruct((8, QROWS), jnp.float32),
            jax.ShapeDtypeStruct((HD + 16, QROWS), jnp.bfloat16),
        ],
        in_specs=[smem] + [vmem] * (5 + NZ),
        out_specs=[vmem] * 3,
        scratch_shapes=[
            pltpu.VMEM((HD, 2 * QROWS), jnp.float32),
            pltpu.VMEM((8, 2 * QROWS), jnp.float32),
        ],
        name="attend",
        compiler_params=pltpu.CompilerParams(vmem_limit_bytes=32 * 1024 * 1024),
        cost_estimate=pl.CostEstimate(
            flops=4 * 2 * QROWS * MAXC * HALF * HD,
            bytes_accessed=MAXC * HALF * 2 * HD * 2,
            transcendentals=2 * QROWS * MAXC * HALF,
        ),
    )(which_half.reshape(1), own, other, eff, fresh_eff, pos_row, *arrived)
    got = exchange(sent)
    attended = call(merge_kernel, jax.ShapeDtypeStruct((ROWS, QW), jnp.bfloat16), "merge")(
        own_part, stats, got
    )
    return attended.reshape(1, ROWS, 1, QW)


def solution(mesh):
    fine = Mesh(mesh.devices.reshape(NX, NZ, NY, NC), ("x", "z", "y", "c"))
    in_specs = (
        P(STORE, None, TP),
        P(),
        P(STORE, TP, None),
        P(STORE, TP, None),
        P(STORE, TP, None, None),
        P(),
        P(STORE, None),
        P(STORE, None),
    )
    return jax.shard_map(
        body, mesh=fine, in_specs=in_specs, out_specs=P(STORE, None, TP, None), check_vma=False
    )
```

```python
import functools
import math

import jax
import jax.numpy as jnp
from jax import lax
from jax.experimental import pallas as pl
from jax.experimental.pallas import tpu as pltpu
from jax.sharding import Mesh
from jax.sharding import PartitionSpec as P

NX, NZ, NY, NC = 4, 8, 8, 2
KVH = 8
HD = 128
STRETCH = 256
MAXC = 32
CH_DEV = 8
QS = 4
HALF = 128
ROWS = 64
D = 8192
QW = QS * HD
COLS = QW + HD
QROWS = QS * ROWS

theta_base = 500000.0
neg_large = -1e30
far_away = 1 << 29

STORE = ("x", "z")
TP = ("y", "c")
NT = (((1,), (1,)), ((), ()))
TN = (((0,), (0,)), ((), ()))


def exchange(block):
    return lax.ppermute(block, "y", [(i, (i + NY // 2) % NY) for i in range(NY)])


def shifted(block, axis, count, by):
    return lax.ppermute(block, axis, [(i, (i + by) % count) for i in range(count)])


def call(kernel, outs, name, flops=0, bytes_accessed=0):
    return pl.pallas_call(
        kernel,
        out_shape=outs,
        name=name,
        compiler_params=pltpu.CompilerParams(vmem_limit_bytes=32 * 1024 * 1024),
        cost_estimate=pl.CostEstimate(
            flops=flops, bytes_accessed=bytes_accessed, transcendentals=0
        ),
    )


def project_kernel(tokens_ref, gain_ref, w0_ref, w1_ref, w2_ref, w3_ref, out_ref):
    weights = jnp.concatenate([w[: 2 * HD, :] for w in (w0_ref, w1_ref, w2_ref, w3_ref)], axis=0)
    gain = gain_ref[...]
    rows = []
    stats = []
    for request in range(NZ):
        tall = []
        for y in range(NY):
            halves = [tokens_ref[y * NC + c, request].astype(jnp.float32) for c in range(NC)]
            tall.append(
                jnp.concatenate(
                    [halves[c][:, k * HD : (k + 1) * HD] for k in range(NX) for c in range(NC)],
                    axis=1,
                )
            )
        wide = jnp.concatenate(tall, axis=0)
        rows.append((wide * gain).astype(jnp.bfloat16))
        squares = jnp.zeros((ROWS, HD), jnp.float32)
        for at in range(0, wide.shape[1], HD):
            piece = wide[:, at : at + HD]
            squares += piece * piece
        squares = jnp.concatenate([squares, jnp.zeros_like(squares)], axis=0)
        row = jnp.sum(squares.T, axis=0, keepdims=True)
        high = row.astype(jnp.bfloat16).astype(jnp.float32)
        stat = jnp.concatenate([high, row - high, jnp.zeros((6, HD), jnp.float32)], axis=0)
        stats.append(jnp.concatenate([stat, jnp.zeros((8, QW), jnp.float32)], axis=1))
    total = jnp.dot(jnp.concatenate(rows, axis=0), weights, preferred_element_type=jnp.float32)
    for request in range(NZ):
        block = total[request * ROWS : (request + 1) * ROWS]
        block = jnp.concatenate([block, stats[request]], axis=0)
        out_ref[request] = block.astype(jnp.bfloat16)


def finish_kernel(parts_ref, cos_ref, sin_ref, fcos_ref, fsin_ref, out_ref):
    inverse = None
    for group in range(QS + 1):
        lanes = pl.ds(group * HD, HD)
        total = parts_ref[0, :, lanes].astype(jnp.float32)
        for part in range(1, NZ):
            total += parts_ref[part, :, lanes].astype(jnp.float32)
        if inverse is None:
            squares = total[ROWS : ROWS + 1, :] + total[ROWS + 1 : ROWS + 2, :]
            inverse = lax.rsqrt(squares * (1.0 / D) + 1e-05)
            inverse = jnp.broadcast_to(inverse, (HD, HD)).T[:ROWS]
        total = total[:ROWS] * inverse
        cos = cos_ref[...] if group < QS else fcos_ref[...]
        sin = sin_ref[...] if group < QS else fsin_ref[...]
        turned = total * cos + pltpu.roll(total, HD // 2, 1) * sin
        out_ref[pl.ds(group * ROWS, ROWS), :] = turned.astype(jnp.bfloat16)


def attend_block(kv_ref, slots, queries, eff_ref, pos, run_ref, acc_ref):
    pieces = []
    for at, slot in slots:
        piece = lax.dot_general(
            kv_ref[at, :, :HD], queries, NT, preferred_element_type=jnp.float32
        )
        pieces.append(jnp.where(eff_ref[:, slot : slot + 1] <= pos, piece, neg_large))
    old_peak = run_ref[0:1, :]
    new_peak = old_peak
    for piece in pieces:
        new_peak = jnp.maximum(new_peak, jnp.max(piece, axis=0, keepdims=True))
    factor = jnp.exp2(old_peak - new_peak)
    total = run_ref[1:2, :] * factor
    acc = acc_ref[...] * factor
    for (at, _), piece in zip(slots, pieces):
        weights = jnp.exp2(piece - new_peak)
        total += jnp.sum(weights, axis=0, keepdims=True)
        acc += lax.dot_general(
            kv_ref[at, :, HD:], weights.astype(jnp.bfloat16), TN, preferred_element_type=jnp.float32
        )
    run_ref[0:1, :] = new_peak
    run_ref[1:2, :] = total
    acc_ref[...] = acc


def attend_early_kernel(which, flag_ref, own_ref, other_ref, eff_ref, fresh_eff_ref, pos_ref, *refs):
    kv_refs, (acc_ref, run_ref) = refs[: len(which)], refs[len(which) :]
    is_first = flag_ref[0] == 0
    queries = jnp.concatenate([own_ref[:QROWS, :], other_ref[:QROWS, :]], axis=0)
    own_piece = own_ref[QROWS:, :]
    other_piece = other_ref[QROWS:, :]
    first = jnp.broadcast_to(is_first, own_piece.shape)
    fresh_keys = jnp.where(first, own_piece, other_piece)
    fresh_values = jnp.where(first, other_piece, own_piece)
    pos = pos_ref[...]
    scores = lax.dot_general(fresh_keys, queries, NT, preferred_element_type=jnp.float32)
    scores = jnp.where(fresh_eff_ref[:, 0:1] <= pos, scores, neg_large)
    peak = jnp.max(scores, axis=0, keepdims=True)
    weights = jnp.exp2(scores - peak)
    run_ref[...] = jnp.zeros(run_ref.shape, jnp.float32)
    run_ref[0:1, :] = peak
    run_ref[1:2, :] = jnp.sum(weights, axis=0, keepdims=True)
    acc_ref[...] = lax.dot_general(
        fresh_values, weights.astype(jnp.bfloat16), TN, preferred_element_type=jnp.float32
    )
    for k, kv_ref in zip(which, kv_refs):
        for half in range(0, NZ, 4):
            slots = [(half + i, k * NZ + half + i) for i in range(4)]
            attend_block(kv_ref, slots, queries, eff_ref, pos, run_ref, acc_ref)


def attend_late_kernel(
    which, own_ref, other_ref, eff_ref, pos_ref, acc_in_ref, run_in_ref, *refs
):
    kv_refs, (own_out_ref, stat_ref, sent_ref, acc_ref, run_ref) = (
        refs[: len(which)],
        refs[len(which) :],
    )
    queries = jnp.concatenate([own_ref[:QROWS, :], other_ref[:QROWS, :]], axis=0)
    pos = pos_ref[...]
    acc_ref[...] = acc_in_ref[...]
    run_ref[...] = run_in_ref[...]
    for k, kv_ref in zip(which, kv_refs):
        for half in range(0, NZ, 4):
            slots = [(half + i, k * NZ + half + i) for i in range(4)]
            attend_block(kv_ref, slots, queries, eff_ref, pos, run_ref, acc_ref)
    peak = run_ref[0:1, :]
    total = run_ref[1:2, :]
    mixed = acc_ref[...] / total
    own_out_ref[...] = mixed[:, :QROWS]
    stat_ref[0:1, :] = peak[:, :QROWS]
    stat_ref[1:2, :] = total[:, :QROWS]
    stat_ref[2:8, :] = jnp.zeros((6, QROWS), jnp.float32)
    peak = peak[:, QROWS:]
    total = total[:, QROWS:]
    peak_high = peak.astype(jnp.bfloat16).astype(jnp.float32)
    total_high = total.astype(jnp.bfloat16).astype(jnp.float32)
    stats = jnp.concatenate(
        [
            peak_high,
            peak - peak_high,
            total_high,
            total - total_high,
            jnp.zeros((12, QROWS), jnp.float32),
        ],
        axis=0,
    )
    sent_ref[:HD, :] = mixed[:, QROWS:].astype(jnp.bfloat16)
    sent_ref[HD:, :] = stats.astype(jnp.bfloat16)


def merge_kernel(own_ref, stat_ref, got_ref, out_ref):
    stats = got_ref[HD:, :].astype(jnp.float32)
    got_peak = stats[0:1, :] + stats[1:2, :]
    got_total = stats[2:3, :] + stats[3:4, :]
    peak = stat_ref[0:1, :]
    total = stat_ref[1:2, :]
    joint = jnp.maximum(peak, got_peak)
    mine = jnp.exp2(peak - joint) * total
    theirs = jnp.exp2(got_peak - joint) * got_total
    whole = mine + theirs
    mixed = own_ref[...] * (mine / whole) + got_ref[:HD, :].astype(jnp.float32) * (theirs / whole)
    turned = mixed.T.astype(jnp.bfloat16)
    for head in range(QS):
        out_ref[:, pl.ds(head * HD, HD)] = turned[head * ROWS : (head + 1) * ROWS, :]


def body(hidden, norm_gain, q_weight, kv_weight, cache_store, location, stretch_ids, rec_pos):
    x = lax.axis_index("x")
    z = lax.axis_index("z")
    y = lax.axis_index("y")
    c = lax.axis_index("c")
    my_tp = y * NC + c
    which_half = my_tp // KVH
    is_first = which_half == 0
    positions = rec_pos[0]
    own_list = stretch_ids[0]
    int_rows = jnp.arange(CH_DEV, dtype=jnp.int32)
    table = jnp.arange(location.shape[0], dtype=jnp.int32)

    store = lax.all_gather(cache_store[:, 0], "z", axis=0, tiled=True)

    blocks = hidden[0].reshape(NY, 8, 2, NC, HD).transpose(2, 0, 3, 1, 4)
    blocks = jnp.broadcast_to(blocks[None], (4, 2, NY, NC, 8, HD))
    blocks = blocks.reshape(NZ * NY * NC, 8, HD)
    blocks = lax.all_to_all(blocks, ("z", "y", "c"), 0, 0, tiled=True)
    blocks = blocks.reshape(NZ, NX, 4, 8, HD)
    blocks = lax.dynamic_index_in_dim(blocks, z // 2, 2, keepdims=False)
    blocks = jnp.concatenate([blocks, blocks], axis=1)
    blocks = lax.dynamic_slice_in_dim(blocks, x, NX, 1)
    blocks = blocks.transpose(0, 2, 1, 3).reshape(NZ, 8, NX * HD)
    tokens = lax.all_to_all(
        jnp.broadcast_to(blocks[None], (NY * NC, NZ, 8, NX * HD)), TP, 0, 0, tiled=True
    )

    listed = jnp.pad(own_list.astype(jnp.bfloat16)[None, :], ((0, 15), (0, COLS - MAXC)))
    weight = jnp.concatenate([q_weight[:, 0], kv_weight[:, 0]], axis=1)
    weight = jnp.concatenate([weight, listed], axis=0)
    weights = [weight] + [shifted(weight, "x", NX, -k) for k in range(1, NX)]
    gain = lax.dynamic_index_in_dim(norm_gain.reshape(NX, NZ, NC * HD), z, 1, keepdims=False)
    gain = lax.dynamic_slice_in_dim(jnp.concatenate([gain, gain], axis=0), x, NX, 0)
    gain = gain.astype(jnp.float32).reshape(1, NX * NC * HD)

    partial = call(
        project_kernel,
        jax.ShapeDtypeStruct((NZ, ROWS + 8, COLS), jnp.bfloat16),
        "project",
        flops=2 * NZ * ROWS * 1024 * COLS,
        bytes_accessed=1 << 22,
    )(tokens, gain, *weights)
    parts = lax.all_to_all(partial, "z", 0, 0, tiled=True)

    lists = jnp.stack([w[NC * HD, :MAXC] for w in weights]).astype(jnp.int32)
    steps = jnp.arange(NZ, dtype=jnp.int32)
    row_ids = (x * NZ + steps)[:, None] * CH_DEV + int_rows[None, :]
    here = location[None, None, :] == row_ids[:, :, None]
    held = jnp.sum(jnp.where(here, table, 0), axis=2)
    wanted = jnp.any(lists[:, :, None, None] == held[None, None], axis=1)
    send_rows = jnp.sum(jnp.where(wanted, int_rows, 0), axis=2) + steps[None, :] * CH_DEV
    send_rows, _ = lax.optimization_barrier((send_rows, partial[0, ROWS:, :HD]))
    arrived = [store[send_rows[0]]]
    for k in range(1, NX):
        arrived.append(shifted(store[send_rows[NX - k]], "x", NX, -k))

    frequency = jnp.exp(
        -math.log(theta_base) * jnp.arange(HD // 2, dtype=jnp.float32) / (HD // 2)
    )
    angles = positions.astype(jnp.float32)[:, None] * frequency[None, :]
    cos = jnp.cos(angles)
    sin = jnp.sin(angles)
    cos = jnp.concatenate([cos, cos], axis=1)
    sin = jnp.concatenate([-sin, sin], axis=1)
    fresh_cos = jnp.where(is_first, cos, 1.0)
    fresh_sin = jnp.where(is_first, sin, 0.0)
    scale = math.log2(math.e) / math.sqrt(HD)

    own = call(
        finish_kernel, jax.ShapeDtypeStruct((QROWS + ROWS, HD), jnp.bfloat16), "finish"
    )(parts, cos * scale, sin * scale, fresh_cos, fresh_sin)
    other = exchange(own)

    own_row = jnp.sum(jnp.where(own_list[:, None] == table[None, :], location[None, :], 0), axis=1)
    own_shard = own_row // CH_DEV
    slot_shard = (x * NZ + jnp.arange(MAXC, dtype=jnp.int32)) % (NX * NZ)
    match = (own_shard[None, :] == slot_shard[:, None]) & (own_list >= 0)[None, :]
    slot_order = jnp.sum(jnp.where(match, jnp.arange(MAXC, dtype=jnp.int32), 0), axis=1)
    slot_live = jnp.any(match, axis=1)
    key_pos = (
        slot_order[None, :] * STRETCH
        + which_half * HALF
        + jnp.arange(HALF, dtype=jnp.int32)[:, None]
    )
    replaced = jnp.any(key_pos[:, :, None] == positions[None, None, :], axis=2)
    eff = jnp.where(replaced | ~slot_live[None, :], far_away, key_pos)
    fresh_eff = jnp.where(positions % STRETCH // HALF == which_half, positions, far_away)
    fresh_eff = jnp.broadcast_to(fresh_eff[:, None], (ROWS, HD))
    pos_row = jnp.tile(positions, 2 * QS).reshape(1, 2 * QROWS)

    smem = pl.BlockSpec(memory_space=pltpu.SMEM)
    vmem = pl.BlockSpec(memory_space=pltpu.VMEM)
    early, late = (0, 1, 3), (2,)
    params = pltpu.CompilerParams(vmem_limit_bytes=32 * 1024 * 1024)
    run_shapes = [
        jax.ShapeDtypeStruct((HD, 2 * QROWS), jnp.float32),
        jax.ShapeDtypeStruct((8, 2 * QROWS), jnp.float32),
    ]

    def cost(count):
        pairs = count * NZ * HALF * 2 * QROWS
        return pl.CostEstimate(flops=4 * pairs * HD, bytes_accessed=count << 19, transcendentals=pairs)

    acc, run = pl.pallas_call(
        functools.partial(attend_early_kernel, early),
        out_shape=run_shapes,
        in_specs=[smem] + [vmem] * (5 + len(early)),
        out_specs=[vmem] * 2,
        name="attend_early",
        compiler_params=params,
        cost_estimate=cost(len(early)),
    )(which_half.reshape(1), own, other, eff, fresh_eff, pos_row, *[arrived[k] for k in early])
    own_part, stats, sent = pl.pallas_call(
        functools.partial(attend_late_kernel, late),
        out_shape=[
            jax.ShapeDtypeStruct((HD, QROWS), jnp.float32),
            jax.ShapeDtypeStruct((8, QROWS), jnp.float32),
            jax.ShapeDtypeStruct((HD + 16, QROWS), jnp.bfloat16),
        ],
        in_specs=[vmem] * (6 + len(late)),
        out_specs=[vmem] * 3,
        scratch_shapes=[pltpu.VMEM(r.shape, r.dtype) for r in run_shapes],
        name="attend_late",
        compiler_params=params,
        cost_estimate=cost(len(late)),
    )(own, other, eff, pos_row, acc, run, *[arrived[k] for k in late])
    got = exchange(sent)
    attended = call(merge_kernel, jax.ShapeDtypeStruct((ROWS, QW), jnp.bfloat16), "merge")(
        own_part, stats, got
    )
    return attended.reshape(1, ROWS, 1, QW)


def solution(mesh):
    fine = Mesh(mesh.devices.reshape(NX, NZ, NY, NC), ("x", "z", "y", "c"))
    in_specs = (
        P(STORE, None, TP),
        P(),
        P(STORE, TP, None),
        P(STORE, TP, None),
        P(STORE, TP, None, None),
        P(),
        P(STORE, None),
        P(STORE, None),
    )
    return jax.shard_map(
        body, mesh=fine, in_specs=in_specs, out_specs=P(STORE, None, TP, None), check_vma=False
    )
```

```python
import functools
import math

import jax
import jax.numpy as jnp
from jax import lax
from jax.experimental import pallas as pl
from jax.experimental.pallas import tpu as pltpu
from jax.sharding import Mesh
from jax.sharding import PartitionSpec as P

NX, NZ, NY, NC = 4, 8, 8, 2
KVH = 8
HD = 128
STRETCH = 256
MAXC = 32
CH_DEV = 8
QS = 4
HALF = 128
ROWS = 64
D = 8192
QW = QS * HD
COLS = QW + HD
QROWS = QS * ROWS

theta_base = 500000.0
neg_large = -1e30
far_away = 1 << 29

STORE = ("x", "z")
TP = ("y", "c")
NT = (((1,), (1,)), ((), ()))
TN = (((0,), (0,)), ((), ()))


def exchange(block):
    return lax.ppermute(block, "y", [(i, (i + NY // 2) % NY) for i in range(NY)])


def swap_cores(block):
    return lax.ppermute(block, "c", [(0, 1), (1, 0)])


def shifted(block, axis, count, by):
    return lax.ppermute(block, axis, [(i, (i + by) % count) for i in range(count)])


def call(kernel, outs, name, flops=0, bytes_accessed=0):
    return pl.pallas_call(
        kernel,
        out_shape=outs,
        name=name,
        compiler_params=pltpu.CompilerParams(vmem_limit_bytes=32 * 1024 * 1024),
        cost_estimate=pl.CostEstimate(
            flops=flops, bytes_accessed=bytes_accessed, transcendentals=0
        ),
    )


def project_kernel(core_ref, mine_ref, mate_ref, gain_ref, w0_ref, w1_ref, w2_ref, w3_ref, out_ref):
    weights = jnp.concatenate([w[: 2 * HD, :] for w in (w0_ref, w1_ref, w2_ref, w3_ref)], axis=0)
    gain = gain_ref[...]
    is_zero = core_ref[0] == 0
    rows = []
    stats = []
    for request in range(NZ):
        tall = []
        for y in range(NY):
            mine = mine_ref[y, request].astype(jnp.float32)
            mate = mate_ref[y, request].astype(jnp.float32)
            zero = jnp.broadcast_to(is_zero, mine.shape)
            halves = [jnp.where(zero, mine, mate), jnp.where(zero, mate, mine)]
            tall.append(
                jnp.concatenate(
                    [halves[c][:, k * HD : (k + 1) * HD] for k in range(NX) for c in range(NC)],
                    axis=1,
                )
            )
        wide = jnp.concatenate(tall, axis=0)
        rows.append((wide * gain).astype(jnp.bfloat16))
        squares = jnp.zeros((ROWS, HD), jnp.float32)
        for at in range(0, wide.shape[1], HD):
            piece = wide[:, at : at + HD]
            squares += piece * piece
        squares = jnp.concatenate([squares, jnp.zeros_like(squares)], axis=0)
        row = jnp.sum(squares.T, axis=0, keepdims=True)
        high = row.astype(jnp.bfloat16).astype(jnp.float32)
        stat = jnp.concatenate([high, row - high, jnp.zeros((6, HD), jnp.float32)], axis=0)
        stats.append(jnp.concatenate([stat, jnp.zeros((8, QW), jnp.float32)], axis=1))
    total = jnp.dot(jnp.concatenate(rows, axis=0), weights, preferred_element_type=jnp.float32)
    for request in range(NZ):
        block = total[request * ROWS : (request + 1) * ROWS]
        block = jnp.concatenate([block, stats[request]], axis=0)
        out_ref[request] = block.astype(jnp.bfloat16)


def finish_kernel(parts_ref, cos_ref, sin_ref, fcos_ref, fsin_ref, out_ref):
    inverse = None
    for group in range(QS + 1):
        lanes = pl.ds(group * HD, HD)
        total = parts_ref[0, :, lanes].astype(jnp.float32)
        for part in range(1, NZ):
            total += parts_ref[part, :, lanes].astype(jnp.float32)
        if inverse is None:
            squares = total[ROWS : ROWS + 1, :] + total[ROWS + 1 : ROWS + 2, :]
            inverse = lax.rsqrt(squares * (1.0 / D) + 1e-05)
            inverse = jnp.broadcast_to(inverse, (HD, HD)).T[:ROWS]
        total = total[:ROWS] * inverse
        cos = cos_ref[...] if group < QS else fcos_ref[...]
        sin = sin_ref[...] if group < QS else fsin_ref[...]
        turned = total * cos + pltpu.roll(total, HD // 2, 1) * sin
        out_ref[pl.ds(group * ROWS, ROWS), :] = turned.astype(jnp.bfloat16)


def pick_kernel(rows_ref, store_ref, *refs):
    outs, sem = refs[:NX], refs[NX]
    copies = []
    for k in (2, 1, 3, 0):
        for i in range(NZ):
            row = rows_ref[((NX - k) % NX) * NZ + i]
            copies.append(
                pltpu.make_async_copy(store_ref.at[row], outs[k].at[i], sem.at[k * NZ + i])
            )
            copies[-1].start()
    for copy in copies:
        copy.wait()


def attend_block(kv_ref, slots, queries, eff_ref, pos, run_ref, acc_ref):
    pieces = []
    for at, slot in slots:
        piece = lax.dot_general(
            kv_ref[at, :, :HD], queries, NT, preferred_element_type=jnp.float32
        )
        pieces.append(jnp.where(eff_ref[:, slot : slot + 1] <= pos, piece, neg_large))
    old_peak = run_ref[0:1, :]
    new_peak = old_peak
    for piece in pieces:
        new_peak = jnp.maximum(new_peak, jnp.max(piece, axis=0, keepdims=True))
    factor = jnp.exp2(old_peak - new_peak)
    total = run_ref[1:2, :] * factor
    acc = acc_ref[...] * factor
    for (at, _), piece in zip(slots, pieces):
        weights = jnp.exp2(piece - new_peak)
        total += jnp.sum(weights, axis=0, keepdims=True)
        acc += lax.dot_general(
            kv_ref[at, :, HD:], weights.astype(jnp.bfloat16), TN, preferred_element_type=jnp.float32
        )
    run_ref[0:1, :] = new_peak
    run_ref[1:2, :] = total
    acc_ref[...] = acc


def attend_early_kernel(which, flag_ref, own_ref, other_ref, eff_ref, fresh_eff_ref, pos_ref, *refs):
    kv_refs, (acc_ref, run_ref) = refs[: len(which)], refs[len(which) :]
    is_first = flag_ref[0] == 0
    queries = jnp.concatenate([own_ref[:QROWS, :], other_ref[:QROWS, :]], axis=0)
    own_piece = own_ref[QROWS:, :]
    other_piece = other_ref[QROWS:, :]
    first = jnp.broadcast_to(is_first, own_piece.shape)
    fresh_keys = jnp.where(first, own_piece, other_piece)
    fresh_values = jnp.where(first, other_piece, own_piece)
    pos = pos_ref[...]
    scores = lax.dot_general(fresh_keys, queries, NT, preferred_element_type=jnp.float32)
    scores = jnp.where(fresh_eff_ref[:, 0:1] <= pos, scores, neg_large)
    peak = jnp.max(scores, axis=0, keepdims=True)
    weights = jnp.exp2(scores - peak)
    run_ref[...] = jnp.zeros(run_ref.shape, jnp.float32)
    run_ref[0:1, :] = peak
    run_ref[1:2, :] = jnp.sum(weights, axis=0, keepdims=True)
    acc_ref[...] = lax.dot_general(
        fresh_values, weights.astype(jnp.bfloat16), TN, preferred_element_type=jnp.float32
    )
    for k, kv_ref in zip(which, kv_refs):
        for half in range(0, NZ, 4):
            slots = [(half + i, k * NZ + half + i) for i in range(4)]
            attend_block(kv_ref, slots, queries, eff_ref, pos, run_ref, acc_ref)


def attend_late_kernel(
    which, own_ref, other_ref, eff_ref, pos_ref, acc_in_ref, run_in_ref, *refs
):
    kv_refs, (own_out_ref, stat_ref, sent_ref, acc_ref, run_ref) = (
        refs[: len(which)],
        refs[len(which) :],
    )
    queries = jnp.concatenate([own_ref[:QROWS, :], other_ref[:QROWS, :]], axis=0)
    pos = pos_ref[...]
    acc_ref[...] = acc_in_ref[...]
    run_ref[...] = run_in_ref[...]
    for k, kv_ref in zip(which, kv_refs):
        for half in range(0, NZ, 4):
            slots = [(half + i, k * NZ + half + i) for i in range(4)]
            attend_block(kv_ref, slots, queries, eff_ref, pos, run_ref, acc_ref)
    peak = run_ref[0:1, :]
    total = run_ref[1:2, :]
    mixed = acc_ref[...] / total
    own_out_ref[...] = mixed[:, :QROWS]
    stat_ref[0:1, :] = peak[:, :QROWS]
    stat_ref[1:2, :] = total[:, :QROWS]
    stat_ref[2:8, :] = jnp.zeros((6, QROWS), jnp.float32)
    peak = peak[:, QROWS:]
    total = total[:, QROWS:]
    peak_high = peak.astype(jnp.bfloat16).astype(jnp.float32)
    total_high = total.astype(jnp.bfloat16).astype(jnp.float32)
    stats = jnp.concatenate(
        [
            peak_high,
            peak - peak_high,
            total_high,
            total - total_high,
            jnp.zeros((12, QROWS), jnp.float32),
        ],
        axis=0,
    )
    sent_ref[:HD, :] = mixed[:, QROWS:].astype(jnp.bfloat16)
    sent_ref[HD:, :] = stats.astype(jnp.bfloat16)


def merge_kernel(own_ref, stat_ref, got_ref, out_ref):
    stats = got_ref[HD:, :].astype(jnp.float32)
    got_peak = stats[0:1, :] + stats[1:2, :]
    got_total = stats[2:3, :] + stats[3:4, :]
    peak = stat_ref[0:1, :]
    total = stat_ref[1:2, :]
    joint = jnp.maximum(peak, got_peak)
    mine = jnp.exp2(peak - joint) * total
    theirs = jnp.exp2(got_peak - joint) * got_total
    whole = mine + theirs
    mixed = own_ref[...] * (mine / whole) + got_ref[:HD, :].astype(jnp.float32) * (theirs / whole)
    turned = mixed.T.astype(jnp.bfloat16)
    for head in range(QS):
        out_ref[:, pl.ds(head * HD, HD)] = turned[head * ROWS : (head + 1) * ROWS, :]


def body(hidden, norm_gain, q_weight, kv_weight, cache_store, location, stretch_ids, rec_pos):
    x = lax.axis_index("x")
    z = lax.axis_index("z")
    y = lax.axis_index("y")
    c = lax.axis_index("c")
    my_tp = y * NC + c
    which_half = my_tp // KVH
    is_first = which_half == 0
    positions = rec_pos[0]
    own_list = stretch_ids[0]
    int_rows = jnp.arange(CH_DEV, dtype=jnp.int32)
    table = jnp.arange(location.shape[0], dtype=jnp.int32)

    store = lax.all_gather(cache_store[:, 0], "z", axis=0, tiled=True)

    states = hidden[0].reshape(ROWS, 2, NC, HD)
    keep = lax.dynamic_index_in_dim(states, c, 2, keepdims=False)
    give = lax.dynamic_index_in_dim(states, 1 - c, 2, keepdims=False)
    taken = swap_cores(give)
    pairs = jnp.where(c == 0, jnp.stack([keep, taken]), jnp.stack([taken, keep]))
    blocks = pairs.reshape(2, NY, 8, 2, HD).transpose(0, 3, 1, 2, 4)
    blocks = jnp.broadcast_to(blocks[None], (2, 2, 2, NY, 8, HD)).reshape(NZ * NY, 8, HD)
    weight = jnp.concatenate([q_weight[:, 0], kv_weight[:, 0]], axis=1)
    blocks = lax.all_to_all(blocks, ("z", "y"), 0, 0, tiled=True)
    blocks = blocks.reshape(NZ, NX, 2, 8, HD)
    blocks = lax.dynamic_index_in_dim(blocks, z // 4, 2, keepdims=False)
    blocks = jnp.concatenate([blocks, blocks], axis=1)
    blocks = lax.dynamic_slice_in_dim(blocks, x, NX, 1)
    blocks = blocks.transpose(0, 2, 1, 3).reshape(NZ, 8, NX * HD)
    tokens = lax.all_to_all(
        jnp.broadcast_to(blocks[None], (NY, NZ, 8, NX * HD)), "y", 0, 0, tiled=True
    )
    mate_tokens = swap_cores(tokens)

    listed = jnp.pad(own_list.astype(jnp.bfloat16)[None, :], ((0, 15), (0, COLS - MAXC)))
    weight = jnp.concatenate([weight, listed], axis=0)
    weights = [weight] + [shifted(weight, "x", NX, -k) for k in range(1, NX)]
    gain = lax.dynamic_index_in_dim(norm_gain.reshape(NX, NZ, NC * HD), z, 1, keepdims=False)
    gain = lax.dynamic_slice_in_dim(jnp.concatenate([gain, gain], axis=0), x, NX, 0)
    gain = gain.astype(jnp.float32).reshape(1, NX * NC * HD)

    smem = pl.BlockSpec(memory_space=pltpu.SMEM)
    vmem = pl.BlockSpec(memory_space=pltpu.VMEM)
    partial = pl.pallas_call(
        project_kernel,
        out_shape=jax.ShapeDtypeStruct((NZ, ROWS + 8, COLS), jnp.bfloat16),
        in_specs=[smem] + [vmem] * 7,
        out_specs=vmem,
        name="project",
        compiler_params=pltpu.CompilerParams(vmem_limit_bytes=32 * 1024 * 1024),
        cost_estimate=pl.CostEstimate(
            flops=2 * NZ * ROWS * 1024 * COLS, bytes_accessed=1 << 22, transcendentals=0
        ),
    )(c.reshape(1), tokens, mate_tokens, gain, *weights)
    parts = lax.all_to_all(partial, "z", 0, 0, tiled=True)

    lists = jnp.stack([w[NC * HD, :MAXC] for w in weights]).astype(jnp.int32)
    steps = jnp.arange(NZ, dtype=jnp.int32)
    row_ids = (x * NZ + steps)[:, None] * CH_DEV + int_rows[None, :]
    here = location[None, None, :] == row_ids[:, :, None]
    held = jnp.sum(jnp.where(here, table, 0), axis=2)
    wanted = jnp.any(lists[:, :, None, None] == held[None, None], axis=1)
    send_rows = jnp.sum(jnp.where(wanted, int_rows, 0), axis=2) + steps[None, :] * CH_DEV
    send_rows, _ = lax.optimization_barrier((send_rows, partial[0, ROWS:, :HD]))
    picked = pl.pallas_call(
        pick_kernel,
        out_shape=[jax.ShapeDtypeStruct((NZ, HALF, 2 * HD), jnp.bfloat16)] * NX,
        in_specs=[smem, pl.BlockSpec(memory_space=pl.ANY)],
        out_specs=[vmem] * NX,
        scratch_shapes=[pltpu.SemaphoreType.DMA((NX * NZ,))],
        name="pick",
        compiler_params=pltpu.CompilerParams(vmem_limit_bytes=32 * 1024 * 1024),
        cost_estimate=pl.CostEstimate(flops=0, bytes_accessed=1 << 22, transcendentals=0),
    )(send_rows.reshape(-1), store)
    arrived = [picked[0]] + [shifted(picked[k], "x", NX, -k) for k in range(1, NX)]

    frequency = jnp.exp(
        -math.log(theta_base) * jnp.arange(HD // 2, dtype=jnp.float32) / (HD // 2)
    )
    angles = positions.astype(jnp.float32)[:, None] * frequency[None, :]
    cos = jnp.cos(angles)
    sin = jnp.sin(angles)
    cos = jnp.concatenate([cos, cos], axis=1)
    sin = jnp.concatenate([-sin, sin], axis=1)
    fresh_cos = jnp.where(is_first, cos, 1.0)
    fresh_sin = jnp.where(is_first, sin, 0.0)
    scale = math.log2(math.e) / math.sqrt(HD)

    own = call(
        finish_kernel, jax.ShapeDtypeStruct((QROWS + ROWS, HD), jnp.bfloat16), "finish"
    )(parts, cos * scale, sin * scale, fresh_cos, fresh_sin)
    other = exchange(own)

    own_row = jnp.sum(jnp.where(own_list[:, None] == table[None, :], location[None, :], 0), axis=1)
    own_shard = own_row // CH_DEV
    slot_shard = (x * NZ + jnp.arange(MAXC, dtype=jnp.int32)) % (NX * NZ)
    match = (own_shard[None, :] == slot_shard[:, None]) & (own_list >= 0)[None, :]
    slot_order = jnp.sum(jnp.where(match, jnp.arange(MAXC, dtype=jnp.int32), 0), axis=1)
    slot_live = jnp.any(match, axis=1)
    key_pos = (
        slot_order[None, :] * STRETCH
        + which_half * HALF
        + jnp.arange(HALF, dtype=jnp.int32)[:, None]
    )
    replaced = jnp.any(key_pos[:, :, None] == positions[None, None, :], axis=2)
    eff = jnp.where(replaced | ~slot_live[None, :], far_away, key_pos)
    fresh_eff = jnp.where(positions % STRETCH // HALF == which_half, positions, far_away)
    fresh_eff = jnp.broadcast_to(fresh_eff[:, None], (ROWS, HD))
    pos_row = jnp.tile(positions, 2 * QS).reshape(1, 2 * QROWS)

    early, late = (0, 1, 3), (2,)
    params = pltpu.CompilerParams(vmem_limit_bytes=32 * 1024 * 1024)
    run_shapes = [
        jax.ShapeDtypeStruct((HD, 2 * QROWS), jnp.float32),
        jax.ShapeDtypeStruct((8, 2 * QROWS), jnp.float32),
    ]

    def cost(count):
        pairs = count * NZ * HALF * 2 * QROWS
        return pl.CostEstimate(flops=4 * pairs * HD, bytes_accessed=count << 19, transcendentals=pairs)

    acc, run = pl.pallas_call(
        functools.partial(attend_early_kernel, early),
        out_shape=run_shapes,
        in_specs=[smem] + [vmem] * (5 + len(early)),
        out_specs=[vmem] * 2,
        name="attend_early",
        compiler_params=params,
        cost_estimate=cost(len(early)),
    )(which_half.reshape(1), own, other, eff, fresh_eff, pos_row, *[arrived[k] for k in early])
    own_part, stats, sent = pl.pallas_call(
        functools.partial(attend_late_kernel, late),
        out_shape=[
            jax.ShapeDtypeStruct((HD, QROWS), jnp.float32),
            jax.ShapeDtypeStruct((8, QROWS), jnp.float32),
            jax.ShapeDtypeStruct((HD + 16, QROWS), jnp.bfloat16),
        ],
        in_specs=[vmem] * (6 + len(late)),
        out_specs=[vmem] * 3,
        scratch_shapes=[pltpu.VMEM(r.shape, r.dtype) for r in run_shapes],
        name="attend_late",
        compiler_params=params,
        cost_estimate=cost(len(late)),
    )(own, other, eff, pos_row, acc, run, *[arrived[k] for k in late])
    got = exchange(sent)
    attended = call(merge_kernel, jax.ShapeDtypeStruct((ROWS, QW), jnp.bfloat16), "merge")(
        own_part, stats, got
    )
    return attended.reshape(1, ROWS, 1, QW)


def solution(mesh):
    fine = Mesh(mesh.devices.reshape(NX, NZ, NY, NC), ("x", "z", "y", "c"))
    in_specs = (
        P(STORE, None, TP),
        P(),
        P(STORE, TP, None),
        P(STORE, TP, None),
        P(STORE, TP, None, None),
        P(),
        P(STORE, None),
        P(STORE, None),
    )
    return jax.shard_map(
        body, mesh=fine, in_specs=in_specs, out_specs=P(STORE, None, TP, None), check_vma=False
    )
```

```python
import functools
import math

import jax
import jax.numpy as jnp
from jax import lax
from jax.experimental import pallas as pl
from jax.experimental.pallas import tpu as pltpu
from jax.sharding import Mesh
from jax.sharding import PartitionSpec as P

NX, NZ, NY, NC = 4, 8, 8, 2
KVH = 8
HD = 128
STRETCH = 256
MAXC = 32
CH_DEV = 8
QS = 4
HALF = 128
ROWS = 64
D = 8192
QW = QS * HD
COLS = QW + HD
QROWS = QS * ROWS

theta_base = 500000.0
neg_large = -1e30
far_away = 1 << 29

STORE = ("x", "z")
TP = ("y", "c")
NT = (((1,), (1,)), ((), ()))
TN = (((0,), (0,)), ((), ()))


def exchange(block):
    return lax.ppermute(block, "y", [(i, (i + NY // 2) % NY) for i in range(NY)])


def swap_cores(block):
    return lax.ppermute(block, "c", [(0, 1), (1, 0)])


def shifted(block, axis, count, by):
    return lax.ppermute(block, axis, [(i, (i + by) % count) for i in range(count)])


def call(kernel, outs, name, flops=0, bytes_accessed=0):
    return pl.pallas_call(
        kernel,
        out_shape=outs,
        name=name,
        compiler_params=pltpu.CompilerParams(vmem_limit_bytes=32 * 1024 * 1024),
        cost_estimate=pl.CostEstimate(
            flops=flops, bytes_accessed=bytes_accessed, transcendentals=0
        ),
    )


def project_kernel(core_ref, mine_ref, mate_ref, gain_ref, w0_ref, w1_ref, w2_ref, w3_ref, out_ref):
    weights = jnp.concatenate([w[: 2 * HD, :] for w in (w0_ref, w1_ref, w2_ref, w3_ref)], axis=0)
    gain = gain_ref[...]
    is_zero = core_ref[0] == 0
    rows = []
    stats = []
    for request in range(NZ):
        tall = []
        for y in range(NY):
            mine = mine_ref[y, request].astype(jnp.float32)
            mate = mate_ref[y, request].astype(jnp.float32)
            zero = jnp.broadcast_to(is_zero, mine.shape)
            halves = [jnp.where(zero, mine, mate), jnp.where(zero, mate, mine)]
            tall.append(
                jnp.concatenate(
                    [halves[c][:, k * HD : (k + 1) * HD] for k in range(NX) for c in range(NC)],
                    axis=1,
                )
            )
        wide = jnp.concatenate(tall, axis=0)
        rows.append((wide * gain).astype(jnp.bfloat16))
        squares = jnp.zeros((ROWS, HD), jnp.float32)
        for at in range(0, wide.shape[1], HD):
            piece = wide[:, at : at + HD]
            squares += piece * piece
        squares = jnp.concatenate([squares, jnp.zeros_like(squares)], axis=0)
        row = jnp.sum(squares.T, axis=0, keepdims=True)
        high = row.astype(jnp.bfloat16).astype(jnp.float32)
        stat = jnp.concatenate([high, row - high, jnp.zeros((6, HD), jnp.float32)], axis=0)
        stats.append(jnp.concatenate([stat, jnp.zeros((8, QW), jnp.float32)], axis=1))
    total = jnp.dot(jnp.concatenate(rows, axis=0), weights, preferred_element_type=jnp.float32)
    for request in range(NZ):
        block = total[request * ROWS : (request + 1) * ROWS]
        block = jnp.concatenate([block, stats[request]], axis=0)
        out_ref[request] = block.astype(jnp.bfloat16)


def finish_kernel(parts_ref, cos_ref, sin_ref, fcos_ref, fsin_ref, out_ref):
    inverse = None
    for group in range(QS + 1):
        lanes = pl.ds(group * HD, HD)
        total = parts_ref[0, :, lanes].astype(jnp.float32)
        for part in range(1, NZ):
            total += parts_ref[part, :, lanes].astype(jnp.float32)
        if inverse is None:
            squares = total[ROWS : ROWS + 1, :] + total[ROWS + 1 : ROWS + 2, :]
            inverse = lax.rsqrt(squares * (1.0 / D) + 1e-05)
            inverse = jnp.broadcast_to(inverse, (HD, HD)).T[:ROWS]
        total = total[:ROWS] * inverse
        cos = cos_ref[...] if group < QS else fcos_ref[...]
        sin = sin_ref[...] if group < QS else fsin_ref[...]
        turned = total * cos + pltpu.roll(total, HD // 2, 1) * sin
        out_ref[pl.ds(group * ROWS, ROWS), :] = turned.astype(jnp.bfloat16)


def pick_kernel(rows_ref, store_ref, *refs):
    outs, sem = refs[: NX - 1], refs[NX - 1]
    copies = []
    for k in (2, 1, 3):
        for i in range(NZ):
            row = rows_ref[(NX - k) * NZ + i]
            copies.append(
                pltpu.make_async_copy(
                    store_ref.at[row], outs[k - 1].at[i], sem.at[(k - 1) * NZ + i]
                )
            )
            copies[-1].start()
    for copy in copies:
        copy.wait()


def attend_block(kv_ref, slots, queries, eff_ref, pos, run_ref, acc_ref):
    pieces = []
    for at, slot in slots:
        piece = lax.dot_general(
            kv_ref[at, :, :HD], queries, NT, preferred_element_type=jnp.float32
        )
        pieces.append(jnp.where(eff_ref[:, slot : slot + 1] <= pos, piece, neg_large))
    old_peak = run_ref[0:1, :]
    new_peak = old_peak
    for piece in pieces:
        new_peak = jnp.maximum(new_peak, jnp.max(piece, axis=0, keepdims=True))
    factor = jnp.exp2(old_peak - new_peak)
    total = run_ref[1:2, :] * factor
    acc = acc_ref[...] * factor
    for (at, _), piece in zip(slots, pieces):
        weights = jnp.exp2(piece - new_peak)
        total += jnp.sum(weights, axis=0, keepdims=True)
        acc += lax.dot_general(
            kv_ref[at, :, HD:], weights.astype(jnp.bfloat16), TN, preferred_element_type=jnp.float32
        )
    run_ref[0:1, :] = new_peak
    run_ref[1:2, :] = total
    acc_ref[...] = acc


def attend_slots(k, kv_ref, queries, eff_ref, pos, run_ref, acc_ref):
    for half in range(0, NZ, 4):
        slots = [(half + i, k * NZ + half + i) for i in range(4)]
        attend_block(kv_ref, slots, queries, eff_ref, pos, run_ref, acc_ref)


def attend_own_kernel(
    flag_ref,
    rows_ref,
    own_ref,
    other_ref,
    eff_ref,
    fresh_eff_ref,
    pos_ref,
    store_ref,
    acc_ref,
    run_ref,
    kv_ref,
    sem,
):
    copies = [
        pltpu.make_async_copy(store_ref.at[rows_ref[i]], kv_ref.at[i], sem.at[i])
        for i in range(NZ)
    ]
    for copy in copies:
        copy.start()
    is_first = flag_ref[0] == 0
    queries = jnp.concatenate([own_ref[:QROWS, :], other_ref[:QROWS, :]], axis=0)
    own_piece = own_ref[QROWS:, :]
    other_piece = other_ref[QROWS:, :]
    first = jnp.broadcast_to(is_first, own_piece.shape)
    fresh_keys = jnp.where(first, own_piece, other_piece)
    fresh_values = jnp.where(first, other_piece, own_piece)
    pos = pos_ref[...]
    scores = lax.dot_general(fresh_keys, queries, NT, preferred_element_type=jnp.float32)
    scores = jnp.where(fresh_eff_ref[:, 0:1] <= pos, scores, neg_large)
    peak = jnp.max(scores, axis=0, keepdims=True)
    weights = jnp.exp2(scores - peak)
    run_ref[...] = jnp.zeros(run_ref.shape, jnp.float32)
    run_ref[0:1, :] = peak
    run_ref[1:2, :] = jnp.sum(weights, axis=0, keepdims=True)
    acc_ref[...] = lax.dot_general(
        fresh_values, weights.astype(jnp.bfloat16), TN, preferred_element_type=jnp.float32
    )
    for copy in copies:
        copy.wait()
    attend_slots(0, kv_ref, queries, eff_ref, pos, run_ref, acc_ref)


def attend_near_kernel(
    own_ref, other_ref, eff_ref, pos_ref, acc_in_ref, run_in_ref, kv1_ref, kv3_ref, acc_ref, run_ref
):
    queries = jnp.concatenate([own_ref[:QROWS, :], other_ref[:QROWS, :]], axis=0)
    acc_ref[...] = acc_in_ref[...]
    run_ref[...] = run_in_ref[...]
    attend_slots(1, kv1_ref, queries, eff_ref, pos_ref[...], run_ref, acc_ref)
    attend_slots(3, kv3_ref, queries, eff_ref, pos_ref[...], run_ref, acc_ref)


def attend_far_kernel(
    own_ref,
    other_ref,
    eff_ref,
    pos_ref,
    acc_in_ref,
    run_in_ref,
    kv2_ref,
    own_out_ref,
    stat_ref,
    sent_ref,
    acc_ref,
    run_ref,
):
    queries = jnp.concatenate([own_ref[:QROWS, :], other_ref[:QROWS, :]], axis=0)
    acc_ref[...] = acc_in_ref[...]
    run_ref[...] = run_in_ref[...]
    attend_slots(2, kv2_ref, queries, eff_ref, pos_ref[...], run_ref, acc_ref)
    peak = run_ref[0:1, :]
    total = run_ref[1:2, :]
    mixed = acc_ref[...] / total
    own_out_ref[...] = mixed[:, :QROWS]
    stat_ref[0:1, :] = peak[:, :QROWS]
    stat_ref[1:2, :] = total[:, :QROWS]
    stat_ref[2:8, :] = jnp.zeros((6, QROWS), jnp.float32)
    peak = peak[:, QROWS:]
    total = total[:, QROWS:]
    peak_high = peak.astype(jnp.bfloat16).astype(jnp.float32)
    total_high = total.astype(jnp.bfloat16).astype(jnp.float32)
    stats = jnp.concatenate(
        [
            peak_high,
            peak - peak_high,
            total_high,
            total - total_high,
            jnp.zeros((12, QROWS), jnp.float32),
        ],
        axis=0,
    )
    sent_ref[:HD, :] = mixed[:, QROWS:].astype(jnp.bfloat16)
    sent_ref[HD:, :] = stats.astype(jnp.bfloat16)


def merge_kernel(own_ref, stat_ref, got_ref, out_ref):
    stats = got_ref[HD:, :].astype(jnp.float32)
    got_peak = stats[0:1, :] + stats[1:2, :]
    got_total = stats[2:3, :] + stats[3:4, :]
    peak = stat_ref[0:1, :]
    total = stat_ref[1:2, :]
    joint = jnp.maximum(peak, got_peak)
    mine = jnp.exp2(peak - joint) * total
    theirs = jnp.exp2(got_peak - joint) * got_total
    whole = mine + theirs
    mixed = own_ref[...] * (mine / whole) + got_ref[:HD, :].astype(jnp.float32) * (theirs / whole)
    turned = mixed.T.astype(jnp.bfloat16)
    for head in range(QS):
        out_ref[:, pl.ds(head * HD, HD)] = turned[head * ROWS : (head + 1) * ROWS, :]


def body(hidden, norm_gain, q_weight, kv_weight, cache_store, location, stretch_ids, rec_pos):
    x = lax.axis_index("x")
    z = lax.axis_index("z")
    y = lax.axis_index("y")
    c = lax.axis_index("c")
    my_tp = y * NC + c
    which_half = my_tp // KVH
    is_first = which_half == 0
    positions = rec_pos[0]
    own_list = stretch_ids[0]
    int_rows = jnp.arange(CH_DEV, dtype=jnp.int32)
    table = jnp.arange(location.shape[0], dtype=jnp.int32)

    store = lax.all_gather(cache_store[:, 0], "z", axis=0, tiled=True)

    blocks = hidden[0].reshape(NY, 8, 2, NC, HD).transpose(0, 3, 2, 1, 4)
    blocks = lax.all_to_all(blocks.reshape(NY * NC, 2, 8, HD), TP, 0, 0, tiled=True)
    blocks = blocks.reshape(NX, 2, 2, 2, 8, HD).transpose(1, 2, 3, 0, 4, 5)
    blocks = blocks.reshape(NZ, NX, 8, HD)
    first_blocks = blocks
    blocks = lax.all_to_all(blocks, "z", 0, 0, tiled=True)
    blocks = jnp.concatenate([blocks, blocks], axis=1)
    blocks = lax.dynamic_slice_in_dim(blocks, x, NX, 1)
    blocks = blocks.transpose(0, 2, 1, 3).reshape(NZ, 8, NX * HD)
    tokens = lax.all_to_all(
        jnp.broadcast_to(blocks[None], (NY, NZ, 8, NX * HD)), "y", 0, 0, tiled=True
    )
    listed = jnp.pad(own_list.astype(jnp.bfloat16)[None, :], ((0, 15), (0, COLS - MAXC)))
    weight = jnp.concatenate([q_weight[:, 0], kv_weight[:, 0]], axis=1)
    weight = jnp.concatenate([weight, listed], axis=0)
    weight, blocks_seen = lax.optimization_barrier((weight, first_blocks))
    weights = [weight] + [shifted(weight, "x", NX, -k) for k in range(1, NX)]
    tokens, *weights = lax.optimization_barrier((tokens, *weights))
    mate_tokens = swap_cores(tokens)
    gain = lax.dynamic_index_in_dim(norm_gain.reshape(NX, NZ, NC * HD), z, 1, keepdims=False)
    gain = lax.dynamic_slice_in_dim(jnp.concatenate([gain, gain], axis=0), x, NX, 0)
    gain = gain.astype(jnp.float32).reshape(1, NX * NC * HD)

    smem = pl.BlockSpec(memory_space=pltpu.SMEM)
    vmem = pl.BlockSpec(memory_space=pltpu.VMEM)
    hbm = pl.BlockSpec(memory_space=pltpu.MemorySpace.HBM)
    partial = pl.pallas_call(
        project_kernel,
        out_shape=jax.ShapeDtypeStruct((NZ, ROWS + 8, COLS), jnp.bfloat16),
        in_specs=[smem] + [vmem] * 7,
        out_specs=vmem,
        name="project",
        compiler_params=pltpu.CompilerParams(vmem_limit_bytes=32 * 1024 * 1024),
        cost_estimate=pl.CostEstimate(
            flops=2 * NZ * ROWS * 1024 * COLS, bytes_accessed=1 << 22, transcendentals=0
        ),
    )(c.reshape(1), tokens, mate_tokens, gain, *weights)
    parts = lax.all_to_all(partial, "z", 0, 0, tiled=True)

    lists = jnp.stack([w[NC * HD, :MAXC] for w in weights]).astype(jnp.int32)
    steps = jnp.arange(NZ, dtype=jnp.int32)
    row_ids = (x * NZ + steps)[:, None] * CH_DEV + int_rows[None, :]
    here = location[None, None, :] == row_ids[:, :, None]
    held = jnp.sum(jnp.where(here, table, 0), axis=2)
    wanted = jnp.any(lists[:, :, None, None] == held[None, None], axis=1)
    send_rows = jnp.sum(jnp.where(wanted, int_rows, 0), axis=2) + steps[None, :] * CH_DEV
    send_rows, _ = lax.optimization_barrier((send_rows, partial[0, ROWS:, :HD]))
    picked = pl.pallas_call(
        pick_kernel,
        out_shape=[jax.ShapeDtypeStruct((NZ, HALF, 2 * HD), jnp.bfloat16)] * (NX - 1),
        in_specs=[smem, hbm],
        out_specs=[vmem] * (NX - 1),
        scratch_shapes=[pltpu.SemaphoreType.DMA(((NX - 1) * NZ,))],
        name="pick",
        compiler_params=pltpu.CompilerParams(vmem_limit_bytes=32 * 1024 * 1024),
        cost_estimate=pl.CostEstimate(flops=0, bytes_accessed=1 << 22, transcendentals=0),
    )(send_rows.reshape(-1), store)
    arrived = [None] + [shifted(picked[k - 1], "x", NX, -k) for k in range(1, NX)]

    frequency = jnp.exp(
        -math.log(theta_base) * jnp.arange(HD // 2, dtype=jnp.float32) / (HD // 2)
    )
    angles = positions.astype(jnp.float32)[:, None] * frequency[None, :]
    cos = jnp.cos(angles)
    sin = jnp.sin(angles)
    cos = jnp.concatenate([cos, cos], axis=1)
    sin = jnp.concatenate([-sin, sin], axis=1)
    fresh_cos = jnp.where(is_first, cos, 1.0)
    fresh_sin = jnp.where(is_first, sin, 0.0)
    scale = math.log2(math.e) / math.sqrt(HD)

    own = call(
        finish_kernel, jax.ShapeDtypeStruct((QROWS + ROWS, HD), jnp.bfloat16), "finish"
    )(parts, cos * scale, sin * scale, fresh_cos, fresh_sin)
    other = exchange(own)

    own_row = jnp.sum(jnp.where(own_list[:, None] == table[None, :], location[None, :], 0), axis=1)
    own_shard = own_row // CH_DEV
    slot_shard = (x * NZ + jnp.arange(MAXC, dtype=jnp.int32)) % (NX * NZ)
    match = (own_shard[None, :] == slot_shard[:, None]) & (own_list >= 0)[None, :]
    slot_order = jnp.sum(jnp.where(match, jnp.arange(MAXC, dtype=jnp.int32), 0), axis=1)
    slot_live = jnp.any(match, axis=1)
    key_pos = (
        slot_order[None, :] * STRETCH
        + which_half * HALF
        + jnp.arange(HALF, dtype=jnp.int32)[:, None]
    )
    replaced = jnp.any(key_pos[:, :, None] == positions[None, None, :], axis=2)
    eff = jnp.where(replaced | ~slot_live[None, :], far_away, key_pos)
    fresh_eff = jnp.where(positions % STRETCH // HALF == which_half, positions, far_away)
    fresh_eff = jnp.broadcast_to(fresh_eff[:, None], (ROWS, HD))
    pos_row = jnp.tile(positions, 2 * QS).reshape(1, 2 * QROWS)

    params = pltpu.CompilerParams(vmem_limit_bytes=32 * 1024 * 1024)
    run_shapes = [
        jax.ShapeDtypeStruct((HD, 2 * QROWS), jnp.float32),
        jax.ShapeDtypeStruct((8, 2 * QROWS), jnp.float32),
    ]

    def cost(count):
        pairs = count * NZ * HALF * 2 * QROWS
        return pl.CostEstimate(flops=4 * pairs * HD, bytes_accessed=count << 19, transcendentals=pairs)

    acc, run = pl.pallas_call(
        attend_own_kernel,
        out_shape=run_shapes,
        in_specs=[smem] * 2 + [vmem] * 5 + [hbm],
        out_specs=[vmem] * 2,
        scratch_shapes=[
            pltpu.VMEM((NZ, HALF, 2 * HD), jnp.bfloat16),
            pltpu.SemaphoreType.DMA((NZ,)),
        ],
        name="attend_own",
        compiler_params=params,
        cost_estimate=cost(1),
    )(which_half.reshape(1), send_rows[0], own, other, eff, fresh_eff, pos_row, store)
    acc, run = pl.pallas_call(
        attend_near_kernel,
        out_shape=run_shapes,
        in_specs=[vmem] * 8,
        out_specs=[vmem] * 2,
        name="attend_near",
        compiler_params=params,
        cost_estimate=cost(2),
    )(own, other, eff, pos_row, acc, run, arrived[1], arrived[3])
    own_part, stats, sent = pl.pallas_call(
        attend_far_kernel,
        out_shape=[
            jax.ShapeDtypeStruct((HD, QROWS), jnp.float32),
            jax.ShapeDtypeStruct((8, QROWS), jnp.float32),
            jax.ShapeDtypeStruct((HD + 16, QROWS), jnp.bfloat16),
        ],
        in_specs=[vmem] * 7,
        out_specs=[vmem] * 3,
        scratch_shapes=[pltpu.VMEM(r.shape, r.dtype) for r in run_shapes],
        name="attend_far",
        compiler_params=params,
        cost_estimate=cost(1),
    )(own, other, eff, pos_row, acc, run, arrived[2])
    got = exchange(sent)
    attended = call(merge_kernel, jax.ShapeDtypeStruct((ROWS, QW), jnp.bfloat16), "merge")(
        own_part, stats, got
    )
    return attended.reshape(1, ROWS, 1, QW)


def solution(mesh):
    fine = Mesh(mesh.devices.reshape(NX, NZ, NY, NC), ("x", "z", "y", "c"))
    in_specs = (
        P(STORE, None, TP),
        P(),
        P(STORE, TP, None),
        P(STORE, TP, None),
        P(STORE, TP, None, None),
        P(),
        P(STORE, None),
        P(STORE, None),
    )
    return jax.shard_map(
        body, mesh=fine, in_specs=in_specs, out_specs=P(STORE, None, TP, None), check_vma=False
    )
```

```python
import functools
import math

import jax
import jax.numpy as jnp
from jax import lax
from jax.experimental import pallas as pl
from jax.experimental.pallas import tpu as pltpu
from jax.sharding import Mesh
from jax.sharding import PartitionSpec as P

NX, NZ, NY, NC = 4, 8, 8, 2
KVH = 8
HD = 128
STRETCH = 256
MAXC = 32
CH_DEV = 8
QS = 4
HALF = 128
ROWS = 64
D = 8192
QW = QS * HD
COLS = QW + HD
QROWS = QS * ROWS

theta_base = 500000.0
neg_large = -1e30
far_away = 1 << 29

STORE = ("x", "z")
TP = ("y", "c")
NT = (((1,), (1,)), ((), ()))
TN = (((0,), (0,)), ((), ()))


def exchange(block):
    return lax.ppermute(block, "y", [(i, (i + NY // 2) % NY) for i in range(NY)])


def swap_cores(block):
    return lax.ppermute(block, "c", [(0, 1), (1, 0)])


def shifted(block, axis, count, by):
    return lax.ppermute(block, axis, [(i, (i + by) % count) for i in range(count)])


def call(kernel, outs, name, flops=0, bytes_accessed=0):
    return pl.pallas_call(
        kernel,
        out_shape=outs,
        name=name,
        compiler_params=pltpu.CompilerParams(vmem_limit_bytes=32 * 1024 * 1024),
        cost_estimate=pl.CostEstimate(
            flops=flops, bytes_accessed=bytes_accessed, transcendentals=0
        ),
    )


def project_kernel(core_ref, mine_ref, mate_ref, gain_ref, w0_ref, w1_ref, w2_ref, w3_ref, out_ref):
    weights = jnp.concatenate([w[: 2 * HD, :] for w in (w0_ref, w1_ref, w2_ref, w3_ref)], axis=0)
    gain = gain_ref[...]
    is_zero = core_ref[0] == 0
    rows = []
    stats = []
    for request in range(NZ):
        tall = []
        for y in range(NY):
            mine = mine_ref[y, request].astype(jnp.float32)
            mate = mate_ref[y, request].astype(jnp.float32)
            zero = jnp.broadcast_to(is_zero, mine.shape)
            halves = [jnp.where(zero, mine, mate), jnp.where(zero, mate, mine)]
            tall.append(
                jnp.concatenate(
                    [halves[c][:, k * HD : (k + 1) * HD] for k in range(NX) for c in range(NC)],
                    axis=1,
                )
            )
        wide = jnp.concatenate(tall, axis=0)
        rows.append((wide * gain).astype(jnp.bfloat16))
        squares = jnp.zeros((ROWS, HD), jnp.float32)
        for at in range(0, wide.shape[1], HD):
            piece = wide[:, at : at + HD]
            squares += piece * piece
        squares = jnp.concatenate([squares, jnp.zeros_like(squares)], axis=0)
        row = jnp.sum(squares.T, axis=0, keepdims=True)
        high = row.astype(jnp.bfloat16).astype(jnp.float32)
        stat = jnp.concatenate([high, row - high, jnp.zeros((6, HD), jnp.float32)], axis=0)
        stats.append(jnp.concatenate([stat, jnp.zeros((8, QW), jnp.float32)], axis=1))
    total = jnp.dot(jnp.concatenate(rows, axis=0), weights, preferred_element_type=jnp.float32)
    for request in range(NZ):
        block = total[request * ROWS : (request + 1) * ROWS]
        block = jnp.concatenate([block, stats[request]], axis=0)
        out_ref[request] = block.astype(jnp.bfloat16)


def finish_kernel(parts_ref, cos_ref, sin_ref, fcos_ref, fsin_ref, out_ref):
    inverse = None
    for group in range(QS + 1):
        lanes = pl.ds(group * HD, HD)
        total = parts_ref[0, :, lanes].astype(jnp.float32)
        for part in range(1, NZ):
            total += parts_ref[part, :, lanes].astype(jnp.float32)
        if inverse is None:
            squares = total[ROWS : ROWS + 1, :] + total[ROWS + 1 : ROWS + 2, :]
            inverse = lax.rsqrt(squares * (1.0 / D) + 1e-05)
            inverse = jnp.broadcast_to(inverse, (HD, HD)).T[:ROWS]
        total = total[:ROWS] * inverse
        cos = cos_ref[...] if group < QS else fcos_ref[...]
        sin = sin_ref[...] if group < QS else fsin_ref[...]
        turned = total * cos + pltpu.roll(total, HD // 2, 1) * sin
        out_ref[pl.ds(group * ROWS, ROWS), :] = turned.astype(jnp.bfloat16)


def pick_kernel(rows_ref, store_ref, *refs):
    outs, sem = refs[: NX - 1], refs[NX - 1]
    copies = []
    for k in (2, 1, 3):
        for i in range(NZ):
            row = rows_ref[(NX - k) * NZ + i]
            copies.append(
                pltpu.make_async_copy(
                    store_ref.at[row], outs[k - 1].at[i], sem.at[(k - 1) * NZ + i]
                )
            )
            copies[-1].start()
    for copy in copies:
        copy.wait()


def attend_block(kv_ref, slots, queries, eff_ref, pos, run_ref, acc_ref):
    pieces = []
    for at, slot in slots:
        piece = lax.dot_general(
            kv_ref[at, :, :HD], queries, NT, preferred_element_type=jnp.float32
        )
        pieces.append(jnp.where(eff_ref[:, slot : slot + 1] <= pos, piece, neg_large))
    old_peak = run_ref[0:1, :]
    new_peak = old_peak
    for piece in pieces:
        new_peak = jnp.maximum(new_peak, jnp.max(piece, axis=0, keepdims=True))
    factor = jnp.exp2(old_peak - new_peak)
    total = run_ref[1:2, :] * factor
    acc = acc_ref[...] * factor
    for (at, _), piece in zip(slots, pieces):
        weights = jnp.exp2(piece - new_peak)
        total += jnp.sum(weights, axis=0, keepdims=True)
        acc += lax.dot_general(
            kv_ref[at, :, HD:], weights.astype(jnp.bfloat16), TN, preferred_element_type=jnp.float32
        )
    run_ref[0:1, :] = new_peak
    run_ref[1:2, :] = total
    acc_ref[...] = acc


def attend_slots(k, kv_ref, queries, eff_ref, pos, run_ref, acc_ref):
    for half in range(0, NZ, 4):
        slots = [(half + i, k * NZ + half + i) for i in range(4)]
        attend_block(kv_ref, slots, queries, eff_ref, pos, run_ref, acc_ref)


def attend_own_kernel(
    flag_ref,
    rows_ref,
    own_ref,
    other_ref,
    eff_ref,
    fresh_eff_ref,
    pos_ref,
    store_ref,
    acc_ref,
    run_ref,
    kv_ref,
    sem,
):
    copies = [
        pltpu.make_async_copy(store_ref.at[rows_ref[i]], kv_ref.at[i], sem.at[i])
        for i in range(NZ)
    ]
    for copy in copies:
        copy.start()
    is_first = flag_ref[0] == 0
    queries = jnp.concatenate([own_ref[:QROWS, :], other_ref[:QROWS, :]], axis=0)
    own_piece = own_ref[QROWS:, :]
    other_piece = other_ref[QROWS:, :]
    first = jnp.broadcast_to(is_first, own_piece.shape)
    fresh_keys = jnp.where(first, own_piece, other_piece)
    fresh_values = jnp.where(first, other_piece, own_piece)
    pos = pos_ref[...]
    scores = lax.dot_general(fresh_keys, queries, NT, preferred_element_type=jnp.float32)
    scores = jnp.where(fresh_eff_ref[:, 0:1] <= pos, scores, neg_large)
    peak = jnp.max(scores, axis=0, keepdims=True)
    weights = jnp.exp2(scores - peak)
    run_ref[...] = jnp.zeros(run_ref.shape, jnp.float32)
    run_ref[0:1, :] = peak
    run_ref[1:2, :] = jnp.sum(weights, axis=0, keepdims=True)
    acc_ref[...] = lax.dot_general(
        fresh_values, weights.astype(jnp.bfloat16), TN, preferred_element_type=jnp.float32
    )
    for copy in copies:
        copy.wait()
    attend_slots(0, kv_ref, queries, eff_ref, pos, run_ref, acc_ref)


def attend_near_kernel(
    own_ref, other_ref, eff_ref, pos_ref, acc_in_ref, run_in_ref, kv1_ref, kv3_ref, acc_ref, run_ref
):
    queries = jnp.concatenate([own_ref[:QROWS, :], other_ref[:QROWS, :]], axis=0)
    acc_ref[...] = acc_in_ref[...]
    run_ref[...] = run_in_ref[...]
    attend_slots(1, kv1_ref, queries, eff_ref, pos_ref[...], run_ref, acc_ref)
    attend_slots(3, kv3_ref, queries, eff_ref, pos_ref[...], run_ref, acc_ref)


def attend_far_kernel(
    own_ref,
    other_ref,
    eff_ref,
    pos_ref,
    acc_in_ref,
    run_in_ref,
    kv2_ref,
    own_out_ref,
    stat_ref,
    sent_ref,
    acc_ref,
    run_ref,
):
    queries = jnp.concatenate([own_ref[:QROWS, :], other_ref[:QROWS, :]], axis=0)
    acc_ref[...] = acc_in_ref[...]
    run_ref[...] = run_in_ref[...]
    attend_slots(2, kv2_ref, queries, eff_ref, pos_ref[...], run_ref, acc_ref)
    peak = run_ref[0:1, :]
    total = run_ref[1:2, :]
    mixed = acc_ref[...] / total
    own_out_ref[...] = mixed[:, :QROWS]
    stat_ref[0:1, :] = peak[:, :QROWS]
    stat_ref[1:2, :] = total[:, :QROWS]
    stat_ref[2:8, :] = jnp.zeros((6, QROWS), jnp.float32)
    peak = peak[:, QROWS:]
    total = total[:, QROWS:]
    peak_high = peak.astype(jnp.bfloat16).astype(jnp.float32)
    total_high = total.astype(jnp.bfloat16).astype(jnp.float32)
    stats = jnp.concatenate(
        [
            peak_high,
            peak - peak_high,
            total_high,
            total - total_high,
            jnp.zeros((12, QROWS), jnp.float32),
        ],
        axis=0,
    )
    sent_ref[:HD, :] = mixed[:, QROWS:].astype(jnp.bfloat16)
    sent_ref[HD:, :] = stats.astype(jnp.bfloat16)


def merge_kernel(own_ref, stat_ref, got_ref, out_ref):
    stats = got_ref[HD:, :].astype(jnp.float32)
    got_peak = stats[0:1, :] + stats[1:2, :]
    got_total = stats[2:3, :] + stats[3:4, :]
    peak = stat_ref[0:1, :]
    total = stat_ref[1:2, :]
    joint = jnp.maximum(peak, got_peak)
    mine = jnp.exp2(peak - joint) * total
    theirs = jnp.exp2(got_peak - joint) * got_total
    whole = mine + theirs
    mixed = own_ref[...] * (mine / whole) + got_ref[:HD, :].astype(jnp.float32) * (theirs / whole)
    turned = mixed.T.astype(jnp.bfloat16)
    for head in range(QS):
        out_ref[:, pl.ds(head * HD, HD)] = turned[head * ROWS : (head + 1) * ROWS, :]


def body(hidden, norm_gain, q_weight, kv_weight, cache_store, location, stretch_ids, rec_pos):
    x = lax.axis_index("x")
    z = lax.axis_index("z")
    y = lax.axis_index("y")
    c = lax.axis_index("c")
    my_tp = y * NC + c
    which_half = my_tp // KVH
    is_first = which_half == 0
    positions = rec_pos[0]
    own_list = stretch_ids[0]
    int_rows = jnp.arange(CH_DEV, dtype=jnp.int32)
    table = jnp.arange(location.shape[0], dtype=jnp.int32)

    store = lax.all_gather(cache_store[:, 0], "z", axis=0, tiled=True)

    listed = jnp.pad(own_list.astype(jnp.bfloat16)[None, :], ((0, 15), (0, COLS - MAXC)))
    weight = jnp.concatenate([q_weight[:, 0], kv_weight[:, 0]], axis=1)
    weight = jnp.concatenate([weight, listed], axis=0)

    blocks = hidden[0].reshape(NY, 8, 2, NC, HD).transpose(0, 3, 2, 1, 4)
    blocks = lax.all_to_all(blocks.reshape(NY * NC, 2, 8, HD), TP, 0, 0, tiled=True)
    blocks = blocks.reshape(NX, 2, 2, 2, 8, HD).transpose(1, 2, 3, 0, 4, 5)
    blocks = blocks.reshape(NZ, NX, 8, HD)
    blocks, weight = lax.optimization_barrier((blocks, weight))
    weights = [weight] + [shifted(weight, "x", NX, -k) for k in range(1, NX)]
    blocks = lax.all_to_all(blocks, "z", 0, 0, tiled=True)
    blocks, first_weight = lax.optimization_barrier((blocks, weights[2]))
    weights[2] = first_weight
    blocks = jnp.concatenate([blocks, blocks], axis=1)
    blocks = lax.dynamic_slice_in_dim(blocks, x, NX, 1)
    blocks = blocks.transpose(0, 2, 1, 3).reshape(NZ, 8, NX * HD)
    tokens = lax.all_to_all(
        jnp.broadcast_to(blocks[None], (NY, NZ, 8, NX * HD)), "y", 0, 0, tiled=True
    )
    tokens, *weights = lax.optimization_barrier((tokens, *weights))
    mate_tokens = swap_cores(tokens)
    gain = lax.dynamic_index_in_dim(norm_gain.reshape(NX, NZ, NC * HD), z, 1, keepdims=False)
    gain = lax.dynamic_slice_in_dim(jnp.concatenate([gain, gain], axis=0), x, NX, 0)
    gain = gain.astype(jnp.float32).reshape(1, NX * NC * HD)

    smem = pl.BlockSpec(memory_space=pltpu.SMEM)
    vmem = pl.BlockSpec(memory_space=pltpu.VMEM)
    hbm = pl.BlockSpec(memory_space=pltpu.MemorySpace.HBM)
    partial = pl.pallas_call(
        project_kernel,
        out_shape=jax.ShapeDtypeStruct((NZ, ROWS + 8, COLS), jnp.bfloat16),
        in_specs=[smem] + [vmem] * 7,
        out_specs=vmem,
        name="project",
        compiler_params=pltpu.CompilerParams(vmem_limit_bytes=32 * 1024 * 1024),
        cost_estimate=pl.CostEstimate(
            flops=2 * NZ * ROWS * 1024 * COLS, bytes_accessed=1 << 22, transcendentals=0
        ),
    )(c.reshape(1), tokens, mate_tokens, gain, *weights)
    parts = lax.all_to_all(partial, "z", 0, 0, tiled=True)

    lists = jnp.stack([w[NC * HD, :MAXC] for w in weights]).astype(jnp.int32)
    steps = jnp.arange(NZ, dtype=jnp.int32)
    row_ids = (x * NZ + steps)[:, None] * CH_DEV + int_rows[None, :]
    here = location[None, None, :] == row_ids[:, :, None]
    held = jnp.sum(jnp.where(here, table, 0), axis=2)
    wanted = jnp.any(lists[:, :, None, None] == held[None, None], axis=1)
    send_rows = jnp.sum(jnp.where(wanted, int_rows, 0), axis=2) + steps[None, :] * CH_DEV
    send_rows, _ = lax.optimization_barrier((send_rows, partial[0, ROWS:, :HD]))
    picked = pl.pallas_call(
        pick_kernel,
        out_shape=[jax.ShapeDtypeStruct((NZ, HALF, 2 * HD), jnp.bfloat16)] * (NX - 1),
        in_specs=[smem, hbm],
        out_specs=[vmem] * (NX - 1),
        scratch_shapes=[pltpu.SemaphoreType.DMA(((NX - 1) * NZ,))],
        name="pick",
        compiler_params=pltpu.CompilerParams(vmem_limit_bytes=60 * 1024 * 1024),
        cost_estimate=pl.CostEstimate(flops=0, bytes_accessed=1 << 22, transcendentals=0),
    )(send_rows.reshape(-1), store)
    arrived = [None] + [shifted(picked[k - 1], "x", NX, -k) for k in range(1, NX)]

    frequency = jnp.exp(
        -math.log(theta_base) * jnp.arange(HD // 2, dtype=jnp.float32) / (HD // 2)
    )
    angles = positions.astype(jnp.float32)[:, None] * frequency[None, :]
    cos = jnp.cos(angles)
    sin = jnp.sin(angles)
    cos = jnp.concatenate([cos, cos], axis=1)
    sin = jnp.concatenate([-sin, sin], axis=1)
    fresh_cos = jnp.where(is_first, cos, 1.0)
    fresh_sin = jnp.where(is_first, sin, 0.0)
    scale = math.log2(math.e) / math.sqrt(HD)

    own = call(
        finish_kernel, jax.ShapeDtypeStruct((QROWS + ROWS, HD), jnp.bfloat16), "finish"
    )(parts, cos * scale, sin * scale, fresh_cos, fresh_sin)
    other = exchange(own)

    own_row = jnp.sum(jnp.where(own_list[:, None] == table[None, :], location[None, :], 0), axis=1)
    own_shard = own_row // CH_DEV
    slot_shard = (x * NZ + jnp.arange(MAXC, dtype=jnp.int32)) % (NX * NZ)
    match = (own_shard[None, :] == slot_shard[:, None]) & (own_list >= 0)[None, :]
    slot_order = jnp.sum(jnp.where(match, jnp.arange(MAXC, dtype=jnp.int32), 0), axis=1)
    slot_live = jnp.any(match, axis=1)
    key_pos = (
        slot_order[None, :] * STRETCH
        + which_half * HALF
        + jnp.arange(HALF, dtype=jnp.int32)[:, None]
    )
    replaced = jnp.any(key_pos[:, :, None] == positions[None, None, :], axis=2)
    eff = jnp.where(replaced | ~slot_live[None, :], far_away, key_pos)
    fresh_eff = jnp.where(positions % STRETCH // HALF == which_half, positions, far_away)
    fresh_eff = jnp.broadcast_to(fresh_eff[:, None], (ROWS, HD))
    pos_row = jnp.tile(positions, 2 * QS).reshape(1, 2 * QROWS)

    params = pltpu.CompilerParams(vmem_limit_bytes=32 * 1024 * 1024)
    run_shapes = [
        jax.ShapeDtypeStruct((HD, 2 * QROWS), jnp.float32),
        jax.ShapeDtypeStruct((8, 2 * QROWS), jnp.float32),
    ]

    def cost(count):
        pairs = count * NZ * HALF * 2 * QROWS
        return pl.CostEstimate(flops=4 * pairs * HD, bytes_accessed=count << 19, transcendentals=pairs)

    acc, run = pl.pallas_call(
        attend_own_kernel,
        out_shape=run_shapes,
        in_specs=[smem] * 2 + [vmem] * 5 + [hbm],
        out_specs=[vmem] * 2,
        scratch_shapes=[
            pltpu.VMEM((NZ, HALF, 2 * HD), jnp.bfloat16),
            pltpu.SemaphoreType.DMA((NZ,)),
        ],
        name="attend_own",
        compiler_params=pltpu.CompilerParams(vmem_limit_bytes=60 * 1024 * 1024),
        cost_estimate=cost(1),
    )(which_half.reshape(1), send_rows[0], own, other, eff, fresh_eff, pos_row, store)
    acc, run = pl.pallas_call(
        attend_near_kernel,
        out_shape=run_shapes,
        in_specs=[vmem] * 8,
        out_specs=[vmem] * 2,
        name="attend_near",
        compiler_params=params,
        cost_estimate=cost(2),
    )(own, other, eff, pos_row, acc, run, arrived[1], arrived[3])
    own_part, stats, sent = pl.pallas_call(
        attend_far_kernel,
        out_shape=[
            jax.ShapeDtypeStruct((HD, QROWS), jnp.float32),
            jax.ShapeDtypeStruct((8, QROWS), jnp.float32),
            jax.ShapeDtypeStruct((HD + 16, QROWS), jnp.bfloat16),
        ],
        in_specs=[vmem] * 7,
        out_specs=[vmem] * 3,
        scratch_shapes=[pltpu.VMEM(r.shape, r.dtype) for r in run_shapes],
        name="attend_far",
        compiler_params=params,
        cost_estimate=cost(1),
    )(own, other, eff, pos_row, acc, run, arrived[2])
    got = exchange(sent)
    attended = call(merge_kernel, jax.ShapeDtypeStruct((ROWS, QW), jnp.bfloat16), "merge")(
        own_part, stats, got
    )
    return attended.reshape(1, ROWS, 1, QW)


def solution(mesh):
    fine = Mesh(mesh.devices.reshape(NX, NZ, NY, NC), ("x", "z", "y", "c"))
    in_specs = (
        P(STORE, None, TP),
        P(),
        P(STORE, TP, None),
        P(STORE, TP, None),
        P(STORE, TP, None, None),
        P(),
        P(STORE, None),
        P(STORE, None),
    )
    return jax.shard_map(
        body, mesh=fine, in_specs=in_specs, out_specs=P(STORE, None, TP, None), check_vma=False
    )
```

```python
import functools
import math

import jax
import jax.numpy as jnp
from jax import lax
from jax.experimental import pallas as pl
from jax.experimental.pallas import tpu as pltpu
from jax.sharding import Mesh
from jax.sharding import PartitionSpec as P

NX, NZ, NY, NC = 4, 8, 8, 2
KVH = 8
HD = 128
STRETCH = 256
MAXC = 32
CH_DEV = 8
QS = 4
HALF = 128
ROWS = 64
D = 8192
QW = QS * HD
COLS = QW + HD
QROWS = QS * ROWS

theta_base = 500000.0
neg_large = -1e30
far_away = 1 << 29

STORE = ("x", "z")
TP = ("y", "c")
NT = (((1,), (1,)), ((), ()))
TN = (((0,), (0,)), ((), ()))


def exchange(block):
    return lax.ppermute(block, "y", [(i, (i + NY // 2) % NY) for i in range(NY)])


def swap_cores(block):
    return lax.ppermute(block, "c", [(0, 1), (1, 0)])


def shifted(block, axis, count, by):
    return lax.ppermute(block, axis, [(i, (i + by) % count) for i in range(count)])


def call(kernel, outs, name, flops=0, bytes_accessed=0):
    return pl.pallas_call(
        kernel,
        out_shape=outs,
        name=name,
        compiler_params=pltpu.CompilerParams(vmem_limit_bytes=32 * 1024 * 1024),
        cost_estimate=pl.CostEstimate(
            flops=flops, bytes_accessed=bytes_accessed, transcendentals=0
        ),
    )


def project_kernel(core_ref, mine_ref, mate_ref, gain_ref, w0_ref, w1_ref, w2_ref, w3_ref, out_ref):
    weights = jnp.concatenate([w[: 2 * HD, :] for w in (w0_ref, w1_ref, w2_ref, w3_ref)], axis=0)
    gain = gain_ref[...]
    is_zero = core_ref[0] == 0
    rows = []
    stats = []
    for request in range(NZ):
        tall = []
        for y in range(NY):
            mine = mine_ref[y, request].astype(jnp.float32)
            mate = mate_ref[y, request].astype(jnp.float32)
            zero = jnp.broadcast_to(is_zero, mine.shape)
            halves = [jnp.where(zero, mine, mate), jnp.where(zero, mate, mine)]
            tall.append(
                jnp.concatenate(
                    [halves[c][:, k * HD : (k + 1) * HD] for k in range(NX) for c in range(NC)],
                    axis=1,
                )
            )
        wide = jnp.concatenate(tall, axis=0)
        rows.append((wide * gain).astype(jnp.bfloat16))
        squares = jnp.zeros((ROWS, HD), jnp.float32)
        for at in range(0, wide.shape[1], HD):
            piece = wide[:, at : at + HD]
            squares += piece * piece
        squares = jnp.concatenate([squares, jnp.zeros_like(squares)], axis=0)
        row = jnp.sum(squares.T, axis=0, keepdims=True)
        high = row.astype(jnp.bfloat16).astype(jnp.float32)
        stat = jnp.concatenate([high, row - high, jnp.zeros((6, HD), jnp.float32)], axis=0)
        stats.append(jnp.concatenate([stat, jnp.zeros((8, QW), jnp.float32)], axis=1))
    total = jnp.dot(jnp.concatenate(rows, axis=0), weights, preferred_element_type=jnp.float32)
    for request in range(NZ):
        block = total[request * ROWS : (request + 1) * ROWS]
        block = jnp.concatenate([block, stats[request]], axis=0)
        out_ref[request] = block.astype(jnp.bfloat16)


def finish_kernel(parts_ref, cos_ref, sin_ref, fcos_ref, fsin_ref, out_ref):
    inverse = None
    for group in range(QS + 1):
        lanes = pl.ds(group * HD, HD)
        total = parts_ref[0, :, lanes].astype(jnp.float32)
        for part in range(1, NZ):
            total += parts_ref[part, :, lanes].astype(jnp.float32)
        if inverse is None:
            squares = total[ROWS : ROWS + 1, :] + total[ROWS + 1 : ROWS + 2, :]
            inverse = lax.rsqrt(squares * (1.0 / D) + 1e-05)
            inverse = jnp.broadcast_to(inverse, (HD, HD)).T[:ROWS]
        total = total[:ROWS] * inverse
        cos = cos_ref[...] if group < QS else fcos_ref[...]
        sin = sin_ref[...] if group < QS else fsin_ref[...]
        turned = total * cos + pltpu.roll(total, HD // 2, 1) * sin
        out_ref[pl.ds(group * ROWS, ROWS), :] = turned.astype(jnp.bfloat16)


def pick_kernel(rows_ref, store_ref, *refs):
    outs, sem = refs[:NX], refs[NX]
    copies = []
    for k in (2, 1, 3, 0):
        for i in range(NZ):
            row = rows_ref[((NX - k) % NX) * NZ + i]
            copies.append(
                pltpu.make_async_copy(store_ref.at[row], outs[k].at[i], sem.at[k * NZ + i])
            )
            copies[-1].start()
    for copy in copies:
        copy.wait()


def attend_block(kv_ref, slots, queries, eff_ref, pos, run_ref, acc_ref):
    pieces = []
    for at, slot in slots:
        piece = lax.dot_general(
            kv_ref[at, :, :HD], queries, NT, preferred_element_type=jnp.float32
        )
        pieces.append(jnp.where(eff_ref[:, slot : slot + 1] <= pos, piece, neg_large))
    old_peak = run_ref[0:1, :]
    new_peak = old_peak
    for piece in pieces:
        new_peak = jnp.maximum(new_peak, jnp.max(piece, axis=0, keepdims=True))
    factor = jnp.exp2(old_peak - new_peak)
    total = run_ref[1:2, :] * factor
    acc = acc_ref[...] * factor
    for (at, _), piece in zip(slots, pieces):
        weights = jnp.exp2(piece - new_peak)
        total += jnp.sum(weights, axis=0, keepdims=True)
        acc += lax.dot_general(
            kv_ref[at, :, HD:], weights.astype(jnp.bfloat16), TN, preferred_element_type=jnp.float32
        )
    run_ref[0:1, :] = new_peak
    run_ref[1:2, :] = total
    acc_ref[...] = acc


def attend_slots(k, kv_ref, queries, eff_ref, pos, run_ref, acc_ref):
    for half in range(0, NZ, 4):
        slots = [(half + i, k * NZ + half + i) for i in range(4)]
        attend_block(kv_ref, slots, queries, eff_ref, pos, run_ref, acc_ref)


def attend_fresh(queries, flag_ref, own_ref, other_ref, fresh_eff_ref, pos, run_ref, acc_ref):
    own_piece = own_ref[QROWS:, :]
    other_piece = other_ref[QROWS:, :]
    first = jnp.broadcast_to(flag_ref[0] == 0, own_piece.shape)
    fresh_keys = jnp.where(first, own_piece, other_piece)
    fresh_values = jnp.where(first, other_piece, own_piece)
    scores = lax.dot_general(fresh_keys, queries, NT, preferred_element_type=jnp.float32)
    scores = jnp.where(fresh_eff_ref[:, 0:1] <= pos, scores, neg_large)
    peak = jnp.max(scores, axis=0, keepdims=True)
    weights = jnp.exp2(scores - peak)
    run_ref[...] = jnp.zeros(run_ref.shape, jnp.float32)
    run_ref[0:1, :] = peak
    run_ref[1:2, :] = jnp.sum(weights, axis=0, keepdims=True)
    acc_ref[...] = lax.dot_general(
        fresh_values, weights.astype(jnp.bfloat16), TN, preferred_element_type=jnp.float32
    )


def other_near_kernel(
    flag_ref,
    own_ref,
    other_ref,
    eff_ref,
    fresh_eff_ref,
    pos_ref,
    kv0_ref,
    kv1_ref,
    kv3_ref,
    acc_ref,
    run_ref,
):
    queries = other_ref[:QROWS, :]
    pos = pos_ref[...]
    attend_fresh(queries, flag_ref, own_ref, other_ref, fresh_eff_ref, pos, run_ref, acc_ref)
    for k, kv_ref in ((0, kv0_ref), (1, kv1_ref), (3, kv3_ref)):
        attend_slots(k, kv_ref, queries, eff_ref, pos, run_ref, acc_ref)


def other_far_kernel(
    other_ref, eff_ref, pos_ref, acc_in_ref, run_in_ref, kv2_ref, sent_ref, acc_ref, run_ref
):
    acc_ref[...] = acc_in_ref[...]
    run_ref[...] = run_in_ref[...]
    attend_slots(2, kv2_ref, other_ref[:QROWS, :], eff_ref, pos_ref[...], run_ref, acc_ref)
    peak = run_ref[0:1, :]
    total = run_ref[1:2, :]
    peak_high = peak.astype(jnp.bfloat16).astype(jnp.float32)
    total_high = total.astype(jnp.bfloat16).astype(jnp.float32)
    stats = jnp.concatenate(
        [
            peak_high,
            peak - peak_high,
            total_high,
            total - total_high,
            jnp.zeros((12, QROWS), jnp.float32),
        ],
        axis=0,
    )
    sent_ref[:HD, :] = (acc_ref[...] / total).astype(jnp.bfloat16)
    sent_ref[HD:, :] = stats.astype(jnp.bfloat16)


def own_kernel(
    flag_ref,
    own_ref,
    other_ref,
    eff_ref,
    fresh_eff_ref,
    pos_ref,
    kv0_ref,
    kv1_ref,
    kv2_ref,
    kv3_ref,
    acc_ref,
    run_ref,
):
    queries = own_ref[:QROWS, :]
    pos = pos_ref[...]
    attend_fresh(queries, flag_ref, own_ref, other_ref, fresh_eff_ref, pos, run_ref, acc_ref)
    for k, kv_ref in ((0, kv0_ref), (1, kv1_ref), (2, kv2_ref), (3, kv3_ref)):
        attend_slots(k, kv_ref, queries, eff_ref, pos, run_ref, acc_ref)


def merge_kernel(acc_ref, run_ref, got_ref, out_ref):
    stats = got_ref[HD:, :].astype(jnp.float32)
    got_peak = stats[0:1, :] + stats[1:2, :]
    got_total = stats[2:3, :] + stats[3:4, :]
    peak = run_ref[0:1, :]
    total = run_ref[1:2, :]
    joint = jnp.maximum(peak, got_peak)
    mine = jnp.exp2(peak - joint)
    theirs = jnp.exp2(got_peak - joint) * got_total
    whole = mine * total + theirs
    mixed = acc_ref[...] * (mine / whole) + got_ref[:HD, :].astype(jnp.float32) * (theirs / whole)
    turned = mixed.T.astype(jnp.bfloat16)
    for head in range(QS):
        out_ref[:, pl.ds(head * HD, HD)] = turned[head * ROWS : (head + 1) * ROWS, :]


def body(hidden, norm_gain, q_weight, kv_weight, cache_store, location, stretch_ids, rec_pos):
    x = lax.axis_index("x")
    z = lax.axis_index("z")
    y = lax.axis_index("y")
    c = lax.axis_index("c")
    my_tp = y * NC + c
    which_half = my_tp // KVH
    is_first = which_half == 0
    positions = rec_pos[0]
    own_list = stretch_ids[0]
    int_rows = jnp.arange(CH_DEV, dtype=jnp.int32)
    table = jnp.arange(location.shape[0], dtype=jnp.int32)

    store = lax.all_gather(cache_store[:, 0], "z", axis=0, tiled=True)

    listed = jnp.pad(own_list.astype(jnp.bfloat16)[None, :], ((0, 15), (0, COLS - MAXC)))
    weight = jnp.concatenate([q_weight[:, 0], kv_weight[:, 0]], axis=1)
    weight = jnp.concatenate([weight, listed], axis=0)

    far_weight = shifted(weight, "x", NX, -2)
    blocks = hidden[0].reshape(NY, 8, 2, NC, HD).transpose(2, 0, 3, 1, 4)
    blocks = jnp.broadcast_to(blocks[None], (4, 2, NY, NC, 8, HD))
    blocks = lax.all_to_all(
        blocks.reshape(NZ * NY * NC, 8, HD), ("z", "y", "c"), 0, 0, tiled=True
    )
    blocks, weight, far_weight = lax.optimization_barrier((blocks, weight, far_weight))
    weights = [weight, shifted(weight, "x", NX, -1), far_weight, shifted(weight, "x", NX, -3)]
    blocks = blocks.reshape(NZ, NX, 4, 8, HD)
    blocks = lax.dynamic_index_in_dim(blocks, z // 2, 2, keepdims=False)
    blocks = jnp.concatenate([blocks, blocks], axis=1)
    blocks = lax.dynamic_slice_in_dim(blocks, x, NX, 1)
    blocks = blocks.transpose(0, 2, 1, 3).reshape(NZ, 8, NX * HD)
    tokens = lax.all_to_all(
        jnp.broadcast_to(blocks[None], (NY, NZ, 8, NX * HD)), "y", 0, 0, tiled=True
    )
    tokens, *weights = lax.optimization_barrier((tokens, *weights))
    mate_tokens = swap_cores(tokens)
    gain = lax.dynamic_index_in_dim(norm_gain.reshape(NX, NZ, NC * HD), z, 1, keepdims=False)
    gain = lax.dynamic_slice_in_dim(jnp.concatenate([gain, gain], axis=0), x, NX, 0)
    gain = gain.astype(jnp.float32).reshape(1, NX * NC * HD)

    smem = pl.BlockSpec(memory_space=pltpu.SMEM)
    vmem = pl.BlockSpec(memory_space=pltpu.VMEM)
    hbm = pl.BlockSpec(memory_space=pltpu.MemorySpace.HBM)
    partial = pl.pallas_call(
        project_kernel,
        out_shape=jax.ShapeDtypeStruct((NZ, ROWS + 8, COLS), jnp.bfloat16),
        in_specs=[smem] + [vmem] * 7,
        out_specs=vmem,
        name="project",
        compiler_params=pltpu.CompilerParams(vmem_limit_bytes=32 * 1024 * 1024),
        cost_estimate=pl.CostEstimate(
            flops=2 * NZ * ROWS * 1024 * COLS, bytes_accessed=1 << 22, transcendentals=0
        ),
    )(c.reshape(1), tokens, mate_tokens, gain, *weights)
    parts = lax.all_to_all(partial, "z", 0, 0, tiled=True)

    lists = jnp.stack([w[NC * HD, :MAXC] for w in weights]).astype(jnp.int32)
    steps = jnp.arange(NZ, dtype=jnp.int32)
    row_ids = (x * NZ + steps)[:, None] * CH_DEV + int_rows[None, :]
    here = location[None, None, :] == row_ids[:, :, None]
    held = jnp.sum(jnp.where(here, table, 0), axis=2)
    wanted = jnp.any(lists[:, :, None, None] == held[None, None], axis=1)
    send_rows = jnp.sum(jnp.where(wanted, int_rows, 0), axis=2) + steps[None, :] * CH_DEV
    send_rows, _ = lax.optimization_barrier((send_rows, partial[0, ROWS:, :HD]))
    picked = pl.pallas_call(
        pick_kernel,
        out_shape=[jax.ShapeDtypeStruct((NZ, HALF, 2 * HD), jnp.bfloat16)] * NX,
        in_specs=[smem, hbm],
        out_specs=[vmem] * NX,
        scratch_shapes=[pltpu.SemaphoreType.DMA((NX * NZ,))],
        name="pick",
        compiler_params=pltpu.CompilerParams(vmem_limit_bytes=60 * 1024 * 1024),
        cost_estimate=pl.CostEstimate(flops=0, bytes_accessed=1 << 22, transcendentals=0),
    )(send_rows.reshape(-1), store)
    arrived = [picked[0]] + [shifted(picked[k], "x", NX, -k) for k in range(1, NX)]

    frequency = jnp.exp(
        -math.log(theta_base) * jnp.arange(HD // 2, dtype=jnp.float32) / (HD // 2)
    )
    angles = positions.astype(jnp.float32)[:, None] * frequency[None, :]
    cos = jnp.cos(angles)
    sin = jnp.sin(angles)
    cos = jnp.concatenate([cos, cos], axis=1)
    sin = jnp.concatenate([-sin, sin], axis=1)
    fresh_cos = jnp.where(is_first, cos, 1.0)
    fresh_sin = jnp.where(is_first, sin, 0.0)
    scale = math.log2(math.e) / math.sqrt(HD)

    own = call(
        finish_kernel, jax.ShapeDtypeStruct((QROWS + ROWS, HD), jnp.bfloat16), "finish"
    )(parts, cos * scale, sin * scale, fresh_cos, fresh_sin)
    other = exchange(own)

    own_row = jnp.sum(jnp.where(own_list[:, None] == table[None, :], location[None, :], 0), axis=1)
    own_shard = own_row // CH_DEV
    slot_shard = (x * NZ + jnp.arange(MAXC, dtype=jnp.int32)) % (NX * NZ)
    match = (own_shard[None, :] == slot_shard[:, None]) & (own_list >= 0)[None, :]
    slot_order = jnp.sum(jnp.where(match, jnp.arange(MAXC, dtype=jnp.int32), 0), axis=1)
    slot_live = jnp.any(match, axis=1)
    key_pos = (
        slot_order[None, :] * STRETCH
        + which_half * HALF
        + jnp.arange(HALF, dtype=jnp.int32)[:, None]
    )
    replaced = jnp.any(key_pos[:, :, None] == positions[None, None, :], axis=2)
    eff = jnp.where(replaced | ~slot_live[None, :], far_away, key_pos)
    fresh_eff = jnp.where(positions % STRETCH // HALF == which_half, positions, far_away)
    fresh_eff = jnp.broadcast_to(fresh_eff[:, None], (ROWS, HD))
    pos_row = jnp.tile(positions, QS).reshape(1, QROWS)

    params = pltpu.CompilerParams(vmem_limit_bytes=32 * 1024 * 1024)
    run_shapes = [
        jax.ShapeDtypeStruct((HD, QROWS), jnp.float32),
        jax.ShapeDtypeStruct((8, QROWS), jnp.float32),
    ]

    def cost(count):
        pairs = count * NZ * HALF * QROWS
        return pl.CostEstimate(flops=4 * pairs * HD, bytes_accessed=count << 19, transcendentals=pairs)

    common = (which_half.reshape(1), own, other, eff, fresh_eff, pos_row)
    acc, run = pl.pallas_call(
        other_near_kernel,
        out_shape=run_shapes,
        in_specs=[smem] + [vmem] * 8,
        out_specs=[vmem] * 2,
        name="other_near",
        compiler_params=params,
        cost_estimate=cost(3),
    )(*common, arrived[0], arrived[1], arrived[3])
    sent = pl.pallas_call(
        other_far_kernel,
        out_shape=jax.ShapeDtypeStruct((HD + 16, QROWS), jnp.bfloat16),
        in_specs=[vmem] * 6,
        out_specs=vmem,
        scratch_shapes=[pltpu.VMEM(r.shape, r.dtype) for r in run_shapes],
        name="other_far",
        compiler_params=params,
        cost_estimate=cost(1),
    )(other, eff, pos_row, acc, run, arrived[2])
    got = exchange(sent)
    queries, allowed, sent = lax.optimization_barrier((own, eff, sent))
    own_acc, own_run = pl.pallas_call(
        own_kernel,
        out_shape=run_shapes,
        in_specs=[smem] + [vmem] * 9,
        out_specs=[vmem] * 2,
        name="own",
        compiler_params=params,
        cost_estimate=cost(4),
    )(which_half.reshape(1), queries, other, allowed, fresh_eff, pos_row, *arrived)
    attended = call(merge_kernel, jax.ShapeDtypeStruct((ROWS, QW), jnp.bfloat16), "merge")(
        own_acc, own_run, got
    )
    return attended.reshape(1, ROWS, 1, QW)


def solution(mesh):
    fine = Mesh(mesh.devices.reshape(NX, NZ, NY, NC), ("x", "z", "y", "c"))
    in_specs = (
        P(STORE, None, TP),
        P(),
        P(STORE, TP, None),
        P(STORE, TP, None),
        P(STORE, TP, None, None),
        P(),
        P(STORE, None),
        P(STORE, None),
    )
    return jax.shard_map(
        body, mesh=fine, in_specs=in_specs, out_specs=P(STORE, None, TP, None), check_vma=False
    )
```

```python
import functools
import math

import jax
import jax.numpy as jnp
from jax import lax
from jax.experimental import pallas as pl
from jax.experimental.pallas import tpu as pltpu
from jax.sharding import Mesh
from jax.sharding import PartitionSpec as P

NX, NZ, NY, NC = 4, 8, 8, 2
KVH = 8
HD = 128
STRETCH = 256
MAXC = 32
CH_DEV = 8
QS = 4
HALF = 128
ROWS = 64
D = 8192
QW = QS * HD
COLS = QW + HD
QROWS = QS * ROWS

theta_base = 500000.0
neg_large = -1e30
far_away = 1 << 29

STORE = ("x", "z")
TP = ("y", "c")
NT = (((1,), (1,)), ((), ()))
TN = (((0,), (0,)), ((), ()))


def exchange(block):
    return lax.ppermute(block, "y", [(i, (i + NY // 2) % NY) for i in range(NY)])


def swap_cores(block):
    return lax.ppermute(block, "c", [(0, 1), (1, 0)])


def shifted(block, axis, count, by):
    return lax.ppermute(block, axis, [(i, (i + by) % count) for i in range(count)])


def call(kernel, outs, name, flops=0, bytes_accessed=0):
    return pl.pallas_call(
        kernel,
        out_shape=outs,
        name=name,
        compiler_params=pltpu.CompilerParams(vmem_limit_bytes=32 * 1024 * 1024),
        cost_estimate=pl.CostEstimate(
            flops=flops, bytes_accessed=bytes_accessed, transcendentals=0
        ),
    )


def project_kernel(
    core_ref,
    mine_ref,
    mate_ref,
    gain_ref,
    held_ref,
    w0_ref,
    w1_ref,
    w2_ref,
    w3_ref,
    out_ref,
    rows_ref,
):
    lane = lax.broadcasted_iota(jnp.int32, (NZ * CH_DEV, HD), 1)
    line = lax.broadcasted_iota(jnp.int32, (NZ * CH_DEV, HD), 0)
    for k, w_ref in enumerate((w0_ref, w1_ref, w2_ref, w3_ref)):
        listed = w_ref[2 * HD :, :HD].astype(jnp.float32)[0:1, :]
        hit = (held_ref[...] == listed) & (lane < MAXC)
        found = jnp.where(hit, (line % CH_DEV).astype(jnp.float32), 0.0)
        found = jnp.sum(found.reshape(NZ, CH_DEV, HD), axis=1)
        found = jnp.sum(found, axis=1, keepdims=True).astype(jnp.int32)
        base = lax.broadcasted_iota(jnp.int32, (NZ, HD), 0) * CH_DEV
        rows_ref[k] = base + found

    weights = jnp.concatenate([w[: 2 * HD, :] for w in (w0_ref, w1_ref, w2_ref, w3_ref)], axis=0)
    gain = gain_ref[...]
    is_zero = core_ref[0] == 0
    rows = []
    stats = []
    for request in range(NZ):
        tall = []
        for y in range(NY):
            mine = mine_ref[y, request].astype(jnp.float32)
            mate = mate_ref[y, request].astype(jnp.float32)
            zero = jnp.broadcast_to(is_zero, mine.shape)
            halves = [jnp.where(zero, mine, mate), jnp.where(zero, mate, mine)]
            tall.append(
                jnp.concatenate(
                    [halves[c][:, k * HD : (k + 1) * HD] for k in range(NX) for c in range(NC)],
                    axis=1,
                )
            )
        wide = jnp.concatenate(tall, axis=0)
        rows.append((wide * gain).astype(jnp.bfloat16))
        squares = jnp.zeros((ROWS, HD), jnp.float32)
        for at in range(0, wide.shape[1], HD):
            piece = wide[:, at : at + HD]
            squares += piece * piece
        squares = jnp.concatenate([squares, jnp.zeros_like(squares)], axis=0)
        row = jnp.sum(squares.T, axis=0, keepdims=True)
        high = row.astype(jnp.bfloat16).astype(jnp.float32)
        stat = jnp.concatenate([high, row - high, jnp.zeros((6, HD), jnp.float32)], axis=0)
        stats.append(jnp.concatenate([stat, jnp.zeros((8, QW), jnp.float32)], axis=1))
    total = jnp.dot(jnp.concatenate(rows, axis=0), weights, preferred_element_type=jnp.float32)
    for request in range(NZ):
        block = total[request * ROWS : (request + 1) * ROWS]
        block = jnp.concatenate([block, stats[request]], axis=0)
        out_ref[request] = block.astype(jnp.bfloat16)


def finish_kernel(parts_ref, cos_ref, sin_ref, fcos_ref, fsin_ref, out_ref):
    inverse = None
    for group in range(QS + 1):
        lanes = pl.ds(group * HD, HD)
        total = parts_ref[0, :, lanes].astype(jnp.float32)
        for part in range(1, NZ):
            total += parts_ref[part, :, lanes].astype(jnp.float32)
        if inverse is None:
            squares = total[ROWS : ROWS + 1, :] + total[ROWS + 1 : ROWS + 2, :]
            inverse = lax.rsqrt(squares * (1.0 / D) + 1e-05)
            inverse = jnp.broadcast_to(inverse, (HD, HD)).T[:ROWS]
        total = total[:ROWS] * inverse
        cos = cos_ref[...] if group < QS else fcos_ref[...]
        sin = sin_ref[...] if group < QS else fsin_ref[...]
        turned = total * cos + pltpu.roll(total, HD // 2, 1) * sin
        out_ref[pl.ds(group * ROWS, ROWS), :] = turned.astype(jnp.bfloat16)


def pick_kernel(which, rows_ref, store_ref, *refs):
    outs, (table_ref, sem, table_sem) = refs[: len(which)], refs[len(which) :]
    table = pltpu.make_async_copy(rows_ref, table_ref, table_sem)
    table.start()
    table.wait()
    copies = []
    for at, k in enumerate(which):
        for i in range(NZ):
            row = table_ref[(NX - k) % NX, i, 0]
            copies.append(
                pltpu.make_async_copy(store_ref.at[row], outs[at].at[i], sem.at[at * NZ + i])
            )
            copies[-1].start()
    for copy in copies:
        copy.wait()


def attend_block(kv_ref, slots, queries, eff_ref, pos, run_ref, acc_ref):
    pieces = []
    for at, slot in slots:
        piece = lax.dot_general(
            kv_ref[at, :, :HD], queries, NT, preferred_element_type=jnp.float32
        )
        pieces.append(jnp.where(eff_ref[:, slot : slot + 1] <= pos, piece, neg_large))
    old_peak = run_ref[0:1, :]
    new_peak = old_peak
    for piece in pieces:
        new_peak = jnp.maximum(new_peak, jnp.max(piece, axis=0, keepdims=True))
    factor = jnp.exp2(old_peak - new_peak)
    total = run_ref[1:2, :] * factor
    acc = acc_ref[...] * factor
    for (at, _), piece in zip(slots, pieces):
        weights = jnp.exp2(piece - new_peak)
        total += jnp.sum(weights, axis=0, keepdims=True)
        acc += lax.dot_general(
            kv_ref[at, :, HD:], weights.astype(jnp.bfloat16), TN, preferred_element_type=jnp.float32
        )
    run_ref[0:1, :] = new_peak
    run_ref[1:2, :] = total
    acc_ref[...] = acc


def attend_slots(k, kv_ref, queries, eff_ref, pos, run_ref, acc_ref):
    for half in range(0, NZ, 4):
        slots = [(half + i, k * NZ + half + i) for i in range(4)]
        attend_block(kv_ref, slots, queries, eff_ref, pos, run_ref, acc_ref)


def attend_fresh(queries, flag_ref, own_ref, other_ref, fresh_eff_ref, pos, run_ref, acc_ref):
    own_piece = own_ref[QROWS:, :]
    other_piece = other_ref[QROWS:, :]
    first = jnp.broadcast_to(flag_ref[0] == 0, own_piece.shape)
    fresh_keys = jnp.where(first, own_piece, other_piece)
    fresh_values = jnp.where(first, other_piece, own_piece)
    scores = lax.dot_general(fresh_keys, queries, NT, preferred_element_type=jnp.float32)
    scores = jnp.where(fresh_eff_ref[:, 0:1] <= pos, scores, neg_large)
    peak = jnp.max(scores, axis=0, keepdims=True)
    weights = jnp.exp2(scores - peak)
    run_ref[...] = jnp.zeros(run_ref.shape, jnp.float32)
    run_ref[0:1, :] = peak
    run_ref[1:2, :] = jnp.sum(weights, axis=0, keepdims=True)
    acc_ref[...] = lax.dot_general(
        fresh_values, weights.astype(jnp.bfloat16), TN, preferred_element_type=jnp.float32
    )


def other_near_kernel(
    flag_ref,
    own_ref,
    other_ref,
    eff_ref,
    fresh_eff_ref,
    pos_ref,
    kv0_ref,
    kv1_ref,
    kv3_ref,
    acc_ref,
    run_ref,
):
    queries = other_ref[:QROWS, :]
    pos = pos_ref[...]
    attend_fresh(queries, flag_ref, own_ref, other_ref, fresh_eff_ref, pos, run_ref, acc_ref)
    for k, kv_ref in ((0, kv0_ref), (1, kv1_ref), (3, kv3_ref)):
        attend_slots(k, kv_ref, queries, eff_ref, pos, run_ref, acc_ref)


def other_far_kernel(
    other_ref, eff_ref, pos_ref, acc_in_ref, run_in_ref, kv2_ref, sent_ref, acc_ref, run_ref
):
    acc_ref[...] = acc_in_ref[...]
    run_ref[...] = run_in_ref[...]
    attend_slots(2, kv2_ref, other_ref[:QROWS, :], eff_ref, pos_ref[...], run_ref, acc_ref)
    peak = run_ref[0:1, :]
    total = run_ref[1:2, :]
    peak_high = peak.astype(jnp.bfloat16).astype(jnp.float32)
    total_high = total.astype(jnp.bfloat16).astype(jnp.float32)
    stats = jnp.concatenate(
        [
            peak_high,
            peak - peak_high,
            total_high,
            total - total_high,
            jnp.zeros((12, QROWS), jnp.float32),
        ],
        axis=0,
    )
    sent_ref[:HD, :] = (acc_ref[...] / total).astype(jnp.bfloat16)
    sent_ref[HD:, :] = stats.astype(jnp.bfloat16)


def own_kernel(
    flag_ref,
    own_ref,
    other_ref,
    eff_ref,
    fresh_eff_ref,
    pos_ref,
    kv0_ref,
    kv1_ref,
    kv2_ref,
    kv3_ref,
    acc_ref,
    run_ref,
):
    queries = own_ref[:QROWS, :]
    pos = pos_ref[...]
    attend_fresh(queries, flag_ref, own_ref, other_ref, fresh_eff_ref, pos, run_ref, acc_ref)
    for k, kv_ref in ((0, kv0_ref), (1, kv1_ref), (2, kv2_ref), (3, kv3_ref)):
        attend_slots(k, kv_ref, queries, eff_ref, pos, run_ref, acc_ref)


def merge_kernel(acc_ref, run_ref, got_ref, out_ref):
    stats = got_ref[HD:, :].astype(jnp.float32)
    got_peak = stats[0:1, :] + stats[1:2, :]
    got_total = stats[2:3, :] + stats[3:4, :]
    peak = run_ref[0:1, :]
    total = run_ref[1:2, :]
    joint = jnp.maximum(peak, got_peak)
    mine = jnp.exp2(peak - joint)
    theirs = jnp.exp2(got_peak - joint) * got_total
    whole = mine * total + theirs
    mixed = acc_ref[...] * (mine / whole) + got_ref[:HD, :].astype(jnp.float32) * (theirs / whole)
    turned = mixed.T.astype(jnp.bfloat16)
    for head in range(QS):
        out_ref[:, pl.ds(head * HD, HD)] = turned[head * ROWS : (head + 1) * ROWS, :]


def body(hidden, norm_gain, q_weight, kv_weight, cache_store, location, stretch_ids, rec_pos):
    x = lax.axis_index("x")
    z = lax.axis_index("z")
    y = lax.axis_index("y")
    c = lax.axis_index("c")
    my_tp = y * NC + c
    which_half = my_tp // KVH
    is_first = which_half == 0
    positions = rec_pos[0]
    own_list = stretch_ids[0]
    int_rows = jnp.arange(CH_DEV, dtype=jnp.int32)
    table = jnp.arange(location.shape[0], dtype=jnp.int32)

    store = lax.all_gather(cache_store[:, 0], "z", axis=0, tiled=True)

    listed = jnp.pad(own_list.astype(jnp.bfloat16)[None, :], ((0, 15), (0, COLS - MAXC)))
    weight = jnp.concatenate([q_weight[:, 0], kv_weight[:, 0]], axis=1)
    weight = jnp.concatenate([weight, listed], axis=0)

    far_weight = shifted(weight, "x", NX, -2)
    blocks = hidden[0].reshape(NY, 8, 2, NC, HD).transpose(2, 0, 3, 1, 4)
    blocks = jnp.broadcast_to(blocks[None], (4, 2, NY, NC, 8, HD))
    blocks = lax.all_to_all(
        blocks.reshape(NZ * NY * NC, 8, HD), ("z", "y", "c"), 0, 0, tiled=True
    )
    blocks, weight, far_weight = lax.optimization_barrier((blocks, weight, far_weight))
    weights = [weight, shifted(weight, "x", NX, -1), far_weight, shifted(weight, "x", NX, -3)]
    blocks = blocks.reshape(NZ, NX, 4, 8, HD)
    blocks = lax.dynamic_index_in_dim(blocks, z // 2, 2, keepdims=False)
    blocks = jnp.concatenate([blocks, blocks], axis=1)
    blocks = lax.dynamic_slice_in_dim(blocks, x, NX, 1)
    blocks = blocks.transpose(0, 2, 1, 3).reshape(NZ, 8, NX * HD)
    tokens = lax.all_to_all(
        jnp.broadcast_to(blocks[None], (NY, NZ, 8, NX * HD)), "y", 0, 0, tiled=True
    )
    steps = jnp.arange(NZ, dtype=jnp.int32)
    row_ids = ((x * NZ + steps)[:, None] * CH_DEV + int_rows[None, :]).reshape(-1)
    here = location[None, :] == row_ids[:, None]
    held = jnp.sum(jnp.where(here, table, 0), axis=1).astype(jnp.float32)
    held = jnp.broadcast_to(held[:, None], (NZ * CH_DEV, HD))

    frequency = jnp.exp(
        -math.log(theta_base) * jnp.arange(HD // 2, dtype=jnp.float32) / (HD // 2)
    )
    angles = positions.astype(jnp.float32)[:, None] * frequency[None, :]
    cos = jnp.cos(angles)
    sin = jnp.sin(angles)
    cos = jnp.concatenate([cos, cos], axis=1)
    sin = jnp.concatenate([-sin, sin], axis=1)
    fresh_cos = jnp.where(is_first, cos, 1.0)
    fresh_sin = jnp.where(is_first, sin, 0.0)
    scale = math.log2(math.e) / math.sqrt(HD)

    own_row = jnp.sum(jnp.where(own_list[:, None] == table[None, :], location[None, :], 0), axis=1)
    own_shard = own_row // CH_DEV
    slot_shard = (x * NZ + jnp.arange(MAXC, dtype=jnp.int32)) % (NX * NZ)
    match = (own_shard[None, :] == slot_shard[:, None]) & (own_list >= 0)[None, :]
    slot_order = jnp.sum(jnp.where(match, jnp.arange(MAXC, dtype=jnp.int32), 0), axis=1)
    slot_live = jnp.any(match, axis=1)
    key_pos = (
        slot_order[None, :] * STRETCH
        + which_half * HALF
        + jnp.arange(HALF, dtype=jnp.int32)[:, None]
    )
    replaced = jnp.any(key_pos[:, :, None] == positions[None, None, :], axis=2)
    eff = jnp.where(replaced | ~slot_live[None, :], far_away, key_pos)
    fresh_eff = jnp.where(positions % STRETCH // HALF == which_half, positions, far_away)
    fresh_eff = jnp.broadcast_to(fresh_eff[:, None], (ROWS, HD))
    pos_row = jnp.tile(positions, QS).reshape(1, QROWS)

    gain = lax.dynamic_index_in_dim(norm_gain.reshape(NX, NZ, NC * HD), z, 1, keepdims=False)
    gain = lax.dynamic_slice_in_dim(jnp.concatenate([gain, gain], axis=0), x, NX, 0)
    gain = gain.astype(jnp.float32).reshape(1, NX * NC * HD)

    turns = (cos * scale, sin * scale, fresh_cos, fresh_sin)
    tokens, weights, turns, eff, fresh_eff, pos_row, gain, held = lax.optimization_barrier(
        (tokens, weights, turns, eff, fresh_eff, pos_row, gain, held)
    )
    mate_tokens = swap_cores(tokens)

    smem = pl.BlockSpec(memory_space=pltpu.SMEM)
    vmem = pl.BlockSpec(memory_space=pltpu.VMEM)
    hbm = pl.BlockSpec(memory_space=pltpu.MemorySpace.HBM)
    partial, send_rows = pl.pallas_call(
        project_kernel,
        out_shape=[
            jax.ShapeDtypeStruct((NZ, ROWS + 8, COLS), jnp.bfloat16),
            jax.ShapeDtypeStruct((NX, NZ, HD), jnp.int32),
        ],
        in_specs=[smem] + [vmem] * 8,
        out_specs=[vmem] * 2,
        name="project",
        compiler_params=pltpu.CompilerParams(vmem_limit_bytes=32 * 1024 * 1024),
        cost_estimate=pl.CostEstimate(
            flops=2 * NZ * ROWS * 1024 * COLS, bytes_accessed=1 << 22, transcendentals=0
        ),
    )(c.reshape(1), tokens, mate_tokens, gain, held, *weights)
    parts = lax.all_to_all(partial, "z", 0, 0, tiled=True)

    def pick(which, rows):
        return pl.pallas_call(
            functools.partial(pick_kernel, which),
            out_shape=[jax.ShapeDtypeStruct((NZ, HALF, 2 * HD), jnp.bfloat16)] * len(which),
            in_specs=[vmem, hbm],
            out_specs=[vmem] * len(which),
            scratch_shapes=[
                pltpu.SMEM((NX, NZ, HD), jnp.int32),
                pltpu.SemaphoreType.DMA((len(which) * NZ,)),
                pltpu.SemaphoreType.DMA,
            ],
            name="pick",
            compiler_params=pltpu.CompilerParams(vmem_limit_bytes=50 * 1024 * 1024),
            cost_estimate=pl.CostEstimate(
                flops=0, bytes_accessed=len(which) << 20, transcendentals=0
            ),
        )(rows, store)

    picked = dict(zip((2, 1, 3), pick((2, 1, 3), send_rows)))
    arrived = {k: shifted(picked[k], "x", NX, -k) for k in (2, 1, 3)}
    own_rows, parts = lax.optimization_barrier((send_rows, parts))
    arrived[0] = pick((0,), own_rows)[0]

    own = call(
        finish_kernel, jax.ShapeDtypeStruct((QROWS + ROWS, HD), jnp.bfloat16), "finish"
    )(parts, *turns)
    other = exchange(own)

    params = pltpu.CompilerParams(vmem_limit_bytes=32 * 1024 * 1024)
    run_shapes = [
        jax.ShapeDtypeStruct((HD, QROWS), jnp.float32),
        jax.ShapeDtypeStruct((8, QROWS), jnp.float32),
    ]

    def cost(count):
        pairs = count * NZ * HALF * QROWS
        return pl.CostEstimate(flops=4 * pairs * HD, bytes_accessed=count << 19, transcendentals=pairs)

    common = (which_half.reshape(1), own, other, eff, fresh_eff, pos_row)
    acc, run = pl.pallas_call(
        other_near_kernel,
        out_shape=run_shapes,
        in_specs=[smem] + [vmem] * 8,
        out_specs=[vmem] * 2,
        name="other_near",
        compiler_params=params,
        cost_estimate=cost(3),
    )(*common, arrived[0], arrived[1], arrived[3])
    sent = pl.pallas_call(
        other_far_kernel,
        out_shape=jax.ShapeDtypeStruct((HD + 16, QROWS), jnp.bfloat16),
        in_specs=[vmem] * 6,
        out_specs=vmem,
        scratch_shapes=[pltpu.VMEM(r.shape, r.dtype) for r in run_shapes],
        name="other_far",
        compiler_params=params,
        cost_estimate=cost(1),
    )(other, eff, pos_row, acc, run, arrived[2])
    got = exchange(sent)
    queries, allowed, sent = lax.optimization_barrier((own, eff, sent))
    own_acc, own_run = pl.pallas_call(
        own_kernel,
        out_shape=run_shapes,
        in_specs=[smem] + [vmem] * 9,
        out_specs=[vmem] * 2,
        name="own",
        compiler_params=params,
        cost_estimate=cost(4),
    )(which_half.reshape(1), queries, other, allowed, fresh_eff, pos_row, *[arrived[k] for k in range(NX)])
    attended = call(merge_kernel, jax.ShapeDtypeStruct((ROWS, QW), jnp.bfloat16), "merge")(
        own_acc, own_run, got
    )
    return attended.reshape(1, ROWS, 1, QW)


def solution(mesh):
    fine = Mesh(mesh.devices.reshape(NX, NZ, NY, NC), ("x", "z", "y", "c"))
    in_specs = (
        P(STORE, None, TP),
        P(),
        P(STORE, TP, None),
        P(STORE, TP, None),
        P(STORE, TP, None, None),
        P(),
        P(STORE, None),
        P(STORE, None),
    )
    return jax.shard_map(
        body, mesh=fine, in_specs=in_specs, out_specs=P(STORE, None, TP, None), check_vma=False
    )
```

```python
import functools
import math

import jax
import jax.numpy as jnp
from jax import lax
from jax.experimental import pallas as pl
from jax.experimental.pallas import tpu as pltpu
from jax.sharding import Mesh
from jax.sharding import PartitionSpec as P

NX, NZ, NY, NC = 4, 8, 8, 2
KVH = 8
HD = 128
STRETCH = 256
MAXC = 32
CH_DEV = 8
QS = 4
HALF = 128
ROWS = 64
D = 8192
QW = QS * HD
COLS = QW + HD
QROWS = QS * ROWS

theta_base = 500000.0
neg_large = -1e30
far_away = 1 << 29

STORE = ("x", "z")
TP = ("y", "c")
NT = (((1,), (1,)), ((), ()))
TN = (((0,), (0,)), ((), ()))


def exchange(block):
    return lax.ppermute(block, "y", [(i, (i + NY // 2) % NY) for i in range(NY)])


def swap_cores(block):
    return lax.ppermute(block, "c", [(0, 1), (1, 0)])


def shifted(block, axis, count, by):
    return lax.ppermute(block, axis, [(i, (i + by) % count) for i in range(count)])


def call(kernel, outs, name, flops=0, bytes_accessed=0):
    return pl.pallas_call(
        kernel,
        out_shape=outs,
        name=name,
        compiler_params=pltpu.CompilerParams(vmem_limit_bytes=32 * 1024 * 1024),
        cost_estimate=pl.CostEstimate(
            flops=flops, bytes_accessed=bytes_accessed, transcendentals=0
        ),
    )


def spread_kernel(hidden_ref, out_ref):
    states = hidden_ref[...].astype(jnp.float32)
    for b in range(2):
        for y in range(NY):
            for c in range(NC):
                lanes = (b * NC + c) * HD
                block = states[y * 8 : (y + 1) * 8, lanes : lanes + HD].astype(jnp.bfloat16)
                for pair in range(4):
                    out_ref[((pair * 2 + b) * NY + y) * NC + c] = block


def gather_kernel(place_ref, blocks_ref, out_ref):
    x = place_ref[0]
    pair = place_ref[1]
    for request in range(NZ):
        block = jnp.concatenate(
            [blocks_ref[request, lax.rem(x + i, NX), pair] for i in range(NX)], axis=1
        )
        for y in range(NY):
            out_ref[y, request] = block


def project_kernel(
    core_ref,
    mine_ref,
    mate_ref,
    gain_ref,
    held_ref,
    w0_ref,
    w1_ref,
    w2_ref,
    w3_ref,
    out_ref,
    rows_ref,
):
    lane = lax.broadcasted_iota(jnp.int32, (NZ * CH_DEV, HD), 1)
    line = lax.broadcasted_iota(jnp.int32, (NZ * CH_DEV, HD), 0)
    for k, w_ref in enumerate((w0_ref, w1_ref, w2_ref, w3_ref)):
        listed = w_ref[2 * HD :, :HD].astype(jnp.float32)[0:1, :]
        hit = (held_ref[...] == listed) & (lane < MAXC)
        found = jnp.where(hit, (line % CH_DEV).astype(jnp.float32), 0.0)
        found = jnp.sum(found.reshape(NZ, CH_DEV, HD), axis=1)
        found = jnp.sum(found, axis=1, keepdims=True).astype(jnp.int32)
        base = lax.broadcasted_iota(jnp.int32, (NZ, HD), 0) * CH_DEV
        rows_ref[k] = base + found

    weights = jnp.concatenate([w[: 2 * HD, :] for w in (w0_ref, w1_ref, w2_ref, w3_ref)], axis=0)
    gain = gain_ref[...]
    is_zero = core_ref[0] == 0
    rows = []
    stats = []
    for request in range(NZ):
        tall = []
        for y in range(NY):
            mine = mine_ref[y, request].astype(jnp.float32)
            mate = mate_ref[y, request].astype(jnp.float32)
            zero = jnp.broadcast_to(is_zero, mine.shape)
            halves = [jnp.where(zero, mine, mate), jnp.where(zero, mate, mine)]
            tall.append(
                jnp.concatenate(
                    [halves[c][:, k * HD : (k + 1) * HD] for k in range(NX) for c in range(NC)],
                    axis=1,
                )
            )
        wide = jnp.concatenate(tall, axis=0)
        rows.append((wide * gain).astype(jnp.bfloat16))
        squares = jnp.zeros((ROWS, HD), jnp.float32)
        for at in range(0, wide.shape[1], HD):
            piece = wide[:, at : at + HD]
            squares += piece * piece
        squares = jnp.concatenate([squares, jnp.zeros_like(squares)], axis=0)
        row = jnp.sum(squares.T, axis=0, keepdims=True)
        high = row.astype(jnp.bfloat16).astype(jnp.float32)
        stat = jnp.concatenate([high, row - high, jnp.zeros((6, HD), jnp.float32)], axis=0)
        stats.append(jnp.concatenate([stat, jnp.zeros((8, QW), jnp.float32)], axis=1))
    total = jnp.dot(jnp.concatenate(rows, axis=0), weights, preferred_element_type=jnp.float32)
    for request in range(NZ):
        block = total[request * ROWS : (request + 1) * ROWS]
        block = jnp.concatenate([block, stats[request]], axis=0)
        out_ref[request] = block.astype(jnp.bfloat16)


def finish_kernel(parts_ref, cos_ref, sin_ref, fcos_ref, fsin_ref, out_ref):
    inverse = None
    for group in range(QS + 1):
        lanes = pl.ds(group * HD, HD)
        total = parts_ref[0, :, lanes].astype(jnp.float32)
        for part in range(1, NZ):
            total += parts_ref[part, :, lanes].astype(jnp.float32)
        if inverse is None:
            squares = total[ROWS : ROWS + 1, :] + total[ROWS + 1 : ROWS + 2, :]
            inverse = lax.rsqrt(squares * (1.0 / D) + 1e-05)
            inverse = jnp.broadcast_to(inverse, (HD, HD)).T[:ROWS]
        total = total[:ROWS] * inverse
        cos = cos_ref[...] if group < QS else fcos_ref[...]
        sin = sin_ref[...] if group < QS else fsin_ref[...]
        turned = total * cos + pltpu.roll(total, HD // 2, 1) * sin
        out_ref[pl.ds(group * ROWS, ROWS), :] = turned.astype(jnp.bfloat16)


def pick_kernel(which, rows_ref, store_ref, *refs):
    outs, (table_ref, sem, table_sem) = refs[: len(which)], refs[len(which) :]
    table = pltpu.make_async_copy(rows_ref, table_ref, table_sem)
    table.start()
    table.wait()
    copies = []
    for at, k in enumerate(which):
        for i in range(NZ):
            row = table_ref[(NX - k) % NX, i, 0]
            copies.append(
                pltpu.make_async_copy(store_ref.at[row], outs[at].at[i], sem.at[at * NZ + i])
            )
            copies[-1].start()
    for copy in copies:
        copy.wait()


def attend_block(kv_ref, slots, queries, eff_ref, pos, run_ref, acc_ref):
    pieces = []
    for at, slot in slots:
        piece = lax.dot_general(
            kv_ref[at, :, :HD], queries, NT, preferred_element_type=jnp.float32
        )
        pieces.append(jnp.where(eff_ref[:, slot : slot + 1] <= pos, piece, neg_large))
    old_peak = run_ref[0:1, :]
    new_peak = old_peak
    for piece in pieces:
        new_peak = jnp.maximum(new_peak, jnp.max(piece, axis=0, keepdims=True))
    factor = jnp.exp2(old_peak - new_peak)
    total = run_ref[1:2, :] * factor
    acc = acc_ref[...] * factor
    for (at, _), piece in zip(slots, pieces):
        weights = jnp.exp2(piece - new_peak)
        total += jnp.sum(weights, axis=0, keepdims=True)
        acc += lax.dot_general(
            kv_ref[at, :, HD:], weights.astype(jnp.bfloat16), TN, preferred_element_type=jnp.float32
        )
    run_ref[0:1, :] = new_peak
    run_ref[1:2, :] = total
    acc_ref[...] = acc


def attend_slots(k, kv_ref, queries, eff_ref, pos, run_ref, acc_ref):
    for half in range(0, NZ, 4):
        slots = [(half + i, k * NZ + half + i) for i in range(4)]
        attend_block(kv_ref, slots, queries, eff_ref, pos, run_ref, acc_ref)


def attend_fresh(queries, flag_ref, own_ref, other_ref, fresh_eff_ref, pos, run_ref, acc_ref):
    own_piece = own_ref[QROWS:, :]
    other_piece = other_ref[QROWS:, :]
    first = jnp.broadcast_to(flag_ref[0] == 0, own_piece.shape)
    fresh_keys = jnp.where(first, own_piece, other_piece)
    fresh_values = jnp.where(first, other_piece, own_piece)
    scores = lax.dot_general(fresh_keys, queries, NT, preferred_element_type=jnp.float32)
    scores = jnp.where(fresh_eff_ref[:, 0:1] <= pos, scores, neg_large)
    peak = jnp.max(scores, axis=0, keepdims=True)
    weights = jnp.exp2(scores - peak)
    run_ref[...] = jnp.zeros(run_ref.shape, jnp.float32)
    run_ref[0:1, :] = peak
    run_ref[1:2, :] = jnp.sum(weights, axis=0, keepdims=True)
    acc_ref[...] = lax.dot_general(
        fresh_values, weights.astype(jnp.bfloat16), TN, preferred_element_type=jnp.float32
    )


def other_near_kernel(
    flag_ref,
    own_ref,
    other_ref,
    eff_ref,
    fresh_eff_ref,
    pos_ref,
    kv0_ref,
    kv1_ref,
    kv3_ref,
    acc_ref,
    run_ref,
):
    queries = other_ref[:QROWS, :]
    pos = pos_ref[...]
    attend_fresh(queries, flag_ref, own_ref, other_ref, fresh_eff_ref, pos, run_ref, acc_ref)
    for k, kv_ref in ((0, kv0_ref), (1, kv1_ref), (3, kv3_ref)):
        attend_slots(k, kv_ref, queries, eff_ref, pos, run_ref, acc_ref)


def other_far_kernel(
    other_ref, eff_ref, pos_ref, acc_in_ref, run_in_ref, kv2_ref, sent_ref, acc_ref, run_ref
):
    acc_ref[...] = acc_in_ref[...]
    run_ref[...] = run_in_ref[...]
    attend_slots(2, kv2_ref, other_ref[:QROWS, :], eff_ref, pos_ref[...], run_ref, acc_ref)
    peak = run_ref[0:1, :]
    total = run_ref[1:2, :]
    peak_high = peak.astype(jnp.bfloat16).astype(jnp.float32)
    total_high = total.astype(jnp.bfloat16).astype(jnp.float32)
    stats = jnp.concatenate(
        [
            peak_high,
            peak - peak_high,
            total_high,
            total - total_high,
            jnp.zeros((12, QROWS), jnp.float32),
        ],
        axis=0,
    )
    sent_ref[:HD, :] = (acc_ref[...] / total).astype(jnp.bfloat16)
    sent_ref[HD:, :] = stats.astype(jnp.bfloat16)


def own_kernel(
    flag_ref,
    own_ref,
    other_ref,
    eff_ref,
    fresh_eff_ref,
    pos_ref,
    kv0_ref,
    kv1_ref,
    kv2_ref,
    kv3_ref,
    acc_ref,
    run_ref,
):
    queries = own_ref[:QROWS, :]
    pos = pos_ref[...]
    attend_fresh(queries, flag_ref, own_ref, other_ref, fresh_eff_ref, pos, run_ref, acc_ref)
    for k, kv_ref in ((0, kv0_ref), (1, kv1_ref), (2, kv2_ref), (3, kv3_ref)):
        attend_slots(k, kv_ref, queries, eff_ref, pos, run_ref, acc_ref)


def merge_kernel(acc_ref, run_ref, got_ref, out_ref):
    stats = got_ref[HD:, :].astype(jnp.float32)
    got_peak = stats[0:1, :] + stats[1:2, :]
    got_total = stats[2:3, :] + stats[3:4, :]
    peak = run_ref[0:1, :]
    total = run_ref[1:2, :]
    joint = jnp.maximum(peak, got_peak)
    mine = jnp.exp2(peak - joint)
    theirs = jnp.exp2(got_peak - joint) * got_total
    whole = mine * total + theirs
    mixed = acc_ref[...] * (mine / whole) + got_ref[:HD, :].astype(jnp.float32) * (theirs / whole)
    turned = mixed.T.astype(jnp.bfloat16)
    for head in range(QS):
        out_ref[:, pl.ds(head * HD, HD)] = turned[head * ROWS : (head + 1) * ROWS, :]


def body(hidden, norm_gain, q_weight, kv_weight, cache_store, location, stretch_ids, rec_pos):
    x = lax.axis_index("x")
    z = lax.axis_index("z")
    y = lax.axis_index("y")
    c = lax.axis_index("c")
    my_tp = y * NC + c
    which_half = my_tp // KVH
    is_first = which_half == 0
    positions = rec_pos[0]
    own_list = stretch_ids[0]
    int_rows = jnp.arange(CH_DEV, dtype=jnp.int32)
    table = jnp.arange(location.shape[0], dtype=jnp.int32)

    store = lax.all_gather(cache_store[:, 0], "z", axis=0, tiled=True)

    listed = jnp.pad(own_list.astype(jnp.bfloat16)[None, :], ((0, 15), (0, COLS - MAXC)))
    weight = jnp.concatenate([q_weight[:, 0], kv_weight[:, 0]], axis=1)
    weight = jnp.concatenate([weight, listed], axis=0)

    far_weight = shifted(weight, "x", NX, -2)
    place = jnp.stack([x, z // 2])
    blocks = call(
        spread_kernel, jax.ShapeDtypeStruct((NZ * NY * NC, 8, HD), jnp.bfloat16), "spread"
    )(hidden[0])
    blocks = lax.all_to_all(blocks, ("z", "y", "c"), 0, 0, tiled=True)
    blocks, weight, far_weight = lax.optimization_barrier((blocks, weight, far_weight))
    weights = [weight, shifted(weight, "x", NX, -1), far_weight, shifted(weight, "x", NX, -3)]
    blocks = blocks.reshape(NZ, NX, 4, 8, HD)
    smem = pl.BlockSpec(memory_space=pltpu.SMEM)
    vmem = pl.BlockSpec(memory_space=pltpu.VMEM)
    hbm = pl.BlockSpec(memory_space=pltpu.MemorySpace.HBM)
    blocks = pl.pallas_call(
        gather_kernel,
        out_shape=jax.ShapeDtypeStruct((NY, NZ, 8, NX * HD), jnp.bfloat16),
        in_specs=[smem, vmem],
        out_specs=vmem,
        name="gather",
        compiler_params=pltpu.CompilerParams(vmem_limit_bytes=32 * 1024 * 1024),
        cost_estimate=pl.CostEstimate(flops=0, bytes_accessed=1 << 20, transcendentals=0),
    )(place, blocks)
    tokens = lax.all_to_all(blocks, "y", 0, 0, tiled=True)

    steps = jnp.arange(NZ, dtype=jnp.int32)
    row_ids = ((x * NZ + steps)[:, None] * CH_DEV + int_rows[None, :]).reshape(-1)
    here = location[None, :] == row_ids[:, None]
    held = jnp.sum(jnp.where(here, table, 0), axis=1).astype(jnp.float32)
    held = jnp.broadcast_to(held[:, None], (NZ * CH_DEV, HD))

    frequency = jnp.exp(
        -math.log(theta_base) * jnp.arange(HD // 2, dtype=jnp.float32) / (HD // 2)
    )
    angles = positions.astype(jnp.float32)[:, None] * frequency[None, :]
    cos = jnp.cos(angles)
    sin = jnp.sin(angles)
    cos = jnp.concatenate([cos, cos], axis=1)
    sin = jnp.concatenate([-sin, sin], axis=1)
    fresh_cos = jnp.where(is_first, cos, 1.0)
    fresh_sin = jnp.where(is_first, sin, 0.0)
    scale = math.log2(math.e) / math.sqrt(HD)

    own_row = jnp.sum(jnp.where(own_list[:, None] == table[None, :], location[None, :], 0), axis=1)
    own_shard = own_row // CH_DEV
    slot_shard = (x * NZ + jnp.arange(MAXC, dtype=jnp.int32)) % (NX * NZ)
    match = (own_shard[None, :] == slot_shard[:, None]) & (own_list >= 0)[None, :]
    slot_order = jnp.sum(jnp.where(match, jnp.arange(MAXC, dtype=jnp.int32), 0), axis=1)
    slot_live = jnp.any(match, axis=1)
    key_pos = (
        slot_order[None, :] * STRETCH
        + which_half * HALF
        + jnp.arange(HALF, dtype=jnp.int32)[:, None]
    )
    replaced = jnp.any(key_pos[:, :, None] == positions[None, None, :], axis=2)
    eff = jnp.where(replaced | ~slot_live[None, :], far_away, key_pos)
    fresh_eff = jnp.where(positions % STRETCH // HALF == which_half, positions, far_away)
    fresh_eff = jnp.broadcast_to(fresh_eff[:, None], (ROWS, HD))
    pos_row = jnp.tile(positions, QS).reshape(1, QROWS)

    gain = lax.dynamic_index_in_dim(norm_gain.reshape(NX, NZ, NC * HD), z, 1, keepdims=False)
    gain = lax.dynamic_slice_in_dim(jnp.concatenate([gain, gain], axis=0), x, NX, 0)
    gain = gain.astype(jnp.float32).reshape(1, NX * NC * HD)

    turns = (cos * scale, sin * scale, fresh_cos, fresh_sin)
    tokens, weights, turns, eff, fresh_eff, pos_row, gain, held = lax.optimization_barrier(
        (tokens, weights, turns, eff, fresh_eff, pos_row, gain, held)
    )
    mate_tokens = swap_cores(tokens)

    partial, send_rows = pl.pallas_call(
        project_kernel,
        out_shape=[
            jax.ShapeDtypeStruct((NZ, ROWS + 8, COLS), jnp.bfloat16),
            jax.ShapeDtypeStruct((NX, NZ, HD), jnp.int32),
        ],
        in_specs=[smem] + [vmem] * 8,
        out_specs=[vmem] * 2,
        name="project",
        compiler_params=pltpu.CompilerParams(vmem_limit_bytes=32 * 1024 * 1024),
        cost_estimate=pl.CostEstimate(
            flops=2 * NZ * ROWS * 1024 * COLS, bytes_accessed=1 << 22, transcendentals=0
        ),
    )(c.reshape(1), tokens, mate_tokens, gain, held, *weights)
    parts = lax.all_to_all(partial, "z", 0, 0, tiled=True)

    def pick(which, rows):
        return pl.pallas_call(
            functools.partial(pick_kernel, which),
            out_shape=[jax.ShapeDtypeStruct((NZ, HALF, 2 * HD), jnp.bfloat16)] * len(which),
            in_specs=[vmem, hbm],
            out_specs=[vmem] * len(which),
            scratch_shapes=[
                pltpu.SMEM((NX, NZ, HD), jnp.int32),
                pltpu.SemaphoreType.DMA((len(which) * NZ,)),
                pltpu.SemaphoreType.DMA,
            ],
            name="pick",
            compiler_params=pltpu.CompilerParams(vmem_limit_bytes=50 * 1024 * 1024),
            cost_estimate=pl.CostEstimate(
                flops=0, bytes_accessed=len(which) << 20, transcendentals=0
            ),
        )(rows, store)

    picked = dict(zip((2, 1, 3), pick((2, 1, 3), send_rows)))
    arrived = {k: shifted(picked[k], "x", NX, -k) for k in (2, 1, 3)}
    own_rows, parts = lax.optimization_barrier((send_rows, parts))
    arrived[0] = pick((0,), own_rows)[0]

    own = call(
        finish_kernel, jax.ShapeDtypeStruct((QROWS + ROWS, HD), jnp.bfloat16), "finish"
    )(parts, *turns)
    other = exchange(own)

    params = pltpu.CompilerParams(vmem_limit_bytes=32 * 1024 * 1024)
    run_shapes = [
        jax.ShapeDtypeStruct((HD, QROWS), jnp.float32),
        jax.ShapeDtypeStruct((8, QROWS), jnp.float32),
    ]

    def cost(count):
        pairs = count * NZ * HALF * QROWS
        return pl.CostEstimate(flops=4 * pairs * HD, bytes_accessed=count << 19, transcendentals=pairs)

    common = (which_half.reshape(1), own, other, eff, fresh_eff, pos_row)
    acc, run = pl.pallas_call(
        other_near_kernel,
        out_shape=run_shapes,
        in_specs=[smem] + [vmem] * 8,
        out_specs=[vmem] * 2,
        name="other_near",
        compiler_params=params,
        cost_estimate=cost(3),
    )(*common, arrived[0], arrived[1], arrived[3])
    sent = pl.pallas_call(
        other_far_kernel,
        out_shape=jax.ShapeDtypeStruct((HD + 16, QROWS), jnp.bfloat16),
        in_specs=[vmem] * 6,
        out_specs=vmem,
        scratch_shapes=[pltpu.VMEM(r.shape, r.dtype) for r in run_shapes],
        name="other_far",
        compiler_params=params,
        cost_estimate=cost(1),
    )(other, eff, pos_row, acc, run, arrived[2])
    got = exchange(sent)
    queries, allowed, sent = lax.optimization_barrier((own, eff, sent))
    own_acc, own_run = pl.pallas_call(
        own_kernel,
        out_shape=run_shapes,
        in_specs=[smem] + [vmem] * 9,
        out_specs=[vmem] * 2,
        name="own",
        compiler_params=params,
        cost_estimate=cost(4),
    )(which_half.reshape(1), queries, other, allowed, fresh_eff, pos_row, *[arrived[k] for k in range(NX)])
    attended = call(merge_kernel, jax.ShapeDtypeStruct((ROWS, QW), jnp.bfloat16), "merge")(
        own_acc, own_run, got
    )
    return attended.reshape(1, ROWS, 1, QW)


def solution(mesh):
    fine = Mesh(mesh.devices.reshape(NX, NZ, NY, NC), ("x", "z", "y", "c"))
    in_specs = (
        P(STORE, None, TP),
        P(),
        P(STORE, TP, None),
        P(STORE, TP, None),
        P(STORE, TP, None, None),
        P(),
        P(STORE, None),
        P(STORE, None),
    )
    return jax.shard_map(
        body, mesh=fine, in_specs=in_specs, out_specs=P(STORE, None, TP, None), check_vma=False
    )
```

```python
import functools
import math

import jax
import jax.numpy as jnp
from jax import lax
from jax.experimental import pallas as pl
from jax.experimental.pallas import tpu as pltpu
from jax.sharding import Mesh
from jax.sharding import PartitionSpec as P

NX, NZ, NY, NC = 4, 8, 8, 2
KVH = 8
HD = 128
STRETCH = 256
MAXC = 32
CH_DEV = 8
QS = 4
HALF = 128
ROWS = 64
D = 8192
QW = QS * HD
COLS = QW + HD
QROWS = QS * ROWS

theta_base = 500000.0
neg_large = -1e30
far_away = 1 << 29

STORE = ("x", "z")
TP = ("y", "c")
NT = (((1,), (1,)), ((), ()))
TN = (((0,), (0,)), ((), ()))


def exchange(block):
    return lax.ppermute(block, "y", [(i, (i + NY // 2) % NY) for i in range(NY)])


def swap_cores(block):
    return lax.ppermute(block, "c", [(0, 1), (1, 0)])


def shifted(block, axis, count, by):
    return lax.ppermute(block, axis, [(i, (i + by) % count) for i in range(count)])


def call(kernel, outs, name, flops=0, bytes_accessed=0):
    return pl.pallas_call(
        kernel,
        out_shape=outs,
        name=name,
        compiler_params=pltpu.CompilerParams(vmem_limit_bytes=32 * 1024 * 1024),
        cost_estimate=pl.CostEstimate(
            flops=flops, bytes_accessed=bytes_accessed, transcendentals=0
        ),
    )


def project_kernel(
    core_ref,
    mine_ref,
    mate_ref,
    gain_ref,
    held_ref,
    w0_ref,
    w1_ref,
    w2_ref,
    w3_ref,
    out_ref,
    rows_ref,
):
    lane = lax.broadcasted_iota(jnp.int32, (NZ * CH_DEV, HD), 1)
    line = lax.broadcasted_iota(jnp.int32, (NZ * CH_DEV, HD), 0)
    for k, w_ref in enumerate((w0_ref, w1_ref, w2_ref, w3_ref)):
        listed = w_ref[2 * HD :, :HD].astype(jnp.float32)[0:1, :]
        hit = (held_ref[...] == listed) & (lane < MAXC)
        found = jnp.where(hit, (line % CH_DEV).astype(jnp.float32), 0.0)
        found = jnp.sum(found.reshape(NZ, CH_DEV, HD), axis=1)
        found = jnp.sum(found, axis=1, keepdims=True).astype(jnp.int32)
        base = lax.broadcasted_iota(jnp.int32, (NZ, HD), 0) * CH_DEV
        rows_ref[k] = base + jnp.minimum(found, CH_DEV - 1)

    weights = jnp.concatenate([w[: 2 * HD, :] for w in (w0_ref, w1_ref, w2_ref, w3_ref)], axis=0)
    gain = gain_ref[...]
    is_zero = core_ref[0] == 0
    rows = []
    stats = []
    for request in range(NZ):
        tall = []
        for y in range(NY):
            mine = mine_ref[y, request].astype(jnp.float32)
            mate = mate_ref[y, request].astype(jnp.float32)
            zero = jnp.broadcast_to(is_zero, mine.shape)
            halves = [jnp.where(zero, mine, mate), jnp.where(zero, mate, mine)]
            tall.append(
                jnp.concatenate(
                    [halves[c][:, k * HD : (k + 1) * HD] for k in range(NX) for c in range(NC)],
                    axis=1,
                )
            )
        wide = jnp.concatenate(tall, axis=0)
        rows.append((wide * gain).astype(jnp.bfloat16))
        squares = jnp.zeros((ROWS, HD), jnp.float32)
        for at in range(0, wide.shape[1], HD):
            piece = wide[:, at : at + HD]
            squares += piece * piece
        squares = jnp.concatenate([squares, jnp.zeros_like(squares)], axis=0)
        row = jnp.sum(squares.T, axis=0, keepdims=True)
        high = row.astype(jnp.bfloat16).astype(jnp.float32)
        stat = jnp.concatenate([high, row - high, jnp.zeros((6, HD), jnp.float32)], axis=0)
        stats.append(jnp.concatenate([stat, jnp.zeros((8, QW), jnp.float32)], axis=1))
    total = jnp.dot(jnp.concatenate(rows, axis=0), weights, preferred_element_type=jnp.float32)
    for request in range(NZ):
        block = total[request * ROWS : (request + 1) * ROWS]
        block = jnp.concatenate([block, stats[request]], axis=0)
        out_ref[request] = block.astype(jnp.bfloat16)


def finish_kernel(parts_ref, cos_ref, sin_ref, fcos_ref, fsin_ref, out_ref):
    inverse = None
    for group in range(QS + 1):
        lanes = pl.ds(group * HD, HD)
        total = parts_ref[0, :, lanes].astype(jnp.float32)
        for part in range(1, NZ):
            total += parts_ref[part, :, lanes].astype(jnp.float32)
        if inverse is None:
            squares = total[ROWS : ROWS + 1, :] + total[ROWS + 1 : ROWS + 2, :]
            inverse = lax.rsqrt(squares * (1.0 / D) + 1e-05)
            inverse = jnp.broadcast_to(inverse, (HD, HD)).T[:ROWS]
        total = total[:ROWS] * inverse
        cos = cos_ref[...] if group < QS else fcos_ref[...]
        sin = sin_ref[...] if group < QS else fsin_ref[...]
        turned = total * cos + pltpu.roll(total, HD // 2, 1) * sin
        out_ref[pl.ds(group * ROWS, ROWS), :] = turned.astype(jnp.bfloat16)


def pick_kernel(which, rows_ref, store_ref, *refs):
    outs, (table_ref, sem, table_sem) = refs[: len(which)], refs[len(which) :]
    table = pltpu.make_async_copy(rows_ref, table_ref, table_sem)
    table.start()
    table.wait()
    copies = []
    for at, k in enumerate(which):
        for i in range(NZ):
            row = table_ref[(NX - k) % NX, i, 0]
            copies.append(
                pltpu.make_async_copy(store_ref.at[row], outs[at].at[i], sem.at[at * NZ + i])
            )
            copies[-1].start()
    for copy in copies:
        copy.wait()


def attend_block(kv_ref, slots, queries, eff_ref, pos, run_ref, acc_ref):
    pieces = []
    for at, slot in slots:
        piece = lax.dot_general(
            kv_ref[at, :, :HD], queries, NT, preferred_element_type=jnp.float32
        )
        pieces.append(jnp.where(eff_ref[:, slot : slot + 1] <= pos, piece, neg_large))
    old_peak = run_ref[0:1, :]
    new_peak = old_peak
    for piece in pieces:
        new_peak = jnp.maximum(new_peak, jnp.max(piece, axis=0, keepdims=True))
    factor = jnp.exp2(old_peak - new_peak)
    total = run_ref[1:2, :] * factor
    acc = acc_ref[...] * factor
    for (at, _), piece in zip(slots, pieces):
        weights = jnp.exp2(piece - new_peak)
        total += jnp.sum(weights, axis=0, keepdims=True)
        acc += lax.dot_general(
            kv_ref[at, :, HD:], weights.astype(jnp.bfloat16), TN, preferred_element_type=jnp.float32
        )
    run_ref[0:1, :] = new_peak
    run_ref[1:2, :] = total
    acc_ref[...] = acc


def attend_slots(k, kv_ref, queries, eff_ref, pos, run_ref, acc_ref):
    for half in range(0, NZ, 4):
        slots = [(half + i, k * NZ + half + i) for i in range(4)]
        attend_block(kv_ref, slots, queries, eff_ref, pos, run_ref, acc_ref)


def attend_fresh(queries, flag_ref, own_ref, other_ref, fresh_eff_ref, pos, run_ref, acc_ref):
    own_piece = own_ref[QROWS:, :]
    other_piece = other_ref[QROWS:, :]
    first = jnp.broadcast_to(flag_ref[0] == 0, own_piece.shape)
    fresh_keys = jnp.where(first, own_piece, other_piece)
    fresh_values = jnp.where(first, other_piece, own_piece)
    scores = lax.dot_general(fresh_keys, queries, NT, preferred_element_type=jnp.float32)
    scores = jnp.where(fresh_eff_ref[:, 0:1] <= pos, scores, neg_large)
    peak = jnp.max(scores, axis=0, keepdims=True)
    weights = jnp.exp2(scores - peak)
    run_ref[...] = jnp.zeros(run_ref.shape, jnp.float32)
    run_ref[0:1, :] = peak
    run_ref[1:2, :] = jnp.sum(weights, axis=0, keepdims=True)
    acc_ref[...] = lax.dot_general(
        fresh_values, weights.astype(jnp.bfloat16), TN, preferred_element_type=jnp.float32
    )


def other_near_kernel(
    flag_ref,
    own_ref,
    other_ref,
    eff_ref,
    fresh_eff_ref,
    pos_ref,
    kv0_ref,
    kv1_ref,
    kv3_ref,
    acc_ref,
    run_ref,
):
    queries = other_ref[:QROWS, :]
    pos = pos_ref[...]
    attend_fresh(queries, flag_ref, own_ref, other_ref, fresh_eff_ref, pos, run_ref, acc_ref)
    for k, kv_ref in ((0, kv0_ref), (1, kv1_ref), (3, kv3_ref)):
        attend_slots(k, kv_ref, queries, eff_ref, pos, run_ref, acc_ref)


def other_far_kernel(
    other_ref, eff_ref, pos_ref, acc_in_ref, run_in_ref, kv2_ref, sent_ref, acc_ref, run_ref
):
    acc_ref[...] = acc_in_ref[...]
    run_ref[...] = run_in_ref[...]
    attend_slots(2, kv2_ref, other_ref[:QROWS, :], eff_ref, pos_ref[...], run_ref, acc_ref)
    peak = run_ref[0:1, :]
    total = run_ref[1:2, :]
    peak_high = peak.astype(jnp.bfloat16).astype(jnp.float32)
    total_high = total.astype(jnp.bfloat16).astype(jnp.float32)
    stats = jnp.concatenate(
        [
            peak_high,
            peak - peak_high,
            total_high,
            total - total_high,
            jnp.zeros((12, QROWS), jnp.float32),
        ],
        axis=0,
    )
    sent_ref[:HD, :] = (acc_ref[...] / total).astype(jnp.bfloat16)
    sent_ref[HD:, :] = stats.astype(jnp.bfloat16)


def own_kernel(
    flag_ref,
    own_ref,
    other_ref,
    eff_ref,
    fresh_eff_ref,
    pos_ref,
    kv0_ref,
    kv1_ref,
    kv2_ref,
    kv3_ref,
    acc_ref,
    run_ref,
):
    queries = own_ref[:QROWS, :]
    pos = pos_ref[...]
    attend_fresh(queries, flag_ref, own_ref, other_ref, fresh_eff_ref, pos, run_ref, acc_ref)
    for k, kv_ref in ((0, kv0_ref), (1, kv1_ref), (2, kv2_ref), (3, kv3_ref)):
        attend_slots(k, kv_ref, queries, eff_ref, pos, run_ref, acc_ref)


def merge_kernel(acc_ref, run_ref, got_ref, out_ref):
    stats = got_ref[HD:, :].astype(jnp.float32)
    got_peak = stats[0:1, :] + stats[1:2, :]
    got_total = stats[2:3, :] + stats[3:4, :]
    peak = run_ref[0:1, :]
    total = run_ref[1:2, :]
    joint = jnp.maximum(peak, got_peak)
    mine = jnp.exp2(peak - joint)
    theirs = jnp.exp2(got_peak - joint) * got_total
    whole = mine * total + theirs
    mixed = acc_ref[...] * (mine / whole) + got_ref[:HD, :].astype(jnp.float32) * (theirs / whole)
    turned = mixed.T.astype(jnp.bfloat16)
    for head in range(QS):
        out_ref[:, pl.ds(head * HD, HD)] = turned[head * ROWS : (head + 1) * ROWS, :]


def body(hidden, norm_gain, q_weight, kv_weight, cache_store, location, stretch_ids, rec_pos):
    x = lax.axis_index("x")
    z = lax.axis_index("z")
    y = lax.axis_index("y")
    c = lax.axis_index("c")
    my_tp = y * NC + c
    which_half = my_tp // KVH
    is_first = which_half == 0
    positions = rec_pos[0]
    own_list = stretch_ids[0]
    int_rows = jnp.arange(CH_DEV, dtype=jnp.int32)
    table = jnp.arange(location.shape[0], dtype=jnp.int32)

    store = lax.all_gather(cache_store[:, 0], "z", axis=0, tiled=True)

    listed = jnp.pad(own_list.astype(jnp.bfloat16)[None, :], ((0, 15), (0, COLS - MAXC)))
    weight = jnp.concatenate([q_weight[:, 0], kv_weight[:, 0]], axis=1)
    weight = jnp.concatenate([weight, listed], axis=0)

    far_weight = shifted(weight, "x", NX, -2)
    back_weight = shifted(weight, "x", NX, -3)
    blocks = hidden[0].reshape(NY, 8, 2, NC, HD).transpose(2, 0, 3, 1, 4)
    blocks = jnp.broadcast_to(blocks[None], (4, 2, NY, NC, 8, HD))
    blocks = lax.all_to_all(
        blocks.reshape(NZ * NY * NC, 8, HD), ("z", "y", "c"), 0, 0, tiled=True
    )
    blocks, weight, far_weight, back_weight = lax.optimization_barrier(
        (blocks, weight, far_weight, back_weight)
    )
    weights = [weight, shifted(weight, "x", NX, -1), far_weight, back_weight]
    blocks = blocks.reshape(NZ, NX, 4, 8, HD)
    blocks = lax.dynamic_index_in_dim(blocks, z // 2, 2, keepdims=False)
    blocks = jnp.concatenate([blocks, blocks], axis=1)
    blocks = lax.dynamic_slice_in_dim(blocks, x, NX, 1)
    blocks = blocks.transpose(0, 2, 1, 3).reshape(NZ, 8, NX * HD)
    tokens = lax.all_to_all(
        jnp.broadcast_to(blocks[None], (NY, NZ, 8, NX * HD)), "y", 0, 0, tiled=True
    )
    steps = jnp.arange(NZ, dtype=jnp.int32)
    row_ids = ((x * NZ + steps)[:, None] * CH_DEV + int_rows[None, :]).reshape(-1)
    here = location[None, :] == row_ids[:, None]
    held = jnp.sum(jnp.where(here, table, 0), axis=1).astype(jnp.float32)
    held = jnp.broadcast_to(held[:, None], (NZ * CH_DEV, HD))

    frequency = jnp.exp(
        -math.log(theta_base) * jnp.arange(HD // 2, dtype=jnp.float32) / (HD // 2)
    )
    angles = positions.astype(jnp.float32)[:, None] * frequency[None, :]
    cos = jnp.cos(angles)
    sin = jnp.sin(angles)
    cos = jnp.concatenate([cos, cos], axis=1)
    sin = jnp.concatenate([-sin, sin], axis=1)
    fresh_cos = jnp.where(is_first, cos, 1.0)
    fresh_sin = jnp.where(is_first, sin, 0.0)
    scale = math.log2(math.e) / math.sqrt(HD)

    own_row = jnp.sum(jnp.where(own_list[:, None] == table[None, :], location[None, :], 0), axis=1)
    own_shard = own_row // CH_DEV
    slot_shard = (x * NZ + jnp.arange(MAXC, dtype=jnp.int32)) % (NX * NZ)
    match = (own_shard[None, :] == slot_shard[:, None]) & (own_list >= 0)[None, :]
    slot_order = jnp.sum(jnp.where(match, jnp.arange(MAXC, dtype=jnp.int32), 0), axis=1)
    slot_live = jnp.any(match, axis=1)
    key_pos = (
        slot_order[None, :] * STRETCH
        + which_half * HALF
        + jnp.arange(HALF, dtype=jnp.int32)[:, None]
    )
    replaced = jnp.any(key_pos[:, :, None] == positions[None, None, :], axis=2)
    eff = jnp.where(replaced | ~slot_live[None, :], far_away, key_pos)
    fresh_eff = jnp.where(positions % STRETCH // HALF == which_half, positions, far_away)
    fresh_eff = jnp.broadcast_to(fresh_eff[:, None], (ROWS, HD))
    pos_row = jnp.tile(positions, QS).reshape(1, QROWS)

    gain = lax.dynamic_index_in_dim(norm_gain.reshape(NX, NZ, NC * HD), z, 1, keepdims=False)
    gain = lax.dynamic_slice_in_dim(jnp.concatenate([gain, gain], axis=0), x, NX, 0)
    gain = gain.astype(jnp.float32).reshape(1, NX * NC * HD)

    turns = (cos * scale, sin * scale, fresh_cos, fresh_sin)
    tokens, weights, turns, eff, fresh_eff, pos_row, gain, held = lax.optimization_barrier(
        (tokens, weights, turns, eff, fresh_eff, pos_row, gain, held)
    )
    mate_tokens = swap_cores(tokens)

    smem = pl.BlockSpec(memory_space=pltpu.SMEM)
    vmem = pl.BlockSpec(memory_space=pltpu.VMEM)
    hbm = pl.BlockSpec(memory_space=pltpu.MemorySpace.HBM)
    partial, send_rows = pl.pallas_call(
        project_kernel,
        out_shape=[
            jax.ShapeDtypeStruct((NZ, ROWS + 8, COLS), jnp.bfloat16),
            jax.ShapeDtypeStruct((NX, NZ, HD), jnp.int32),
        ],
        in_specs=[smem] + [vmem] * 8,
        out_specs=[vmem] * 2,
        name="project",
        compiler_params=pltpu.CompilerParams(vmem_limit_bytes=32 * 1024 * 1024),
        cost_estimate=pl.CostEstimate(
            flops=2 * NZ * ROWS * 1024 * COLS, bytes_accessed=1 << 22, transcendentals=0
        ),
    )(c.reshape(1), tokens, mate_tokens, gain, held, *weights)
    parts = lax.all_to_all(partial, "z", 0, 0, tiled=True)

    def pick(which, rows):
        return pl.pallas_call(
            functools.partial(pick_kernel, which),
            out_shape=[jax.ShapeDtypeStruct((NZ, HALF, 2 * HD), jnp.bfloat16)] * len(which),
            in_specs=[vmem, hbm],
            out_specs=[vmem] * len(which),
            scratch_shapes=[
                pltpu.SMEM((NX, NZ, HD), jnp.int32),
                pltpu.SemaphoreType.DMA((len(which) * NZ,)),
                pltpu.SemaphoreType.DMA,
            ],
            name="pick",
            compiler_params=pltpu.CompilerParams(vmem_limit_bytes=50 * 1024 * 1024),
            cost_estimate=pl.CostEstimate(
                flops=0, bytes_accessed=len(which) << 20, transcendentals=0
            ),
        )(rows, store)

    picked = dict(zip((2, 1, 3), pick((2, 1, 3), send_rows)))
    arrived = {k: shifted(picked[k], "x", NX, -k) for k in (2, 1, 3)}
    own_rows, parts = lax.optimization_barrier((send_rows, parts))
    arrived[0] = pick((0,), own_rows)[0]

    own = call(
        finish_kernel, jax.ShapeDtypeStruct((QROWS + ROWS, HD), jnp.bfloat16), "finish"
    )(parts, *turns)
    other = exchange(own)

    params = pltpu.CompilerParams(vmem_limit_bytes=32 * 1024 * 1024)
    run_shapes = [
        jax.ShapeDtypeStruct((HD, QROWS), jnp.float32),
        jax.ShapeDtypeStruct((8, QROWS), jnp.float32),
    ]

    def cost(count):
        pairs = count * NZ * HALF * QROWS
        return pl.CostEstimate(flops=4 * pairs * HD, bytes_accessed=count << 19, transcendentals=pairs)

    common = (which_half.reshape(1), own, other, eff, fresh_eff, pos_row)
    acc, run = pl.pallas_call(
        other_near_kernel,
        out_shape=run_shapes,
        in_specs=[smem] + [vmem] * 8,
        out_specs=[vmem] * 2,
        name="other_near",
        compiler_params=params,
        cost_estimate=cost(3),
    )(*common, arrived[0], arrived[1], arrived[3])
    sent = pl.pallas_call(
        other_far_kernel,
        out_shape=jax.ShapeDtypeStruct((HD + 16, QROWS), jnp.bfloat16),
        in_specs=[vmem] * 6,
        out_specs=vmem,
        scratch_shapes=[pltpu.VMEM(r.shape, r.dtype) for r in run_shapes],
        name="other_far",
        compiler_params=params,
        cost_estimate=cost(1),
    )(other, eff, pos_row, acc, run, arrived[2])
    got = exchange(sent)
    queries, allowed, sent = lax.optimization_barrier((own, eff, sent))
    own_acc, own_run = pl.pallas_call(
        own_kernel,
        out_shape=run_shapes,
        in_specs=[smem] + [vmem] * 9,
        out_specs=[vmem] * 2,
        name="own",
        compiler_params=params,
        cost_estimate=cost(4),
    )(which_half.reshape(1), queries, other, allowed, fresh_eff, pos_row, *[arrived[k] for k in range(NX)])
    attended = call(merge_kernel, jax.ShapeDtypeStruct((ROWS, QW), jnp.bfloat16), "merge")(
        own_acc, own_run, got
    )
    return attended.reshape(1, ROWS, 1, QW)


def solution(mesh):
    fine = Mesh(mesh.devices.reshape(NX, NZ, NY, NC), ("x", "z", "y", "c"))
    in_specs = (
        P(STORE, None, TP),
        P(),
        P(STORE, TP, None),
        P(STORE, TP, None),
        P(STORE, TP, None, None),
        P(),
        P(STORE, None),
        P(STORE, None),
    )
    return jax.shard_map(
        body, mesh=fine, in_specs=in_specs, out_specs=P(STORE, None, TP, None), check_vma=False
    )
```

```python
import functools
import math

import jax
import jax.numpy as jnp
from jax import lax
from jax.experimental import pallas as pl
from jax.experimental.pallas import tpu as pltpu
from jax.sharding import Mesh
from jax.sharding import PartitionSpec as P

NX, NZ, NY, NC = 4, 8, 8, 2
KVH = 8
HD = 128
STRETCH = 256
MAXC = 32
CH_DEV = 8
QS = 4
HALF = 128
ROWS = 64
D = 8192
QW = QS * HD
COLS = QW + HD
QROWS = QS * ROWS

theta_base = 500000.0
neg_large = -1e30
far_away = 1 << 29

STORE = ("x", "z")
TP = ("y", "c")
NT = (((1,), (1,)), ((), ()))
TN = (((0,), (0,)), ((), ()))


def exchange(block):
    return lax.ppermute(block, "y", [(i, (i + NY // 2) % NY) for i in range(NY)])


def swap_cores(block):
    return lax.ppermute(block, "c", [(0, 1), (1, 0)])


def shifted(block, axis, count, by):
    return lax.ppermute(block, axis, [(i, (i + by) % count) for i in range(count)])


def call(kernel, outs, name, flops=0, bytes_accessed=0):
    return pl.pallas_call(
        kernel,
        out_shape=outs,
        name=name,
        compiler_params=pltpu.CompilerParams(vmem_limit_bytes=32 * 1024 * 1024),
        cost_estimate=pl.CostEstimate(
            flops=flops, bytes_accessed=bytes_accessed, transcendentals=0
        ),
    )


def project_kernel(
    core_ref,
    mine_ref,
    mate_ref,
    gain_ref,
    held_ref,
    w0_ref,
    w1_ref,
    w2_ref,
    w3_ref,
    out_ref,
    rows_ref,
):
    lane = lax.broadcasted_iota(jnp.int32, (NZ * CH_DEV, HD), 1)
    line = lax.broadcasted_iota(jnp.int32, (NZ * CH_DEV, HD), 0)
    for k, w_ref in enumerate((w0_ref, w1_ref, w2_ref, w3_ref)):
        listed = w_ref[2 * HD :, :HD].astype(jnp.float32)[0:1, :]
        hit = (held_ref[...] == listed) & (lane < MAXC)
        found = jnp.where(hit, (line % CH_DEV).astype(jnp.float32), 0.0)
        found = jnp.sum(found.reshape(NZ, CH_DEV, HD), axis=1)
        found = jnp.sum(found, axis=1, keepdims=True).astype(jnp.int32)
        base = lax.broadcasted_iota(jnp.int32, (NZ, HD), 0) * CH_DEV
        rows_ref[k] = base + jnp.minimum(found, CH_DEV - 1)

    weights = jnp.concatenate([w[: 2 * HD, :] for w in (w0_ref, w1_ref, w2_ref, w3_ref)], axis=0)
    gain = gain_ref[...]
    is_zero = core_ref[0] == 0
    rows = []
    stats = []
    for request in range(NZ):
        tall = []
        for y in range(NY):
            mine = mine_ref[y, request].astype(jnp.float32)
            mate = mate_ref[y, request].astype(jnp.float32)
            zero = jnp.broadcast_to(is_zero, mine.shape)
            halves = [jnp.where(zero, mine, mate), jnp.where(zero, mate, mine)]
            tall.append(
                jnp.concatenate(
                    [halves[c][:, k * HD : (k + 1) * HD] for k in range(NX) for c in range(NC)],
                    axis=1,
                )
            )
        wide = jnp.concatenate(tall, axis=0)
        rows.append((wide * gain).astype(jnp.bfloat16))
        squares = jnp.zeros((ROWS, HD), jnp.float32)
        for at in range(0, wide.shape[1], HD):
            piece = wide[:, at : at + HD]
            squares += piece * piece
        squares = jnp.concatenate([squares, jnp.zeros_like(squares)], axis=0)
        row = jnp.sum(squares.T, axis=0, keepdims=True)
        high = row.astype(jnp.bfloat16).astype(jnp.float32)
        stat = jnp.concatenate([high, row - high, jnp.zeros((6, HD), jnp.float32)], axis=0)
        stats.append(jnp.concatenate([stat, jnp.zeros((8, QW), jnp.float32)], axis=1))
    total = jnp.dot(jnp.concatenate(rows, axis=0), weights, preferred_element_type=jnp.float32)
    for request in range(NZ):
        block = total[request * ROWS : (request + 1) * ROWS]
        block = jnp.concatenate([block, stats[request]], axis=0)
        out_ref[request] = block.astype(jnp.bfloat16)


def finish_kernel(parts_ref, cos_ref, sin_ref, fcos_ref, fsin_ref, out_ref):
    inverse = None
    for group in range(QS + 1):
        lanes = pl.ds(group * HD, HD)
        total = parts_ref[0, :, lanes].astype(jnp.float32)
        for part in range(1, NZ):
            total += parts_ref[part, :, lanes].astype(jnp.float32)
        if inverse is None:
            squares = total[ROWS : ROWS + 1, :] + total[ROWS + 1 : ROWS + 2, :]
            inverse = lax.rsqrt(squares * (1.0 / D) + 1e-05)
            inverse = jnp.broadcast_to(inverse, (HD, HD)).T[:ROWS]
        total = total[:ROWS] * inverse
        cos = cos_ref[...] if group < QS else fcos_ref[...]
        sin = sin_ref[...] if group < QS else fsin_ref[...]
        turned = total * cos + pltpu.roll(total, HD // 2, 1) * sin
        out_ref[pl.ds(group * ROWS, ROWS), :] = turned.astype(jnp.bfloat16)


def pick_kernel(which, rows_ref, store_ref, *refs):
    outs, (table_ref, sem, table_sem) = refs[: len(which)], refs[len(which) :]
    table = pltpu.make_async_copy(rows_ref, table_ref, table_sem)
    table.start()
    table.wait()
    copies = []
    for at, k in enumerate(which):
        for i in range(NZ):
            row = table_ref[(NX - k) % NX, i, 0]
            copies.append(
                pltpu.make_async_copy(store_ref.at[row], outs[at].at[i], sem.at[at * NZ + i])
            )
            copies[-1].start()
    for copy in copies:
        copy.wait()


def attend_block(kv_ref, slots, queries, eff_ref, pos, run_ref, acc_ref):
    pieces = []
    for at, slot in slots:
        piece = lax.dot_general(
            kv_ref[at, :, :HD], queries, NT, preferred_element_type=jnp.float32
        )
        pieces.append(jnp.where(eff_ref[:, slot : slot + 1] <= pos, piece, neg_large))
    old_peak = run_ref[0:1, :]
    new_peak = old_peak
    for piece in pieces:
        new_peak = jnp.maximum(new_peak, jnp.max(piece, axis=0, keepdims=True))
    factor = jnp.exp2(old_peak - new_peak)
    total = run_ref[1:2, :] * factor
    acc = acc_ref[...] * factor
    for (at, _), piece in zip(slots, pieces):
        weights = jnp.exp2(piece - new_peak)
        total += jnp.sum(weights, axis=0, keepdims=True)
        acc += lax.dot_general(
            kv_ref[at, :, HD:], weights.astype(jnp.bfloat16), TN, preferred_element_type=jnp.float32
        )
    run_ref[0:1, :] = new_peak
    run_ref[1:2, :] = total
    acc_ref[...] = acc


def attend_slots(k, kv_ref, queries, eff_ref, pos, run_ref, acc_ref):
    for half in range(0, NZ, 4):
        slots = [(half + i, k * NZ + half + i) for i in range(4)]
        attend_block(kv_ref, slots, queries, eff_ref, pos, run_ref, acc_ref)


def attend_fresh(queries, flag_ref, own_ref, other_ref, fresh_eff_ref, pos, run_ref, acc_ref):
    own_piece = own_ref[QROWS:, :]
    other_piece = other_ref[QROWS:, :]
    first = jnp.broadcast_to(flag_ref[0] == 0, own_piece.shape)
    fresh_keys = jnp.where(first, own_piece, other_piece)
    fresh_values = jnp.where(first, other_piece, own_piece)
    scores = lax.dot_general(fresh_keys, queries, NT, preferred_element_type=jnp.float32)
    scores = jnp.where(fresh_eff_ref[:, 0:1] <= pos, scores, neg_large)
    peak = jnp.max(scores, axis=0, keepdims=True)
    weights = jnp.exp2(scores - peak)
    run_ref[...] = jnp.zeros(run_ref.shape, jnp.float32)
    run_ref[0:1, :] = peak
    run_ref[1:2, :] = jnp.sum(weights, axis=0, keepdims=True)
    acc_ref[...] = lax.dot_general(
        fresh_values, weights.astype(jnp.bfloat16), TN, preferred_element_type=jnp.float32
    )


def other_near_kernel(
    flag_ref,
    own_ref,
    other_ref,
    eff_ref,
    fresh_eff_ref,
    pos_ref,
    kv0_ref,
    kv2_ref,
    kv1_ref,
    acc_ref,
    run_ref,
):
    queries = other_ref[:QROWS, :]
    pos = pos_ref[...]
    attend_fresh(queries, flag_ref, own_ref, other_ref, fresh_eff_ref, pos, run_ref, acc_ref)
    for k, kv_ref in ((0, kv0_ref), (2, kv2_ref), (1, kv1_ref)):
        attend_slots(k, kv_ref, queries, eff_ref, pos, run_ref, acc_ref)


def other_far_kernel(
    other_ref, eff_ref, pos_ref, acc_in_ref, run_in_ref, kv3_ref, sent_ref, acc_ref, run_ref
):
    acc_ref[...] = acc_in_ref[...]
    run_ref[...] = run_in_ref[...]
    attend_slots(3, kv3_ref, other_ref[:QROWS, :], eff_ref, pos_ref[...], run_ref, acc_ref)
    peak = run_ref[0:1, :]
    total = run_ref[1:2, :]
    peak_high = peak.astype(jnp.bfloat16).astype(jnp.float32)
    total_high = total.astype(jnp.bfloat16).astype(jnp.float32)
    stats = jnp.concatenate(
        [
            peak_high,
            peak - peak_high,
            total_high,
            total - total_high,
            jnp.zeros((12, QROWS), jnp.float32),
        ],
        axis=0,
    )
    sent_ref[:HD, :] = (acc_ref[...] / total).astype(jnp.bfloat16)
    sent_ref[HD:, :] = stats.astype(jnp.bfloat16)


def own_kernel(
    flag_ref,
    own_ref,
    other_ref,
    eff_ref,
    fresh_eff_ref,
    pos_ref,
    kv0_ref,
    kv1_ref,
    kv2_ref,
    kv3_ref,
    acc_ref,
    run_ref,
):
    queries = own_ref[:QROWS, :]
    pos = pos_ref[...]
    attend_fresh(queries, flag_ref, own_ref, other_ref, fresh_eff_ref, pos, run_ref, acc_ref)
    for k, kv_ref in ((0, kv0_ref), (1, kv1_ref), (2, kv2_ref), (3, kv3_ref)):
        attend_slots(k, kv_ref, queries, eff_ref, pos, run_ref, acc_ref)


def merge_kernel(acc_ref, run_ref, got_ref, out_ref):
    stats = got_ref[HD:, :].astype(jnp.float32)
    got_peak = stats[0:1, :] + stats[1:2, :]
    got_total = stats[2:3, :] + stats[3:4, :]
    peak = run_ref[0:1, :]
    total = run_ref[1:2, :]
    joint = jnp.maximum(peak, got_peak)
    mine = jnp.exp2(peak - joint)
    theirs = jnp.exp2(got_peak - joint) * got_total
    whole = mine * total + theirs
    mixed = acc_ref[...] * (mine / whole) + got_ref[:HD, :].astype(jnp.float32) * (theirs / whole)
    turned = mixed.T.astype(jnp.bfloat16)
    for head in range(QS):
        out_ref[:, pl.ds(head * HD, HD)] = turned[head * ROWS : (head + 1) * ROWS, :]


def body(hidden, norm_gain, q_weight, kv_weight, cache_store, location, stretch_ids, rec_pos):
    x = lax.axis_index("x")
    z = lax.axis_index("z")
    y = lax.axis_index("y")
    c = lax.axis_index("c")
    my_tp = y * NC + c
    which_half = my_tp // KVH
    is_first = which_half == 0
    positions = rec_pos[0]
    own_list = stretch_ids[0]
    int_rows = jnp.arange(CH_DEV, dtype=jnp.int32)
    table = jnp.arange(location.shape[0], dtype=jnp.int32)

    store = lax.all_gather(cache_store[:, 0], "z", axis=0, tiled=True)

    listed = jnp.pad(own_list.astype(jnp.bfloat16)[None, :], ((0, 15), (0, COLS - MAXC)))
    weight = jnp.concatenate([q_weight[:, 0], kv_weight[:, 0]], axis=1)
    weight = jnp.concatenate([weight, listed], axis=0)

    far_weight = shifted(weight, "x", NX, -2)
    blocks = hidden[0].reshape(NY, 8, 2, NC, HD).transpose(2, 0, 3, 1, 4)
    blocks = jnp.broadcast_to(blocks[None], (4, 2, NY, NC, 8, HD))
    blocks = lax.all_to_all(
        blocks.reshape(NZ * NY * NC, 8, HD), ("z", "y", "c"), 0, 0, tiled=True
    )
    blocks, weight, far_weight = lax.optimization_barrier((blocks, weight, far_weight))
    weights = [weight, shifted(weight, "x", NX, -1), far_weight, shifted(weight, "x", NX, -3)]
    blocks = blocks.reshape(NZ, NX, 4, 8, HD)
    blocks = lax.dynamic_index_in_dim(blocks, z // 2, 2, keepdims=False)
    blocks = jnp.concatenate([blocks, blocks], axis=1)
    blocks = lax.dynamic_slice_in_dim(blocks, x, NX, 1)
    blocks = blocks.transpose(0, 2, 1, 3).reshape(NZ, 8, NX * HD)
    tokens = lax.all_to_all(
        jnp.broadcast_to(blocks[None], (NY, NZ, 8, NX * HD)), "y", 0, 0, tiled=True
    )
    steps = jnp.arange(NZ, dtype=jnp.int32)
    row_ids = ((x * NZ + steps)[:, None] * CH_DEV + int_rows[None, :]).reshape(-1)
    here = location[None, :] == row_ids[:, None]
    held = jnp.sum(jnp.where(here, table, 0), axis=1).astype(jnp.float32)
    held = jnp.broadcast_to(held[:, None], (NZ * CH_DEV, HD))

    frequency = jnp.exp(
        -math.log(theta_base) * jnp.arange(HD // 2, dtype=jnp.float32) / (HD // 2)
    )
    angles = positions.astype(jnp.float32)[:, None] * frequency[None, :]
    cos = jnp.cos(angles)
    sin = jnp.sin(angles)
    cos = jnp.concatenate([cos, cos], axis=1)
    sin = jnp.concatenate([-sin, sin], axis=1)
    fresh_cos = jnp.where(is_first, cos, 1.0)
    fresh_sin = jnp.where(is_first, sin, 0.0)
    scale = math.log2(math.e) / math.sqrt(HD)

    own_row = jnp.sum(jnp.where(own_list[:, None] == table[None, :], location[None, :], 0), axis=1)
    own_shard = own_row // CH_DEV
    slot_shard = (x * NZ + jnp.arange(MAXC, dtype=jnp.int32)) % (NX * NZ)
    match = (own_shard[None, :] == slot_shard[:, None]) & (own_list >= 0)[None, :]
    slot_order = jnp.sum(jnp.where(match, jnp.arange(MAXC, dtype=jnp.int32), 0), axis=1)
    slot_live = jnp.any(match, axis=1)
    key_pos = (
        slot_order[None, :] * STRETCH
        + which_half * HALF
        + jnp.arange(HALF, dtype=jnp.int32)[:, None]
    )
    replaced = jnp.any(key_pos[:, :, None] == positions[None, None, :], axis=2)
    eff = jnp.where(replaced | ~slot_live[None, :], far_away, key_pos)
    fresh_eff = jnp.where(positions % STRETCH // HALF == which_half, positions, far_away)
    fresh_eff = jnp.broadcast_to(fresh_eff[:, None], (ROWS, HD))
    pos_row = jnp.tile(positions, QS).reshape(1, QROWS)

    gain = lax.dynamic_index_in_dim(norm_gain.reshape(NX, NZ, NC * HD), z, 1, keepdims=False)
    gain = lax.dynamic_slice_in_dim(jnp.concatenate([gain, gain], axis=0), x, NX, 0)
    gain = gain.astype(jnp.float32).reshape(1, NX * NC * HD)

    turns = (cos * scale, sin * scale, fresh_cos, fresh_sin)
    tokens, weights, turns, eff, fresh_eff, pos_row, gain, held = lax.optimization_barrier(
        (tokens, weights, turns, eff, fresh_eff, pos_row, gain, held)
    )
    mate_tokens = swap_cores(tokens)

    smem = pl.BlockSpec(memory_space=pltpu.SMEM)
    vmem = pl.BlockSpec(memory_space=pltpu.VMEM)
    hbm = pl.BlockSpec(memory_space=pltpu.MemorySpace.HBM)
    partial, send_rows = pl.pallas_call(
        project_kernel,
        out_shape=[
            jax.ShapeDtypeStruct((NZ, ROWS + 8, COLS), jnp.bfloat16),
            jax.ShapeDtypeStruct((NX, NZ, HD), jnp.int32),
        ],
        in_specs=[smem] + [vmem] * 8,
        out_specs=[vmem] * 2,
        name="project",
        compiler_params=pltpu.CompilerParams(vmem_limit_bytes=32 * 1024 * 1024),
        cost_estimate=pl.CostEstimate(
            flops=2 * NZ * ROWS * 1024 * COLS, bytes_accessed=1 << 22, transcendentals=0
        ),
    )(c.reshape(1), tokens, mate_tokens, gain, held, *weights)
    parts = lax.all_to_all(partial, "z", 0, 0, tiled=True)

    def pick(which, rows):
        return pl.pallas_call(
            functools.partial(pick_kernel, which),
            out_shape=[jax.ShapeDtypeStruct((NZ, HALF, 2 * HD), jnp.bfloat16)] * len(which),
            in_specs=[vmem, hbm],
            out_specs=[vmem] * len(which),
            scratch_shapes=[
                pltpu.SMEM((NX, NZ, HD), jnp.int32),
                pltpu.SemaphoreType.DMA((len(which) * NZ,)),
                pltpu.SemaphoreType.DMA,
            ],
            name="pick",
            compiler_params=pltpu.CompilerParams(vmem_limit_bytes=50 * 1024 * 1024),
            cost_estimate=pl.CostEstimate(
                flops=0, bytes_accessed=len(which) << 20, transcendentals=0
            ),
        )(rows, store)

    picked = dict(zip((2, 1, 3), pick((2, 1, 3), send_rows)))
    arrived = {k: shifted(picked[k], "x", NX, -k) for k in (2, 1, 3)}
    own_rows, parts = lax.optimization_barrier((send_rows, parts))
    arrived[0] = pick((0,), own_rows)[0]

    own = call(
        finish_kernel, jax.ShapeDtypeStruct((QROWS + ROWS, HD), jnp.bfloat16), "finish"
    )(parts, *turns)
    other = exchange(own)

    params = pltpu.CompilerParams(vmem_limit_bytes=32 * 1024 * 1024)
    run_shapes = [
        jax.ShapeDtypeStruct((HD, QROWS), jnp.float32),
        jax.ShapeDtypeStruct((8, QROWS), jnp.float32),
    ]

    def cost(count):
        pairs = count * NZ * HALF * QROWS
        return pl.CostEstimate(flops=4 * pairs * HD, bytes_accessed=count << 19, transcendentals=pairs)

    common = (which_half.reshape(1), own, other, eff, fresh_eff, pos_row)
    acc, run = pl.pallas_call(
        other_near_kernel,
        out_shape=run_shapes,
        in_specs=[smem] + [vmem] * 8,
        out_specs=[vmem] * 2,
        name="other_near",
        compiler_params=params,
        cost_estimate=cost(3),
    )(*common, arrived[0], arrived[2], arrived[1])
    sent = pl.pallas_call(
        other_far_kernel,
        out_shape=jax.ShapeDtypeStruct((HD + 16, QROWS), jnp.bfloat16),
        in_specs=[vmem] * 6,
        out_specs=vmem,
        scratch_shapes=[pltpu.VMEM(r.shape, r.dtype) for r in run_shapes],
        name="other_far",
        compiler_params=params,
        cost_estimate=cost(1),
    )(other, eff, pos_row, acc, run, arrived[3])
    got = exchange(sent)
    queries, allowed, sent = lax.optimization_barrier((own, eff, sent))
    own_acc, own_run = pl.pallas_call(
        own_kernel,
        out_shape=run_shapes,
        in_specs=[smem] + [vmem] * 9,
        out_specs=[vmem] * 2,
        name="own",
        compiler_params=params,
        cost_estimate=cost(4),
    )(which_half.reshape(1), queries, other, allowed, fresh_eff, pos_row, *[arrived[k] for k in range(NX)])
    attended = call(merge_kernel, jax.ShapeDtypeStruct((ROWS, QW), jnp.bfloat16), "merge")(
        own_acc, own_run, got
    )
    return attended.reshape(1, ROWS, 1, QW)


def solution(mesh):
    fine = Mesh(mesh.devices.reshape(NX, NZ, NY, NC), ("x", "z", "y", "c"))
    in_specs = (
        P(STORE, None, TP),
        P(),
        P(STORE, TP, None),
        P(STORE, TP, None),
        P(STORE, TP, None, None),
        P(),
        P(STORE, None),
        P(STORE, None),
    )
    return jax.shard_map(
        body, mesh=fine, in_specs=in_specs, out_specs=P(STORE, None, TP, None), check_vma=False
    )
```

```python
import functools
import math

import jax
import jax.numpy as jnp
from jax import lax
from jax.experimental import pallas as pl
from jax.experimental.pallas import tpu as pltpu
from jax.sharding import Mesh
from jax.sharding import PartitionSpec as P

NX, NZ, NY, NC = 4, 8, 8, 2
KVH = 8
HD = 128
STRETCH = 256
MAXC = 32
CH_DEV = 8
QS = 4
HALF = 128
ROWS = 64
D = 8192
QW = QS * HD
COLS = QW + HD
QROWS = QS * ROWS

theta_base = 500000.0
neg_large = -1e30
far_away = 1 << 29

STORE = ("x", "z")
TP = ("y", "c")
NT = (((1,), (1,)), ((), ()))
TN = (((0,), (0,)), ((), ()))


def exchange(block):
    return lax.ppermute(block, "y", [(i, (i + NY // 2) % NY) for i in range(NY)])


def swap_cores(block):
    return lax.ppermute(block, "c", [(0, 1), (1, 0)])


def shifted(block, axis, count, by):
    return lax.ppermute(block, axis, [(i, (i + by) % count) for i in range(count)])


def call(kernel, outs, name, flops=0, bytes_accessed=0):
    return pl.pallas_call(
        kernel,
        out_shape=outs,
        name=name,
        compiler_params=pltpu.CompilerParams(vmem_limit_bytes=32 * 1024 * 1024),
        cost_estimate=pl.CostEstimate(
            flops=flops, bytes_accessed=bytes_accessed, transcendentals=0
        ),
    )


def project_kernel(
    core_ref,
    mine_ref,
    mate_ref,
    gain_ref,
    held_ref,
    w0_ref,
    w1_ref,
    w2_ref,
    w3_ref,
    out_ref,
    rows_ref,
):
    lane = lax.broadcasted_iota(jnp.int32, (NZ * CH_DEV, HD), 1)
    line = lax.broadcasted_iota(jnp.int32, (NZ * CH_DEV, HD), 0)
    for k, w_ref in enumerate((w0_ref, w1_ref, w2_ref, w3_ref)):
        listed = w_ref[2 * HD :, :HD].astype(jnp.float32)[0:1, :]
        hit = (held_ref[...] == listed) & (lane < MAXC)
        found = jnp.where(hit, (line % CH_DEV).astype(jnp.float32), 0.0)
        found = jnp.sum(found.reshape(NZ, CH_DEV, HD), axis=1)
        found = jnp.sum(found, axis=1, keepdims=True).astype(jnp.int32)
        base = lax.broadcasted_iota(jnp.int32, (NZ, HD), 0) * CH_DEV
        rows_ref[k] = base + jnp.minimum(found, CH_DEV - 1)

    weights = jnp.concatenate([w[: 2 * HD, :] for w in (w0_ref, w1_ref, w2_ref, w3_ref)], axis=0)
    gain = gain_ref[...]
    is_zero = core_ref[0] == 0
    rows = []
    stats = []
    for request in range(NZ):
        tall = []
        for y in range(NY):
            mine = mine_ref[y, request].astype(jnp.float32)
            mate = mate_ref[y, request].astype(jnp.float32)
            zero = jnp.broadcast_to(is_zero, mine.shape)
            halves = [jnp.where(zero, mine, mate), jnp.where(zero, mate, mine)]
            tall.append(
                jnp.concatenate(
                    [halves[c][:, k * HD : (k + 1) * HD] for k in range(NX) for c in range(NC)],
                    axis=1,
                )
            )
        wide = jnp.concatenate(tall, axis=0)
        rows.append((wide * gain).astype(jnp.bfloat16))
        squares = jnp.zeros((ROWS, HD), jnp.float32)
        for at in range(0, wide.shape[1], HD):
            piece = wide[:, at : at + HD]
            squares += piece * piece
        squares = jnp.concatenate([squares, jnp.zeros_like(squares)], axis=0)
        row = jnp.sum(squares.T, axis=0, keepdims=True)
        high = row.astype(jnp.bfloat16).astype(jnp.float32)
        stat = jnp.concatenate([high, row - high, jnp.zeros((6, HD), jnp.float32)], axis=0)
        stats.append(jnp.concatenate([stat, jnp.zeros((8, QW), jnp.float32)], axis=1))
    total = jnp.dot(jnp.concatenate(rows, axis=0), weights, preferred_element_type=jnp.float32)
    for request in range(NZ):
        block = total[request * ROWS : (request + 1) * ROWS]
        block = jnp.concatenate([block, stats[request]], axis=0)
        out_ref[request] = block.astype(jnp.bfloat16)


def finish_kernel(parts_ref, cos_ref, sin_ref, fcos_ref, fsin_ref, out_ref):
    inverse = None
    for group in range(QS + 1):
        lanes = pl.ds(group * HD, HD)
        total = parts_ref[0, :, lanes].astype(jnp.float32)
        for part in range(1, NZ):
            total += parts_ref[part, :, lanes].astype(jnp.float32)
        if inverse is None:
            squares = total[ROWS : ROWS + 1, :] + total[ROWS + 1 : ROWS + 2, :]
            inverse = lax.rsqrt(squares * (1.0 / D) + 1e-05)
            inverse = jnp.broadcast_to(inverse, (HD, HD)).T[:ROWS]
        total = total[:ROWS] * inverse
        cos = cos_ref[...] if group < QS else fcos_ref[...]
        sin = sin_ref[...] if group < QS else fsin_ref[...]
        turned = total * cos + pltpu.roll(total, HD // 2, 1) * sin
        out_ref[pl.ds(group * ROWS, ROWS), :] = turned.astype(jnp.bfloat16)


def pick_kernel(which, rows_ref, store_ref, *refs):
    outs, (table_ref, sem, table_sem) = refs[: len(which)], refs[len(which) :]
    table = pltpu.make_async_copy(rows_ref, table_ref, table_sem)
    table.start()
    table.wait()
    copies = []
    for at, k in enumerate(which):
        for i in range(NZ):
            row = table_ref[(NX - k) % NX, i, 0]
            copies.append(
                pltpu.make_async_copy(store_ref.at[row], outs[at].at[i], sem.at[at * NZ + i])
            )
            copies[-1].start()
    for copy in copies:
        copy.wait()


def attend_block(kv_ref, slots, queries, eff_ref, pos, run_ref, acc_ref):
    pieces = []
    for at, slot in slots:
        piece = lax.dot_general(
            kv_ref[at, :, :HD], queries, NT, preferred_element_type=jnp.float32
        )
        pieces.append(jnp.where(eff_ref[:, slot : slot + 1] <= pos, piece, neg_large))
    old_peak = run_ref[0:1, :]
    new_peak = old_peak
    for piece in pieces:
        new_peak = jnp.maximum(new_peak, jnp.max(piece, axis=0, keepdims=True))
    factor = jnp.exp2(old_peak - new_peak)
    total = run_ref[1:2, :] * factor
    acc = acc_ref[...] * factor
    for (at, _), piece in zip(slots, pieces):
        weights = jnp.exp2(piece - new_peak)
        total += jnp.sum(weights, axis=0, keepdims=True)
        acc += lax.dot_general(
            kv_ref[at, :, HD:], weights.astype(jnp.bfloat16), TN, preferred_element_type=jnp.float32
        )
    run_ref[0:1, :] = new_peak
    run_ref[1:2, :] = total
    acc_ref[...] = acc


def attend_slots(k, kv_ref, queries, eff_ref, pos, run_ref, acc_ref):
    for half in range(0, NZ, 4):
        slots = [(half + i, k * NZ + half + i) for i in range(4)]
        attend_block(kv_ref, slots, queries, eff_ref, pos, run_ref, acc_ref)


def attend_fresh(queries, flag_ref, own_ref, other_ref, fresh_eff_ref, pos, run_ref, acc_ref):
    own_piece = own_ref[QROWS:, :]
    other_piece = other_ref[QROWS:, :]
    first = jnp.broadcast_to(flag_ref[0] == 0, own_piece.shape)
    fresh_keys = jnp.where(first, own_piece, other_piece)
    fresh_values = jnp.where(first, other_piece, own_piece)
    scores = lax.dot_general(fresh_keys, queries, NT, preferred_element_type=jnp.float32)
    scores = jnp.where(fresh_eff_ref[:, 0:1] <= pos, scores, neg_large)
    peak = jnp.max(scores, axis=0, keepdims=True)
    weights = jnp.exp2(scores - peak)
    run_ref[...] = jnp.zeros(run_ref.shape, jnp.float32)
    run_ref[0:1, :] = peak
    run_ref[1:2, :] = jnp.sum(weights, axis=0, keepdims=True)
    acc_ref[...] = lax.dot_general(
        fresh_values, weights.astype(jnp.bfloat16), TN, preferred_element_type=jnp.float32
    )


def other_kernel(
    flag_ref,
    own_ref,
    other_ref,
    eff_ref,
    fresh_eff_ref,
    pos_ref,
    kv0_ref,
    kv2_ref,
    kv1_ref,
    kv3_ref,
    sent_ref,
    acc_ref,
    run_ref,
):
    queries = other_ref[:QROWS, :]
    pos = pos_ref[...]
    attend_fresh(queries, flag_ref, own_ref, other_ref, fresh_eff_ref, pos, run_ref, acc_ref)
    for k, kv_ref in ((0, kv0_ref), (2, kv2_ref), (1, kv1_ref), (3, kv3_ref)):
        attend_slots(k, kv_ref, queries, eff_ref, pos, run_ref, acc_ref)
    peak = run_ref[0:1, :]
    total = run_ref[1:2, :]
    peak_high = peak.astype(jnp.bfloat16).astype(jnp.float32)
    total_high = total.astype(jnp.bfloat16).astype(jnp.float32)
    stats = jnp.concatenate(
        [
            peak_high,
            peak - peak_high,
            total_high,
            total - total_high,
            jnp.zeros((12, QROWS), jnp.float32),
        ],
        axis=0,
    )
    sent_ref[:HD, :] = (acc_ref[...] / total).astype(jnp.bfloat16)
    sent_ref[HD:, :] = stats.astype(jnp.bfloat16)


def own_kernel(
    flag_ref,
    own_ref,
    other_ref,
    eff_ref,
    fresh_eff_ref,
    pos_ref,
    kv0_ref,
    kv1_ref,
    kv2_ref,
    kv3_ref,
    acc_ref,
    run_ref,
):
    queries = own_ref[:QROWS, :]
    pos = pos_ref[...]
    attend_fresh(queries, flag_ref, own_ref, other_ref, fresh_eff_ref, pos, run_ref, acc_ref)
    for k, kv_ref in ((0, kv0_ref), (1, kv1_ref), (2, kv2_ref), (3, kv3_ref)):
        attend_slots(k, kv_ref, queries, eff_ref, pos, run_ref, acc_ref)


def merge_kernel(acc_ref, run_ref, got_ref, out_ref):
    stats = got_ref[HD:, :].astype(jnp.float32)
    got_peak = stats[0:1, :] + stats[1:2, :]
    got_total = stats[2:3, :] + stats[3:4, :]
    peak = run_ref[0:1, :]
    total = run_ref[1:2, :]
    joint = jnp.maximum(peak, got_peak)
    mine = jnp.exp2(peak - joint)
    theirs = jnp.exp2(got_peak - joint) * got_total
    whole = mine * total + theirs
    mixed = acc_ref[...] * (mine / whole) + got_ref[:HD, :].astype(jnp.float32) * (theirs / whole)
    turned = mixed.T.astype(jnp.bfloat16)
    for head in range(QS):
        out_ref[:, pl.ds(head * HD, HD)] = turned[head * ROWS : (head + 1) * ROWS, :]


def body(hidden, norm_gain, q_weight, kv_weight, cache_store, location, stretch_ids, rec_pos):
    x = lax.axis_index("x")
    z = lax.axis_index("z")
    y = lax.axis_index("y")
    c = lax.axis_index("c")
    my_tp = y * NC + c
    which_half = my_tp // KVH
    is_first = which_half == 0
    positions = rec_pos[0]
    own_list = stretch_ids[0]
    int_rows = jnp.arange(CH_DEV, dtype=jnp.int32)
    table = jnp.arange(location.shape[0], dtype=jnp.int32)

    store = lax.all_gather(cache_store[:, 0], "z", axis=0, tiled=True)

    listed = jnp.pad(own_list.astype(jnp.bfloat16)[None, :], ((0, 15), (0, COLS - MAXC)))
    weight = jnp.concatenate([q_weight[:, 0], kv_weight[:, 0]], axis=1)
    weight = jnp.concatenate([weight, listed], axis=0)

    far_weight = shifted(weight, "x", NX, -2)
    blocks = hidden[0].reshape(NY, 8, 2, NC, HD).transpose(2, 0, 3, 1, 4)
    blocks = jnp.broadcast_to(blocks[None], (4, 2, NY, NC, 8, HD))
    blocks = lax.all_to_all(
        blocks.reshape(NZ * NY * NC, 8, HD), ("z", "y", "c"), 0, 0, tiled=True
    )
    blocks, weight, far_weight = lax.optimization_barrier((blocks, weight, far_weight))
    weights = [weight, shifted(weight, "x", NX, -1), far_weight, shifted(weight, "x", NX, -3)]
    blocks = blocks.reshape(NZ, NX, 4, 8, HD)
    blocks = lax.dynamic_index_in_dim(blocks, z // 2, 2, keepdims=False)
    blocks = jnp.concatenate([blocks, blocks], axis=1)
    blocks = lax.dynamic_slice_in_dim(blocks, x, NX, 1)
    blocks = blocks.transpose(0, 2, 1, 3).reshape(NZ, 8, NX * HD)
    tokens = lax.all_to_all(
        jnp.broadcast_to(blocks[None], (NY, NZ, 8, NX * HD)), "y", 0, 0, tiled=True
    )
    steps = jnp.arange(NZ, dtype=jnp.int32)
    row_ids = ((x * NZ + steps)[:, None] * CH_DEV + int_rows[None, :]).reshape(-1)
    here = location[None, :] == row_ids[:, None]
    held = jnp.sum(jnp.where(here, table, 0), axis=1).astype(jnp.float32)
    held = jnp.broadcast_to(held[:, None], (NZ * CH_DEV, HD))

    frequency = jnp.exp(
        -math.log(theta_base) * jnp.arange(HD // 2, dtype=jnp.float32) / (HD // 2)
    )
    angles = positions.astype(jnp.float32)[:, None] * frequency[None, :]
    cos = jnp.cos(angles)
    sin = jnp.sin(angles)
    cos = jnp.concatenate([cos, cos], axis=1)
    sin = jnp.concatenate([-sin, sin], axis=1)
    fresh_cos = jnp.where(is_first, cos, 1.0)
    fresh_sin = jnp.where(is_first, sin, 0.0)
    scale = math.log2(math.e) / math.sqrt(HD)

    own_row = jnp.sum(jnp.where(own_list[:, None] == table[None, :], location[None, :], 0), axis=1)
    own_shard = own_row // CH_DEV
    slot_shard = (x * NZ + jnp.arange(MAXC, dtype=jnp.int32)) % (NX * NZ)
    match = (own_shard[None, :] == slot_shard[:, None]) & (own_list >= 0)[None, :]
    slot_order = jnp.sum(jnp.where(match, jnp.arange(MAXC, dtype=jnp.int32), 0), axis=1)
    slot_live = jnp.any(match, axis=1)
    key_pos = (
        slot_order[None, :] * STRETCH
        + which_half * HALF
        + jnp.arange(HALF, dtype=jnp.int32)[:, None]
    )
    replaced = jnp.any(key_pos[:, :, None] == positions[None, None, :], axis=2)
    eff = jnp.where(replaced | ~slot_live[None, :], far_away, key_pos)
    fresh_eff = jnp.where(positions % STRETCH // HALF == which_half, positions, far_away)
    fresh_eff = jnp.broadcast_to(fresh_eff[:, None], (ROWS, HD))
    pos_row = jnp.tile(positions, QS).reshape(1, QROWS)

    gain = lax.dynamic_index_in_dim(norm_gain.reshape(NX, NZ, NC * HD), z, 1, keepdims=False)
    gain = lax.dynamic_slice_in_dim(jnp.concatenate([gain, gain], axis=0), x, NX, 0)
    gain = gain.astype(jnp.float32).reshape(1, NX * NC * HD)

    turns = (cos * scale, sin * scale, fresh_cos, fresh_sin)
    tokens, weights, turns, eff, fresh_eff, pos_row, gain, held = lax.optimization_barrier(
        (tokens, weights, turns, eff, fresh_eff, pos_row, gain, held)
    )
    mate_tokens = swap_cores(tokens)

    smem = pl.BlockSpec(memory_space=pltpu.SMEM)
    vmem = pl.BlockSpec(memory_space=pltpu.VMEM)
    hbm = pl.BlockSpec(memory_space=pltpu.MemorySpace.HBM)
    partial, send_rows = pl.pallas_call(
        project_kernel,
        out_shape=[
            jax.ShapeDtypeStruct((NZ, ROWS + 8, COLS), jnp.bfloat16),
            jax.ShapeDtypeStruct((NX, NZ, HD), jnp.int32),
        ],
        in_specs=[smem] + [vmem] * 8,
        out_specs=[vmem] * 2,
        name="project",
        compiler_params=pltpu.CompilerParams(vmem_limit_bytes=32 * 1024 * 1024),
        cost_estimate=pl.CostEstimate(
            flops=2 * NZ * ROWS * 1024 * COLS, bytes_accessed=1 << 22, transcendentals=0
        ),
    )(c.reshape(1), tokens, mate_tokens, gain, held, *weights)
    parts = lax.all_to_all(partial, "z", 0, 0, tiled=True)

    def pick(which, rows):
        return pl.pallas_call(
            functools.partial(pick_kernel, which),
            out_shape=[jax.ShapeDtypeStruct((NZ, HALF, 2 * HD), jnp.bfloat16)] * len(which),
            in_specs=[vmem, hbm],
            out_specs=[vmem] * len(which),
            scratch_shapes=[
                pltpu.SMEM((NX, NZ, HD), jnp.int32),
                pltpu.SemaphoreType.DMA((len(which) * NZ,)),
                pltpu.SemaphoreType.DMA,
            ],
            name="pick",
            compiler_params=pltpu.CompilerParams(vmem_limit_bytes=50 * 1024 * 1024),
            cost_estimate=pl.CostEstimate(
                flops=0, bytes_accessed=len(which) << 20, transcendentals=0
            ),
        )(rows, store)

    picked = dict(zip((2, 1, 3), pick((2, 1, 3), send_rows)))
    arrived = {k: shifted(picked[k], "x", NX, -k) for k in (2, 1, 3)}
    own_rows, parts = lax.optimization_barrier((send_rows, parts))
    arrived[0] = pick((0,), own_rows)[0]

    own = call(
        finish_kernel, jax.ShapeDtypeStruct((QROWS + ROWS, HD), jnp.bfloat16), "finish"
    )(parts, *turns)
    other = exchange(own)

    params = pltpu.CompilerParams(vmem_limit_bytes=32 * 1024 * 1024)
    run_shapes = [
        jax.ShapeDtypeStruct((HD, QROWS), jnp.float32),
        jax.ShapeDtypeStruct((8, QROWS), jnp.float32),
    ]

    def cost(count):
        pairs = count * NZ * HALF * QROWS
        return pl.CostEstimate(flops=4 * pairs * HD, bytes_accessed=count << 19, transcendentals=pairs)

    common = (which_half.reshape(1), own, other, eff, fresh_eff, pos_row)
    sent = pl.pallas_call(
        other_kernel,
        out_shape=jax.ShapeDtypeStruct((HD + 16, QROWS), jnp.bfloat16),
        in_specs=[smem] + [vmem] * 9,
        out_specs=vmem,
        scratch_shapes=[pltpu.VMEM(r.shape, r.dtype) for r in run_shapes],
        name="other",
        compiler_params=params,
        cost_estimate=cost(4),
    )(*common, *[arrived[k] for k in (0, 2, 1, 3)])
    got = exchange(sent)
    queries, allowed, sent = lax.optimization_barrier((own, eff, sent))
    own_acc, own_run = pl.pallas_call(
        own_kernel,
        out_shape=run_shapes,
        in_specs=[smem] + [vmem] * 9,
        out_specs=[vmem] * 2,
        name="own",
        compiler_params=params,
        cost_estimate=cost(4),
    )(which_half.reshape(1), queries, other, allowed, fresh_eff, pos_row, *[arrived[k] for k in range(NX)])
    attended = call(merge_kernel, jax.ShapeDtypeStruct((ROWS, QW), jnp.bfloat16), "merge")(
        own_acc, own_run, got
    )
    return attended.reshape(1, ROWS, 1, QW)


def solution(mesh):
    fine = Mesh(mesh.devices.reshape(NX, NZ, NY, NC), ("x", "z", "y", "c"))
    in_specs = (
        P(STORE, None, TP),
        P(),
        P(STORE, TP, None),
        P(STORE, TP, None),
        P(STORE, TP, None, None),
        P(),
        P(STORE, None),
        P(STORE, None),
    )
    return jax.shard_map(
        body, mesh=fine, in_specs=in_specs, out_specs=P(STORE, None, TP, None), check_vma=False
    )
```
